32 devices in a mesh: nodes: 8 (over z, y), hid: 4 (over x, core).
Axes of the slice: x: 2, y: 2, z: 4, core: 2. Of those that a mesh axis runs over, the one named last changes fastest.
Arguments:
- states: float32 [32768, 512], P(('nodes', 'hid')), may hold values from -6 to 6
- condition: float32 [16], replicated, may hold values from -4 to 4
- mod_w: bfloat16 [16, 2048], replicated, may hold values from -0.5 to 0.5
- w_query: bfloat16 [512, 512], replicated, may hold values from -0.25 to 0.25
- w_key: bfloat16 [512, 512], replicated, may hold values from -0.25 to 0.25
- w_value: bfloat16 [512, 512], replicated, may hold values from -0.25 to 0.25
- w_out: bfloat16 [512, 512], replicated, may hold values from -1 to 1
- w_gate: bfloat16 [512, 2048], P(None, 'hid'), may hold values from -0.25 to 0.25
- w_up: bfloat16 [512, 2048], P(None, 'hid'), may hold values from -0.25 to 0.25
- w_down: bfloat16 [2048, 512], P('hid'), may hold values from -0.125 to 0.125
- counts: int32 [32], P(('nodes', 'hid')), may hold values from 512 to 1024, as said below
- send_rows: int32 [32, 4, 128], P(('nodes', 'hid')), may hold values from 0 to 1023, as said below
- neighbours: int32 [32768, 16], P(('nodes', 'hid')), may hold values from 0 to 1535, as said below
- cotangent: float32 [32768, 512], P(('nodes', 'hid')), may hold values from -6 to 6
Outputs:
- output: float32 [32768, 512], P(('nodes', 'hid'))
- grad_states: float32 [32768, 512], P(('nodes', 'hid'))
- grad_condition: float32 [16], replicated
- grad_mod_w: float32 [16, 2048], replicated
- grad_w_query: float32 [512, 512], replicated
- grad_w_key: float32 [512, 512], replicated
- grad_w_value: float32 [512, 512], replicated
- grad_w_out: float32 [512, 512], replicated
- grad_w_gate: float32 [512, 2048], P(None, 'hid')
- grad_w_up: float32 [512, 2048], P(None, 'hid')
- grad_w_down: float32 [2048, 512], P('hid')
The draws below stay inside these ranges and needn't reach their ends.
Inputs may be any that keep to these rules, and one draw needn't show every extreme that they name: counts[d] is the number of mesh nodes of device d; its slots below counts[d] hold nodes, the rest are padding. send_rows[d, j, c] is below counts[d]. `neighbours`: an entry below 1024 in a row of device d is below counts[d]; entries from 1024 up name received rows as in the reference program.
All inputs are finite; a program needn't handle non-finite values.
Results may differ from the reference program's by a relative error of at most 0.013.
Values may be sent and summed in bfloat16 or wider, within the bound.
No kernel may reach another device: no remote copies, remote signals or barrier semaphores. Data moves between devices by JAX's collectives and lax.ppermute only.
A program may use at most 192 MiB of HBM per device.

```python
import jax
import jax.numpy as jnp
from jax import lax

D = 512
HEADS = 4
HEAD_DIM = 128
FF = 2048
NEIGH = 16
COND = 16
SLOTS = 1024
SENDS = 128
SHARDS = 32
TOKENS = 32768


def patch_sizes(key):
    first, second = jax.random.split(key)
    sizes = jax.random.randint(first, (SHARDS,), SLOTS // 2, SLOTS + 1)
    order = jax.random.permutation(second, SHARDS)
    sizes = sizes.at[order[0]].set(SLOTS).at[order[1]].set(SLOTS // 2)
    return (sizes.astype(jnp.int32), order[0])


def draw_counts(key, part):
    sizes, fullest = patch_sizes(key)
    return sizes


def draw_send_rows(key, part):
    sizes, fullest = patch_sizes(key)
    key = jax.random.fold_in(key, 11)
    raw = jax.random.randint(key, (SHARDS, 4, SENDS), 0, 1 << 20)
    chosen = raw % sizes[:, None, None]
    chosen = chosen.at[fullest, 0, 0].set(SLOTS - 1).at[fullest, 0, 1].set(0)
    return chosen.astype(jnp.int32)


def draw_neighbours(key, part):
    sizes, fullest = patch_sizes(key)
    key = jax.random.fold_in(key, 23)
    first, second, third = jax.random.split(key, 3)
    owners = jnp.arange(TOKENS, dtype=jnp.int32) // SLOTS
    local_rows = jax.random.randint(first, (TOKENS, NEIGH), 0, 1 << 20) % sizes[owners][:, None]
    remote_rows = SLOTS + jax.random.randint(second, (TOKENS, NEIGH), 0, 4 * SENDS)
    picked = jax.random.randint(third, (TOKENS, NEIGH), 0, 4) == 0
    chosen = jnp.where(picked, remote_rows, local_rows)
    chosen = chosen.at[0, 0].set(SLOTS + 4 * SENDS - 1).at[0, 1].set(0)
    return chosen.astype(jnp.int32)


def block_levels(key, extent, pieces, smallest, high):
    def one(axis_at, shards_of):
        draws = jax.random.uniform(jax.random.fold_in(jax.random.fold_in(key, 6), axis_at), (shards_of,), jnp.float32, smallest / len(pieces), high / len(pieces))
        return jnp.repeat(jnp.exp(draws), extent[axis_at] // shards_of).reshape((-1,) + (1,) * (len(extent) - axis_at - 1))

    level = one(*pieces[0])
    for cut in pieces[1:]:
        level = level * one(*cut)
    return level


def gaussian(own_key, extent, width, limit, cuts=(), held_as=jnp.bfloat16):
    result = jax.random.normal(own_key, extent, jnp.float32) * width
    if len(cuts) > 0:
        result = block_levels(own_key, extent, cuts, -0.22, 0.18) * result
    return jnp.clip(result, min=-limit, max=limit).astype(held_as)


def setup_inputs(seed: int = 0) -> dict:
    keys = jax.random.split(jax.random.key(seed), 15)
    states = gaussian(keys[0], (TOKENS, D), 1.0, 6.0, ((0, 32),), jnp.float32)
    condition = gaussian(keys[1], (COND,), 1.0, 4.0, (), jnp.float32)
    mod_w = gaussian(keys[2], (COND, 4 * D), (10 * COND) ** -0.5, 0.5)
    w_query = gaussian(keys[3], (D, D), D ** -0.5, 0.25)
    w_key = gaussian(keys[4], (D, D), D ** -0.5, 0.25)
    w_value = gaussian(keys[5], (D, D), D ** -0.5, 0.25)
    w_out = gaussian(keys[6], (D, D), (D // 16) ** -0.5, 1.0)
    w_gate = gaussian(keys[7], (D, FF), D ** -0.5, 0.25, ((1, 4),))
    w_up = gaussian(keys[8], (D, FF), D ** -0.5, 0.25, ((1, 4),))
    w_down = gaussian(keys[9], (FF, D), FF ** -0.5, 0.125, ((0, 4),))
    counts = draw_counts(jax.random.fold_in(keys[14], 71), 0)
    send_rows = draw_send_rows(jax.random.fold_in(keys[14], 71), 0)
    neighbours = draw_neighbours(jax.random.fold_in(keys[14], 71), 0)
    cotangent = gaussian(keys[13], (TOKENS, D), 1.0, 6.0, ((0, 32),), jnp.float32)
    return {"states": states, "condition": condition, "mod_w": mod_w, "w_query": w_query, "w_key": w_key, "w_value": w_value, "w_out": w_out, "w_gate": w_gate, "w_up": w_up, "w_down": w_down, "counts": counts, "send_rows": send_rows, "neighbours": neighbours, "cotangent": cotangent}


@jax.custom_vjp
def low(v):
    return lax.optimization_barrier(v.astype(jnp.bfloat16)).astype(jnp.float32)

@jax.custom_vjp
def low_back(v):
    return v

def low_keep(v):
    return (low(v), None)

def low_pass(kept, grad):
    return (grad,)

def back_keep(v):
    return (v, None)

def back_low(kept, grad):
    return (low(grad),)
low.defvjp(low_keep, low_pass)
low_back.defvjp(back_keep, back_low)
epsilon = 1e-06
halo_steps = (1, -1, 2, -2)
highest = lax.Precision.HIGHEST

def normalize(states):
    centred = states - lax.optimization_barrier(jnp.mean(states, axis=-1, keepdims=True))
    return centred * lax.rsqrt(lax.optimization_barrier(jnp.mean(centred * centred, axis=-1, keepdims=True)) + epsilon)

def neighbour_ids(neighbours, send_rows):
    row_ids = jnp.arange(TOKENS, dtype=jnp.int32)
    owners = row_ids // SLOTS
    local_ids = owners[:, None] * SLOTS + neighbours
    extra_ids = jnp.clip(neighbours - SLOTS, 0, 4 * SENDS - 1).astype(jnp.int32)
    which_hop = extra_ids // SENDS
    slot_place = extra_ids % SENDS
    moved = jnp.array(halo_steps, dtype=jnp.int32)[which_hop]
    source = (owners[:, None] - moved) % SHARDS
    remote_ids = source * SLOTS + send_rows[source, which_hop, slot_place]
    return jnp.where(neighbours < SLOTS, local_ids, remote_ids).astype(jnp.int32)

def forward(states, condition, mod_w, w_query, w_key, w_value, w_out, w_gate, w_up, w_down, neighbour_rows, live):
    modulation = jnp.dot(condition, mod_w, precision=highest)
    scale_one, bias_one, scale_two, bias_two = jnp.split(modulation, 4)
    normed = low(normalize(states) * (1.0 + scale_one) + bias_one)
    queries = low(low_back(jnp.dot(normed, w_query, precision=highest)))
    key_rows = low(low_back(jnp.dot(normed, w_key, precision=highest)))
    value_rows = low(low_back(jnp.dot(normed, w_value, precision=highest)))
    block_rows = min(TOKENS, 512)
    block_count = TOKENS // block_rows

    def attend(inputs_pair):
        query_block, id_block = inputs_pair
        near_keys = key_rows[id_block].reshape(block_rows, NEIGH, HEADS, HEAD_DIM)
        near_values = value_rows[id_block].reshape(block_rows, NEIGH, HEADS, HEAD_DIM)
        heads_query = query_block.reshape(block_rows, HEADS, HEAD_DIM)
        scores = low_back(jnp.einsum('bhd,bkhd->bhk', heads_query, near_keys, precision=highest) * HEAD_DIM ** (-0.5))
        raised = jnp.exp(scores - lax.optimization_barrier(jnp.max(scores, axis=-1, keepdims=True)))
        attn_probs = low(raised / lax.optimization_barrier(jnp.sum(raised, axis=-1, keepdims=True)))
        mixed = jnp.einsum('bhk,bkhd->bhd', attn_probs, near_values, precision=highest)
        return mixed.reshape(block_rows, D)
    attended = lax.map(jax.checkpoint(attend), (queries.reshape(block_count, block_rows, D), neighbour_rows.reshape(block_count, block_rows, NEIGH)))
    attended = low(low_back(attended.reshape(TOKENS, D)))
    middle = states + live * low_back(jnp.dot(attended, w_out, precision=highest))
    second = low(normalize(middle) * (1.0 + scale_two) + bias_two)
    gate = low_back(jnp.dot(second, w_gate, precision=highest))
    up_proj = low_back(jnp.dot(second, w_up, precision=highest))
    hidden = low(gate * jax.nn.sigmoid(gate) * up_proj)
    return middle + live * low_back(jnp.dot(hidden, w_down, precision=highest))

def reference(states, condition, mod_w, w_query, w_key, w_value, w_out, w_gate, w_up, w_down, counts, send_rows, neighbours, cotangent):
    weight_list = [item.astype(jnp.float32) for item in (mod_w, w_query, w_key, w_value, w_out, w_gate, w_up, w_down)]
    row_ids = jnp.arange(TOKENS, dtype=jnp.int32)
    live = (row_ids % SLOTS < counts[row_ids // SLOTS]).astype(jnp.float32)[:, None]
    neighbour_rows = neighbour_ids(neighbours, send_rows)

    def layer_fn(states_in, condition_in, mod_in, query_in, key_in, value_in, out_in, gate_in, up_in, down_in):
        return forward(states_in, condition_in, mod_in, query_in, key_in, value_in, out_in, gate_in, up_in, down_in, neighbour_rows, live)
    output, pull_back = jax.vjp(layer_fn, states, condition, *weight_list)
    gradients = pull_back(cotangent)
    return (output, gradients[0], gradients[1], gradients[2], gradients[3], gradients[4], gradients[5], gradients[6], gradients[7], gradients[8], gradients[9])
```

```python
import jax
import jax.numpy as jnp
from jax import lax
from jax.experimental import pallas as pl
from jax.experimental.pallas import tpu as pltpu
from jax.sharding import PartitionSpec as P

HEADS = 4
HEAD_DIM = 128
NEIGH = 16


epsilon = 1e-06
halo_steps = (1, -1, 2, -2)
highest = lax.Precision.HIGHEST


def from_behind(block, axis, distance):
    devices = range(lax.axis_size(axis))
    route = [((i - distance) % len(devices), i) for i in devices]
    return lax.ppermute(block, axis, route)


def matmul(left, right):
    return jnp.dot(left, right, preferred_element_type=jnp.float32)


def times_transposed(left, right):
    return lax.dot_general(
        left, right, (((1,), (1,)), ((), ())), preferred_element_type=jnp.float32
    )


def transposed_times(left, right):
    return lax.dot_general(
        left, right, (((0,), (0,)), ((), ())), preferred_element_type=jnp.float32
    )


def norm_parts(states):
    centred = states - jnp.mean(states, axis=-1, keepdims=True)
    inverse = lax.rsqrt(jnp.mean(centred * centred, axis=-1, keepdims=True) + epsilon)
    return (centred * inverse, inverse)


def norm_back(grad_plain, plain, inverse):
    first_mean = jnp.mean(grad_plain, axis=-1, keepdims=True)
    second_mean = jnp.mean(grad_plain * plain, axis=-1, keepdims=True)
    return inverse * (grad_plain - first_mean - plain * second_mean)


def silu_parts(gate):
    sigmoid = jax.nn.sigmoid(gate)
    return (gate * sigmoid, sigmoid * (1.0 + gate * (1.0 - sigmoid)))


def dot(left, right, left_dim, right_dim):
    return lax.dot_general(
        left, right, (((left_dim,), (right_dim,)), ((), ())), preferred_element_type=jnp.float32
    )


BLOCK = 512
score_scale = HEAD_DIM ** (-0.5)


def attend_kernel(near_ref, query_ref, key_ref, value_t_ref, attended_ref, raised_ref, inverse_ref, bias, scores):
    ext, rows = bias.shape
    groups = ext // 128
    half = groups // 2

    @pl.when(pl.program_id(0) == 0)
    def _():
        @pl.loop(0, rows // 128)
        def _(step):
            cols = pl.ds(pl.multiple_of(step * 128, 128), 128)
            near = near_ref[:, cols]
            group = near >> 7
            upper = group >= half
            unit = jnp.left_shift(1, 5 * jnp.where(upper, group - half, group))
            low = near & 127
            low_unit = jnp.where(upper, 0, unit)
            high_unit = jnp.where(upper, unit, 0)
            place = lax.broadcasted_iota(jnp.int32, (128, 128), 0)
            low_count = jnp.zeros((128, 128), jnp.int32)
            high_count = low_count
            for n in range(NEIGH):
                same = low[n : n + 1] == place
                low_count = low_count + jnp.where(same, low_unit[n : n + 1], 0)
                high_count = high_count + jnp.where(same, high_unit[n : n + 1], 0)
            for g in range(groups):
                packed = low_count if g < half else high_count
                count = (packed >> (5 * (g % half))) & 31
                bias[g * 128 : (g + 1) * 128, cols] = jnp.where(
                    count > 0, jnp.log(count.astype(jnp.float32)), -1e30
                )

    width = scores.shape[1]

    @pl.loop(0, rows // width)
    def _(step):
        cols = pl.ds(pl.multiple_of(step * width, width), width)
        query = query_ref[cols, :]
        top = jnp.full((8, width), -jnp.inf, jnp.float32)
        for g in range(groups):
            part = slice(g * 128, (g + 1) * 128)
            score = dot(key_ref[part, :], query, 1, 1) * score_scale + bias[part, cols]
            scores[part, :] = score
            top = jnp.maximum(top, jnp.max(score.reshape(16, 8, width), axis=0))
        top = jnp.max(top, axis=0, keepdims=True)
        total = jnp.zeros((8, width), jnp.float32)
        for g in range(groups):
            part = slice(g * 128, (g + 1) * 128)
            raised = jnp.exp(scores[part, :] - top)
            total = total + jnp.sum(raised.reshape(16, 8, width), axis=0)
            raised_ref[0, part, cols] = raised.astype(jnp.bfloat16)
        inverse = 1.0 / jnp.sum(total, axis=0, keepdims=True)
        inverse_ref[0, :, cols] = inverse
        mixed = dot(value_t_ref[...], raised_ref[0, :, cols], 1, 0) * inverse
        attended_ref[cols, :] = mixed.T.astype(jnp.bfloat16)


def attend(near, queries, keys, values_t):
    rows, ext = queries.shape[0], keys.shape[0]
    return pl.pallas_call(
        attend_kernel,
        grid=(HEADS,),
        in_specs=[
            pl.BlockSpec((NEIGH, rows), lambda h: (0, 0)),
            pl.BlockSpec((rows, HEAD_DIM), lambda h: (0, h)),
            pl.BlockSpec((ext, HEAD_DIM), lambda h: (0, h)),
            pl.BlockSpec((HEAD_DIM, ext), lambda h: (h, 0)),
        ],
        out_specs=[
            pl.BlockSpec((rows, HEAD_DIM), lambda h: (0, h)),
            pl.BlockSpec((1, ext, rows), lambda h: (h, 0, 0)),
            pl.BlockSpec((1, 1, rows), lambda h: (h, 0, 0)),
        ],
        out_shape=[
            jax.ShapeDtypeStruct((rows, HEADS * HEAD_DIM), jnp.bfloat16),
            jax.ShapeDtypeStruct((HEADS, ext, rows), jnp.bfloat16),
            jax.ShapeDtypeStruct((HEADS, 1, rows), jnp.float32),
        ],
        scratch_shapes=[pltpu.VMEM((ext, rows), jnp.float32), pltpu.VMEM((ext, BLOCK), jnp.float32)],
        compiler_params=pltpu.CompilerParams(vmem_limit_bytes=48 * 2**20),
        cost_estimate=pl.CostEstimate(flops=4 * ext * rows * 512, bytes_accessed=2**24, transcendentals=4 * ext * rows),
    )(near, queries, keys, values_t)


def attend_back_kernel(
    query_ref, key_t_ref, value_ref, grad_ref, raised_ref, inverse_ref, grad_query_ref, grad_key_ref, grad_value_ref, terms, low
):
    ext, rows = low.shape
    width = terms.shape[1]

    @pl.loop(0, rows // width)
    def _(step):
        cols = pl.ds(pl.multiple_of(step * width, width), width)
        grad = grad_ref[cols, :]
        total = jnp.zeros((8, width), jnp.float32)
        for g in range(ext // 128):
            part = slice(g * 128, (g + 1) * 128)
            term = dot(value_ref[part, :], grad, 1, 1) * raised_ref[0, part, cols].astype(jnp.float32)
            terms[part, :] = term
            total = total + jnp.sum(term.reshape(16, 8, width), axis=0)
        mean = jnp.sum(total, axis=0, keepdims=True) * inverse_ref[0, :, cols]
        for g in range(ext // 128):
            part = slice(g * 128, (g + 1) * 128)
            low[part, cols] = (terms[part, :] - raised_ref[0, part, cols].astype(jnp.float32) * mean).astype(
                jnp.bfloat16
            )
        grad_query = dot(key_t_ref[...], low[:, cols], 1, 0) * score_scale
        grad_query_ref[cols, :] = grad_query.T.astype(jnp.bfloat16)

    grad_value_ref[...] = dot(raised_ref[0], grad_ref[...], 1, 0)
    grad_key_ref[...] = dot(low[...], query_ref[...], 1, 0) * score_scale


def attend_back(queries, keys_t, values, grads, raised, inverse):
    rows, ext = queries.shape[0], values.shape[0]
    by_row = pl.BlockSpec((rows, HEAD_DIM), lambda h: (0, h))
    by_ext = pl.BlockSpec((ext, HEAD_DIM), lambda h: (0, h))
    return pl.pallas_call(
        attend_back_kernel,
        grid=(HEADS,),
        in_specs=[
            by_row,
            pl.BlockSpec((HEAD_DIM, ext), lambda h: (h, 0)),
            by_ext,
            by_row,
            pl.BlockSpec((1, ext, rows), lambda h: (h, 0, 0)),
            pl.BlockSpec((1, 1, rows), lambda h: (h, 0, 0)),
        ],
        out_specs=[by_row, by_ext, by_ext],
        out_shape=[
            jax.ShapeDtypeStruct((rows, HEADS * HEAD_DIM), jnp.bfloat16),
            jax.ShapeDtypeStruct((ext, HEADS * HEAD_DIM), jnp.float32),
            jax.ShapeDtypeStruct((ext, HEADS * HEAD_DIM), jnp.float32),
        ],
        scratch_shapes=[pltpu.VMEM((ext, BLOCK), jnp.float32), pltpu.VMEM((ext, rows), jnp.bfloat16)],
        compiler_params=pltpu.CompilerParams(vmem_limit_bytes=48 * 2**20),
        cost_estimate=pl.CostEstimate(flops=8 * ext * rows * 512, bytes_accessed=2**24, transcendentals=0),
    )(queries, keys_t, values, grads, raised, inverse)


def body(
    states,
    condition,
    mod_w,
    w_query,
    w_key,
    w_value,
    w_out,
    w_gate,
    w_up,
    w_down,
    counts,
    send_rows,
    neighbours,
    cotangent,
):
    slot_count, model_width = states.shape
    live = (jnp.arange(slot_count) < counts[0]).astype(jnp.float32)[:, None]
    modulation = jnp.dot(condition, mod_w.astype(jnp.float32), precision=highest)
    scale_one, bias_one, scale_two, bias_two = jnp.split(modulation, 4)
    plain_one, inverse_one = norm_parts(states)
    normed = (plain_one * (1.0 + scale_one) + bias_one).astype(jnp.bfloat16)
    queries = matmul(normed, w_query).astype(jnp.bfloat16)
    key_values = jnp.concatenate([matmul(normed, w_key), matmul(normed, w_value)], axis=1).astype(
        jnp.bfloat16
    )
    send_list = send_rows[0]
    sends = send_list.shape[1]
    landed = []
    for position, hop_size in enumerate(halo_steps):
        parcel = key_values[send_list[position]]
        landed.append(from_behind(parcel, ("nodes", "hid"), hop_size))
    extended = jnp.concatenate([key_values] + landed, axis=0)

    keys, values = extended[:, :model_width], extended[:, model_width:]
    attended, raised, inverse_total = attend(neighbours.T, queries, keys, values.T)
    middle = states + live * matmul(attended, w_out)
    plain_two, inverse_two = norm_parts(middle)
    second = (plain_two * (1.0 + scale_two) + bias_two).astype(jnp.bfloat16)
    grad_branch = (live * cotangent).astype(jnp.bfloat16)
    rows_all = lax.all_gather(second, "hid", axis=0, tiled=True)
    gate = matmul(rows_all, w_gate)
    up_proj = matmul(rows_all, w_up)
    activated, slope = silu_parts(gate)
    hidden = (activated * up_proj).astype(jnp.bfloat16)
    mlp_out = lax.psum_scatter(
        matmul(hidden, w_down).astype(jnp.bfloat16), "hid", scatter_dimension=0, tiled=True
    ).astype(jnp.float32)
    grad_rows = lax.all_gather(grad_branch, "hid", axis=0, tiled=True)
    grad_hidden = times_transposed(grad_rows, w_down)
    grad_gate = (grad_hidden * up_proj * slope).astype(jnp.bfloat16)
    grad_up = (grad_hidden * activated).astype(jnp.bfloat16)
    grad_second = lax.psum_scatter(
        times_transposed(grad_gate, w_gate) + times_transposed(grad_up, w_up),
        "hid",
        scatter_dimension=0,
        tiled=True,
    )
    mlp_grads = (
        transposed_times(rows_all, grad_gate),
        transposed_times(rows_all, grad_up),
        transposed_times(hidden, grad_rows),
    )
    output = middle + live * mlp_out
    grad_w_gate, grad_w_up, grad_w_down = (
        lax.psum(mlp_grads[0].astype(jnp.bfloat16), "nodes").astype(jnp.float32),
        lax.psum(mlp_grads[1].astype(jnp.bfloat16), "nodes").astype(jnp.float32),
        lax.psum(mlp_grads[2].astype(jnp.bfloat16), "nodes").astype(jnp.float32),
    )
    grad_scale_two = jnp.sum(grad_second * plain_two, axis=0)
    grad_bias_two = jnp.sum(grad_second, axis=0)
    grad_middle = cotangent + norm_back(grad_second * (1.0 + scale_two), plain_two, inverse_two)
    grad_attn = (live * grad_middle).astype(jnp.bfloat16)
    grad_w_out_part = transposed_times(attended, grad_attn)
    spread = jnp.repeat(inverse_total[:, 0].T, HEAD_DIM, axis=1)
    grad_attended = (times_transposed(grad_attn, w_out) * spread).astype(jnp.bfloat16)
    grad_queries, *grad_extended = attend_back(
        queries, keys.T, values, grad_attended, raised, inverse_total
    )
    grad_extended = jnp.concatenate(grad_extended, axis=1)
    grad_own = grad_extended[:slot_count]
    for position, hop_size in enumerate(halo_steps):
        lower = slot_count + position * sends
        parcel = grad_extended[lower : lower + sends]
        returned = from_behind(parcel.astype(jnp.bfloat16), ("nodes", "hid"), -hop_size).astype(
            parcel.dtype
        )
        grad_own = grad_own.at[send_list[position]].add(returned)
    grad_keys = grad_own[:, :model_width].astype(jnp.bfloat16)
    grad_values = grad_own[:, model_width:].astype(jnp.bfloat16)
    grad_normed = (
        times_transposed(grad_queries, w_query)
        + times_transposed(grad_keys, w_key)
        + times_transposed(grad_values, w_value)
    )
    grad_scale_one = jnp.sum(grad_normed * plain_one, axis=0)
    grad_bias_one = jnp.sum(grad_normed, axis=0)
    grad_states = grad_middle + norm_back(grad_normed * (1.0 + scale_one), plain_one, inverse_one)
    mod_part = jnp.concatenate([grad_scale_one, grad_bias_one, grad_scale_two, grad_bias_two])
    attn_parts = (
        transposed_times(normed, grad_queries),
        transposed_times(normed, grad_keys),
        transposed_times(normed, grad_values),
        grad_w_out_part,
        mod_part,
    )
    grad_w_query, grad_w_key, grad_w_value, grad_w_out, mod_grad = lax.psum(
        (attn_parts[0], attn_parts[1], attn_parts[2], attn_parts[3], attn_parts[4]),
        ("nodes", "hid"),
    )
    grad_mod_w = condition[:, None] * mod_grad[None, :]
    grad_condition = jnp.dot(mod_w.astype(jnp.float32), mod_grad, precision=highest)
    return (
        output,
        grad_states,
        grad_condition,
        grad_mod_w,
        grad_w_query,
        grad_w_key,
        grad_w_value,
        grad_w_out,
        grad_w_gate,
        grad_w_up,
        grad_w_down,
    )


def solution(mesh):
    placed = (
        P(("nodes", "hid"), None),
        P(),
        P(),
        P(),
        P(),
        P(),
        P(),
        P(None, "hid"),
        P(None, "hid"),
        P("hid", None),
        P(("nodes", "hid")),
        P(("nodes", "hid"), None, None),
        P(("nodes", "hid"), None),
        P(("nodes", "hid"), None),
    )
    return jax.shard_map(
        body,
        mesh=mesh,
        in_specs=placed,
        out_specs=(
            P(("nodes", "hid"), None),
            P(("nodes", "hid"), None),
            P(),
            P(),
            P(),
            P(),
            P(),
            P(),
            P(None, "hid"),
            P(None, "hid"),
            P("hid", None),
        ),
        check_vma=False,
    )
```

```python
import functools

import jax
import jax.numpy as jnp
from jax import lax
from jax.experimental import pallas as pl
from jax.experimental.pallas import tpu as pltpu
from jax.sharding import PartitionSpec as P

HEADS = 4
HEAD_DIM = 128
NEIGH = 16
BLOCK = 512
ROW_BLOCK = 256

epsilon = 1e-06
halo_steps = (1, -1, 2, -2)
highest = lax.Precision.HIGHEST
score_scale = HEAD_DIM ** (-0.5)
low_type = jnp.bfloat16
everywhere = ("nodes", "hid")
whole = pl.BlockSpec(memory_space=pltpu.VMEM)
scalars = pl.BlockSpec(memory_space=pltpu.SMEM)


def dot(left, right, left_dim, right_dim):
    return lax.dot_general(
        left, right, (((left_dim,), (right_dim,)), ((), ())), preferred_element_type=jnp.float32
    )


def shaped(shape, dtype=low_type):
    return jax.ShapeDtypeStruct(shape, dtype)


def norm_parts(states):
    centred = states - jnp.mean(states, axis=-1, keepdims=True)
    inverse = lax.rsqrt(jnp.mean(centred * centred, axis=-1, keepdims=True) + epsilon)
    return (centred * inverse, inverse)


def norm_back(grad_plain, plain, inverse):
    first_mean = jnp.mean(grad_plain, axis=-1, keepdims=True)
    second_mean = jnp.mean(grad_plain * plain, axis=-1, keepdims=True)
    return inverse * (grad_plain - first_mean - plain * second_mean)


def call(kernel, out_shape, args, specs=None, scratch=(), flops=0, moved=0):
    single = not isinstance(out_shape, list)
    return pl.pallas_call(
        kernel,
        in_specs=specs or [whole] * len(args),
        out_specs=whole if single else [whole] * len(out_shape),
        out_shape=out_shape,
        scratch_shapes=list(scratch),
        compiler_params=pltpu.CompilerParams(vmem_limit_bytes=56 * 2**20),
        cost_estimate=pl.CostEstimate(flops=flops, bytes_accessed=moved, transcendentals=0),
    )(*args)


def chosen_rows(send_ref, position, rows):
    sends = send_ref.shape[1]
    place = lax.broadcasted_iota(jnp.int32, (rows, sends), 0)
    return jnp.where(place == send_ref[position : position + 1, :], 1.0, 0.0).astype(low_type)


def prepare_kernel(states_ref, condition_ref, mod_w_ref, send_ref, normed_ref, modulation_ref, *parcel_refs):
    width = states_ref.shape[1]
    mixed = jnp.sum(condition_ref[...] * mod_w_ref[...].astype(jnp.float32), axis=0, keepdims=True)
    for piece in range(4):
        modulation_ref[piece : piece + 1, :] = mixed[:, piece * width : (piece + 1) * width]

    @pl.loop(0, states_ref.shape[0] // ROW_BLOCK)
    def _(step):
        rows = pl.ds(pl.multiple_of(step * ROW_BLOCK, ROW_BLOCK), ROW_BLOCK)
        plain, _ = norm_parts(states_ref[rows, :])
        normed_ref[rows, :] = (plain * (1.0 + modulation_ref[0:1, :]) + modulation_ref[1:2, :]).astype(low_type)

    for position, parcel_ref in enumerate(parcel_refs):
        chosen = chosen_rows(send_ref, position, states_ref.shape[0])
        parcel_ref[...] = dot(chosen, normed_ref[...], 0, 0).astype(low_type)


def project_kernel(normed_ref, near_ref, w_query_ref, w_key_ref, w_value_ref, query_ref, key_ref, value_ref, packed_ref):
    rows = normed_ref.shape[0]

    @pl.loop(0, rows // ROW_BLOCK)
    def _(step):
        part = pl.ds(pl.multiple_of(step * ROW_BLOCK, ROW_BLOCK), ROW_BLOCK)
        for weight_ref, out_ref in ((w_query_ref, query_ref), (w_key_ref, key_ref), (w_value_ref, value_ref)):
            out_ref[part, :] = dot(normed_ref[part, :], weight_ref[...], 1, 0).astype(low_type)

    half = (rows + 512) // 256

    @pl.loop(0, rows // 128)
    def _(step):
        cols = pl.ds(pl.multiple_of(step * 128, 128), 128)
        near = near_ref[:, cols]
        group = near >> 7
        upper = group >= half
        unit = jnp.left_shift(1, 5 * jnp.where(upper, group - half, group))
        low = near & 127
        low_unit = jnp.where(upper, 0, unit)
        high_unit = jnp.where(upper, unit, 0)
        place = lax.broadcasted_iota(jnp.int32, (128, 128), 0)
        low_count = jnp.zeros((128, 128), jnp.int32)
        high_count = low_count
        for n in range(NEIGH):
            same = low[n : n + 1] == place
            low_count = low_count + jnp.where(same, low_unit[n : n + 1], 0)
            high_count = high_count + jnp.where(same, high_unit[n : n + 1], 0)
        packed_ref[0, :, cols] = low_count
        packed_ref[1, :, cols] = high_count


def attend_kernel(
    packed_ref, query_ref, key_own_ref, value_own_ref, w_key_ref, w_value_ref, *refs
):
    landed_refs, (attended_ref, raised_ref, inverse_ref, spread_ref, key_ref, value_ref) = refs[:4], refs[4:10]
    bias, scores, value_t = refs[10:]
    ext, rows = bias.shape
    groups = ext // 128
    half = groups // 2

    @pl.when(pl.program_id(0) == 0)
    def _():
        @pl.loop(0, rows // 128)
        def _(step):
            cols = pl.ds(pl.multiple_of(step * 128, 128), 128)
            for g in range(groups):
                count = (packed_ref[g // half, :, cols] >> (5 * (g % half))) & 31
                bias[g * 128 : (g + 1) * 128, cols] = jnp.where(
                    count > 0, jnp.log(count.astype(jnp.float32)), -1e30
                )

    key_ref[:rows, :] = key_own_ref[...]
    value_ref[:rows, :] = value_own_ref[...]
    for position, landed_ref in enumerate(landed_refs):
        sends = landed_ref.shape[0]
        part = slice(rows + position * sends, rows + (position + 1) * sends)
        key_ref[part, :] = dot(landed_ref[...], w_key_ref[...], 1, 0).astype(low_type)
        value_ref[part, :] = dot(landed_ref[...], w_value_ref[...], 1, 0).astype(low_type)
    value_t[...] = value_ref[...].T

    width = scores.shape[1]

    @pl.loop(0, rows // width)
    def _(step):
        cols = pl.ds(pl.multiple_of(step * width, width), width)
        query = query_ref[cols, :]
        top = jnp.full((8, width), -jnp.inf, jnp.float32)
        for g in range(groups):
            part = slice(g * 128, (g + 1) * 128)
            score = dot(key_ref[part, :], query, 1, 1) * score_scale + bias[part, cols]
            scores[part, :] = score
            top = jnp.maximum(top, jnp.max(score.reshape(16, 8, width), axis=0))
        top = jnp.max(top, axis=0, keepdims=True)
        total = jnp.zeros((8, width), jnp.float32)
        for g in range(groups):
            part = slice(g * 128, (g + 1) * 128)
            raised = jnp.exp(scores[part, :] - top)
            total = total + jnp.sum(raised.reshape(16, 8, width), axis=0)
            raised_ref[0, part, cols] = raised.astype(low_type)
        inverse = 1.0 / jnp.sum(total, axis=0, keepdims=True)
        inverse_ref[0, :, cols] = inverse
        spread_ref[cols, :] = jnp.broadcast_to(inverse, (HEAD_DIM, width)).T
        mixed = dot(value_t[...], raised_ref[0, :, cols], 1, 0) * inverse
        attended_ref[cols, :] = mixed.T.astype(low_type)


def attend(packed, queries, keys, values, w_key, w_value, landed):
    rows, width = queries.shape
    ext = rows + sum(part.shape[0] for part in landed)
    by_row = pl.BlockSpec((rows, HEAD_DIM), lambda h: (0, h))
    by_ext = pl.BlockSpec((ext, HEAD_DIM), lambda h: (0, h))
    by_weight = pl.BlockSpec((width, HEAD_DIM), lambda h: (0, h))
    return pl.pallas_call(
        attend_kernel,
        grid=(HEADS,),
        in_specs=[
            pl.BlockSpec(packed.shape, lambda h: (0, 0, 0)),
            by_row,
            by_row,
            by_row,
            by_weight,
            by_weight,
        ]
        + [pl.BlockSpec(part.shape, lambda h: (0, 0)) for part in landed],
        out_specs=[
            by_row,
            pl.BlockSpec((1, ext, rows), lambda h: (h, 0, 0)),
            pl.BlockSpec((1, 1, rows), lambda h: (h, 0, 0)),
            by_row,
            by_ext,
            by_ext,
        ],
        out_shape=[
            shaped((rows, width)),
            shaped((HEADS, ext, rows)),
            shaped((HEADS, 1, rows), jnp.float32),
            shaped((rows, width), jnp.float32),
            shaped((ext, width)),
            shaped((ext, width)),
        ],
        scratch_shapes=[
            pltpu.VMEM((ext, rows), jnp.float32),
            pltpu.VMEM((ext, BLOCK), jnp.float32),
            pltpu.VMEM((HEAD_DIM, ext), low_type),
        ],
        compiler_params=pltpu.CompilerParams(vmem_limit_bytes=56 * 2**20),
        cost_estimate=pl.CostEstimate(flops=2**35, bytes_accessed=2**24, transcendentals=0),
    )(packed, queries, keys, values, w_key, w_value, *landed)


def attend_back_kernel(
    query_ref, key_ref, value_ref, grad_ref, raised_ref, inverse_ref, grad_query_ref, grad_key_ref, grad_value_ref, terms, low, key_t
):
    ext, rows = low.shape
    width = terms.shape[1]
    key_t[...] = key_ref[...].T

    @pl.loop(0, rows // width)
    def _(step):
        cols = pl.ds(pl.multiple_of(step * width, width), width)
        grad = grad_ref[cols, :]
        total = jnp.zeros((8, width), jnp.float32)
        for g in range(ext // 128):
            part = slice(g * 128, (g + 1) * 128)
            term = dot(value_ref[part, :], grad, 1, 1) * raised_ref[0, part, cols].astype(jnp.float32)
            terms[part, :] = term
            total = total + jnp.sum(term.reshape(16, 8, width), axis=0)
        mean = jnp.sum(total, axis=0, keepdims=True) * inverse_ref[0, :, cols]
        for g in range(ext // 128):
            part = slice(g * 128, (g + 1) * 128)
            low[part, cols] = (terms[part, :] - raised_ref[0, part, cols].astype(jnp.float32) * mean).astype(low_type)
        grad_query = dot(key_t[...], low[:, cols], 1, 0) * score_scale
        grad_query_ref[cols, :] = grad_query.T.astype(low_type)

    grad_value_ref[...] = dot(raised_ref[0], grad_ref[...], 1, 0).astype(low_type)
    grad_key_ref[...] = (dot(low[...], query_ref[...], 1, 0) * score_scale).astype(low_type)


def attend_back(first, heads, queries, keys, values, grads, raised, inverse):
    rows, ext = queries.shape[0], values.shape[0]
    by_row = pl.BlockSpec((rows, HEAD_DIM), lambda h: (0, h + first))
    by_ext = pl.BlockSpec((ext, HEAD_DIM), lambda h: (0, h + first))
    to_row = pl.BlockSpec((rows, HEAD_DIM), lambda h: (0, h))
    to_ext = pl.BlockSpec((ext, HEAD_DIM), lambda h: (0, h))
    return pl.pallas_call(
        attend_back_kernel,
        grid=(heads,),
        in_specs=[
            by_row,
            by_ext,
            by_ext,
            by_row,
            pl.BlockSpec((1, ext, rows), lambda h: (h + first, 0, 0)),
            pl.BlockSpec((1, 1, rows), lambda h: (h + first, 0, 0)),
        ],
        out_specs=[to_row, to_ext, to_ext],
        out_shape=[
            shaped((rows, heads * HEAD_DIM)),
            shaped((ext, heads * HEAD_DIM)),
            shaped((ext, heads * HEAD_DIM)),
        ],
        scratch_shapes=[
            pltpu.VMEM((ext, BLOCK), jnp.float32),
            pltpu.VMEM((ext, rows), low_type),
            pltpu.VMEM((HEAD_DIM, ext), low_type),
        ],
        compiler_params=pltpu.CompilerParams(vmem_limit_bytes=56 * 2**20),
        cost_estimate=pl.CostEstimate(flops=heads * 2**33, bytes_accessed=2**22, transcendentals=0),
    )(queries, keys, values, grads, raised, inverse)


def live_rows(count_ref, start, rows):
    place = lax.broadcasted_iota(jnp.int32, (rows, 1), 0) + start
    return (place < count_ref[0]).astype(jnp.float32)


def feed_chunk(weight_ref, second_ref, branch_ref, out_ref, grad_ref, hidden, grad_gate, grad_up, weight_grad_ref, fresh):
    width = second_ref.shape[1]
    units = weight_ref.shape[1]
    gate_rows, up_rows, down_rows = (slice(i * units, (i + 1) * units) for i in range(3))

    @pl.loop(0, second_ref.shape[0] // ROW_BLOCK)
    def _(step):
        rows = pl.ds(pl.multiple_of(step * ROW_BLOCK, ROW_BLOCK), ROW_BLOCK)
        second = second_ref[rows, :]
        gate = dot(second, weight_ref[gate_rows, :], 1, 0)
        up = dot(second, weight_ref[up_rows, :], 1, 0)
        sigmoid = 1.0 / (1.0 + jnp.exp(-gate))
        activated = gate * sigmoid
        hidden[rows, :] = (activated * up).astype(low_type)
        back = dot(branch_ref[rows, :], weight_ref[down_rows, :], 1, 1)
        grad_gate[rows, :] = (back * up * (sigmoid + activated * (1.0 - sigmoid))).astype(low_type)
        grad_up[rows, :] = (back * activated).astype(low_type)
        out = dot(hidden[rows, :], weight_ref[down_rows, :], 1, 0)
        grad = dot(grad_gate[rows, :], weight_ref[gate_rows, :], 1, 1) + dot(
            grad_up[rows, :], weight_ref[up_rows, :], 1, 1
        )
        if fresh:
            out_ref[rows, :] = out
            grad_ref[rows, :] = grad
        else:
            out_ref[rows, :] += out
            grad_ref[rows, :] += grad

    weight_grad_ref[gate_rows, :] = dot(second_ref[...], grad_gate[...], 0, 0).astype(low_type)
    weight_grad_ref[up_rows, :] = dot(second_ref[...], grad_up[...], 0, 0).astype(low_type)
    weight_grad_ref[down_rows, :] = dot(hidden[...], branch_ref[...], 0, 0).astype(low_type)


def feed_first_kernel(
    count_ref, modulation_ref, states_ref, cotangent_ref, attended_ref, w_out_ref, weight_a_ref, weight_b_ref,
    middle_ref, second_ref, branch_ref, out_ref, grad_ref, weight_grad_a_ref, weight_grad_b_ref,
    hidden, grad_gate, grad_up,
):
    @pl.loop(0, states_ref.shape[0] // ROW_BLOCK)
    def _(step):
        start = pl.multiple_of(step * ROW_BLOCK, ROW_BLOCK)
        rows = pl.ds(start, ROW_BLOCK)
        live = live_rows(count_ref, start, ROW_BLOCK)
        middle = states_ref[rows, :] + live * dot(attended_ref[rows, :], w_out_ref[...], 1, 0)
        middle_ref[rows, :] = middle
        plain, _ = norm_parts(middle)
        second_ref[rows, :] = (plain * (1.0 + modulation_ref[2:3, :]) + modulation_ref[3:4, :]).astype(low_type)
        branch_ref[rows, :] = (live * cotangent_ref[rows, :]).astype(low_type)

    for weight_ref, weight_grad_ref, fresh in (
        (weight_a_ref, weight_grad_a_ref, True),
        (weight_b_ref, weight_grad_b_ref, False),
    ):
        feed_chunk(
            weight_ref, second_ref, branch_ref, out_ref, grad_ref, hidden, grad_gate, grad_up, weight_grad_ref, fresh
        )


def feed_last_kernel(
    count_ref, modulation_ref, cotangent_ref, attended_ref, w_out_ref, spread_ref, weight_a_ref, weight_b_ref,
    middle_ref, second_ref, branch_ref, out_in_ref, grad_in_ref,
    output_ref, grad_middle_ref, grad_attended_ref, w_out_grad_ref, mod_grad_ref, weight_grad_a_ref, weight_grad_b_ref,
    hidden, grad_gate, grad_up, out, grad,
):
    for weight_ref, weight_grad_ref, fresh in (
        (weight_a_ref, weight_grad_a_ref, True),
        (weight_b_ref, weight_grad_b_ref, False),
    ):
        feed_chunk(weight_ref, second_ref, branch_ref, out, grad, hidden, grad_gate, grad_up, weight_grad_ref, fresh)
    mod_grad_ref[...] = jnp.zeros_like(mod_grad_ref)
    low_grad = hidden

    @pl.loop(0, middle_ref.shape[0] // ROW_BLOCK)
    def _(step):
        start = pl.multiple_of(step * ROW_BLOCK, ROW_BLOCK)
        rows = pl.ds(start, ROW_BLOCK)
        live = live_rows(count_ref, start, ROW_BLOCK)
        middle = middle_ref[rows, :]
        output_ref[rows, :] = middle + live * (out_in_ref[rows, :] + out[rows, :])
        plain, inverse = norm_parts(middle)
        grad_second = grad_in_ref[rows, :] + grad[rows, :]
        mod_grad_ref[0:1, :] += jnp.sum(grad_second * plain, axis=0, keepdims=True)
        mod_grad_ref[1:2, :] += jnp.sum(grad_second, axis=0, keepdims=True)
        grad_middle = cotangent_ref[rows, :] + norm_back(grad_second * (1.0 + modulation_ref[2:3, :]), plain, inverse)
        grad_middle_ref[rows, :] = grad_middle
        low_grad[rows, :] = (live * grad_middle).astype(low_type)
        grad_attended = dot(low_grad[rows, :], w_out_ref[...], 1, 1) * spread_ref[rows, :]
        grad_attended_ref[rows, :] = grad_attended.astype(low_type)

    w_out_grad_ref[...] = dot(attended_ref[...], low_grad[...], 0, 0).astype(low_type)


def project_back_kernel(parts, normed_ref, w_query_ref, w_key_ref, w_value_ref, *refs):
    landed_refs, refs = refs[:4], refs[4:]
    pieces, refs = refs[: 3 * parts], refs[3 * parts :]
    weight_grad_ref, grad_normed_ref, *parcel_refs = refs
    rows, width = normed_ref.shape
    cols = width // parts
    for kind, weight_ref in enumerate((w_query_ref, w_key_ref, w_value_ref)):
        for part in range(parts):
            piece = pieces[part * 3 + kind]
            to = slice(part * cols, (part + 1) * cols)
            grad = dot(normed_ref[...], piece[:rows, :], 0, 0)
            if kind:
                for position, landed_ref in enumerate(landed_refs):
                    sends = landed_ref.shape[0]
                    lower = rows + position * sends
                    grad += dot(landed_ref[...], piece[lower : lower + sends, :], 0, 0)
            weight_grad_ref[kind * width : (kind + 1) * width, to] = grad.astype(low_type)
    for position, parcel_ref in enumerate(parcel_refs):
        sends = parcel_ref.shape[0]
        lower = rows + position * sends
        parcel_ref[...] = sum(
            dot(pieces[part * 3 + kind][lower : lower + sends, :], weight_ref[:, part * cols : (part + 1) * cols], 1, 1)
            for part in range(parts)
            for kind, weight_ref in ((1, w_key_ref), (2, w_value_ref))
        ).astype(low_type)

    @pl.loop(0, rows // ROW_BLOCK)
    def _(step):
        block = pl.ds(pl.multiple_of(step * ROW_BLOCK, ROW_BLOCK), ROW_BLOCK)
        grad_normed_ref[block, :] = sum(
            dot(pieces[part * 3 + kind][block, :], weight_ref[:, part * cols : (part + 1) * cols], 1, 1)
            for part in range(parts)
            for kind, weight_ref in enumerate((w_query_ref, w_key_ref, w_value_ref))
        )


def finish_kernel(states_ref, modulation_ref, send_ref, grad_normed_ref, grad_middle_ref, *refs):
    returned_refs, (grad_states_ref, mod_grad_ref, chosen) = refs[:4], refs[4:]
    rows = states_ref.shape[0]
    sends = send_ref.shape[1]
    for position in range(len(returned_refs)):
        chosen[:, position * sends : (position + 1) * sends] = chosen_rows(send_ref, position, rows)
    mod_grad_ref[...] = jnp.zeros_like(mod_grad_ref)

    @pl.loop(0, rows // ROW_BLOCK)
    def _(step):
        block = pl.ds(pl.multiple_of(step * ROW_BLOCK, ROW_BLOCK), ROW_BLOCK)
        grad = grad_normed_ref[block, :]
        for position, returned_ref in enumerate(returned_refs):
            grad += dot(chosen[block, position * sends : (position + 1) * sends], returned_ref[...], 1, 0)
        plain, inverse = norm_parts(states_ref[block, :])
        mod_grad_ref[0:1, :] += jnp.sum(grad * plain, axis=0, keepdims=True)
        mod_grad_ref[1:2, :] += jnp.sum(grad, axis=0, keepdims=True)
        grad_states_ref[block, :] = grad_middle_ref[block, :] + norm_back(
            grad * (1.0 + modulation_ref[0:1, :]), plain, inverse
        )


def from_behind(block, axis, distance):
    devices = range(lax.axis_size(axis))
    route = [((i - distance) % len(devices), i) for i in devices]
    return lax.ppermute(block, axis, route)


def swap(block, axis, bit):
    return lax.ppermute(block, axis, [(i, i ^ (1 << bit)) for i in range(lax.axis_size(axis))])


def axis_bits(axis):
    return [(axis, bit) for bit in range(lax.axis_size(axis).bit_length() - 1)]


def side(axis, bit):
    return (lax.axis_index(axis) >> bit) & 1


def halve_sum(block, links):
    for axis, bit in links:
        half = block.shape[0] // 2
        here = side(axis, bit)
        kept = lax.dynamic_slice_in_dim(block, here * half, half)
        sent = lax.dynamic_slice_in_dim(block, (1 - here) * half, half)
        block = kept + swap(sent, axis, bit)
    return block


def join(block, links):
    for axis, bit in reversed(links):
        other = swap(block, axis, bit)
        here = side(axis, bit)
        block = jnp.where(here == 0, jnp.concatenate([block, other]), jnp.concatenate([other, block]))
    return block


def sum_all(block, links):
    return join(halve_sum(block, links), links)


def body(
    states,
    condition,
    mod_w,
    w_query,
    w_key,
    w_value,
    w_out,
    w_gate,
    w_up,
    w_down,
    counts,
    send_rows,
    neighbours,
    cotangent,
):
    rows, width = states.shape
    sends = send_rows.shape[2]
    ext = rows + len(halo_steps) * sends
    f32 = jnp.float32
    parcel = shaped((sends, width))
    send_list = send_rows[0]

    normed, modulation, *parcels = call(
        prepare_kernel,
        [shaped((rows, width)), shaped((4, width), f32)] + [parcel] * 4,
        (states, condition[:, None], mod_w, send_list),
        flops=2**30,
        moved=2**22,
    )
    landed = [from_behind(part, everywhere, hop) for part, hop in zip(parcels, halo_steps)]
    queries, keys, values, packed = call(
        project_kernel,
        [shaped((rows, width))] * 3 + [shaped((2, 128, rows), jnp.int32)],
        (normed, neighbours.T, w_query, w_key, w_value),
        flops=2**32,
        moved=2**22,
    )

    own_weights = jnp.concatenate([w_gate, w_up, w_down], axis=0)
    core_weights = swap(own_weights, "hid", 0)
    landed, late_weights = lax.optimization_barrier((landed, own_weights))
    far_weights = swap(late_weights, "hid", 1)
    cross_weights = swap(far_weights, "hid", 0)

    attended, raised, inverse, spread, keys, values = attend(packed, queries, keys, values, w_key, w_value, landed)

    low_rows = shaped((rows, width))
    wide_rows = shaped((rows, width), f32)
    weight_grad = shaped(own_weights.shape)
    row_scratch = [pltpu.VMEM((rows, width), low_type)] * 3
    middle, second, branch, out, grad, own_grad, core_grad = call(
        feed_first_kernel,
        [wide_rows, low_rows, low_rows, wide_rows, wide_rows, weight_grad, weight_grad],
        (counts, modulation, states, cotangent, attended, w_out, own_weights, core_weights),
        specs=[scalars] + [whole] * 7,
        scratch=row_scratch,
        flops=2**34,
        moved=2**24,
    )
    output, grad_middle, grad_attended, w_out_grad, mod_two, far_grad, cross_grad = call(
        feed_last_kernel,
        [wide_rows, wide_rows, low_rows, shaped((width, width)), shaped((2, width), f32), weight_grad, weight_grad],
        (counts, modulation, cotangent, attended, w_out, spread, far_weights, cross_weights)
        + (middle, second, branch, out, grad),
        specs=[scalars] + [whole] * 12,
        scratch=row_scratch + [pltpu.VMEM((rows, width), f32)] * 2,
        flops=2**34,
        moved=2**24,
    )

    node_links = axis_bits("nodes")
    all_links = axis_bits("hid") + node_links
    own_grad = own_grad + swap(core_grad, "hid", 0)
    far_grad = far_grad + swap(cross_grad, "hid", 0)
    own_grad = own_grad + swap(far_grad, "hid", 1)
    own_grad = sum_all(own_grad, node_links)
    grad_w_gate, grad_w_up, grad_w_down = jnp.split(own_grad.astype(f32), 3)
    grad_w_out = sum_all(w_out_grad, all_links).astype(f32)

    parts = 2
    pieces = []
    for part in range(parts):
        heads = HEADS // parts
        pieces += attend_back(part * heads, heads, queries, keys, values, grad_attended, raised, inverse)
    attn_grad, grad_normed, *parcels = call(
        functools.partial(project_back_kernel, parts),
        [shaped((3 * width, width)), wide_rows] + [parcel] * 4,
        (normed, w_query, w_key, w_value, *landed, *pieces),
        flops=2**32,
        moved=2**23,
    )
    returned = [from_behind(part, everywhere, -hop) for part, hop in zip(parcels, halo_steps)]
    attn_grad = sum_all(attn_grad, all_links)
    grad_w_query, grad_w_key, grad_w_value = jnp.split(attn_grad.astype(f32), 3)
    grad_states, mod_one = call(
        finish_kernel,
        [wide_rows, shaped((2, width), f32)],
        (states, modulation, send_list, grad_normed, grad_middle, *returned),
        scratch=[pltpu.VMEM((rows, 4 * sends), low_type)],
        flops=2**31,
        moved=2**23,
    )
    mod_grad = jnp.concatenate([mod_one, mod_two])
    for axis, bit in all_links:
        mod_grad = mod_grad + swap(mod_grad, axis, bit)
    mod_grad = mod_grad.reshape(-1)
    grad_mod_w = condition[:, None] * mod_grad[None, :]
    grad_condition = jnp.sum(mod_w.astype(f32) * mod_grad[None, :], axis=1)
    return (
        output,
        grad_states,
        grad_condition,
        grad_mod_w,
        grad_w_query,
        grad_w_key,
        grad_w_value,
        grad_w_out,
        grad_w_gate,
        grad_w_up,
        grad_w_down,
    )


def solution(mesh):
    rows = P(everywhere, None)
    placed = (
        rows,
        P(),
        P(),
        P(),
        P(),
        P(),
        P(),
        P(None, "hid"),
        P(None, "hid"),
        P("hid", None),
        P(everywhere),
        P(everywhere, None, None),
        rows,
        rows,
    )
    return jax.shard_map(
        body,
        mesh=mesh,
        in_specs=placed,
        out_specs=(rows, rows, P(), P(), P(), P(), P(), P(), P(None, "hid"), P(None, "hid"), P("hid", None)),
        check_vma=False,
    )
```

```python
import functools

import jax
import jax.numpy as jnp
from jax import lax
from jax.experimental import pallas as pl
from jax.experimental.pallas import tpu as pltpu
from jax.sharding import PartitionSpec as P

HEADS = 4
HEAD_DIM = 128
NEIGH = 16
BLOCK = 512
ROW_BLOCK = 256

epsilon = 1e-06
halo_steps = (1, -1, 2, -2)
highest = lax.Precision.HIGHEST
score_scale = HEAD_DIM ** (-0.5)
low_type = jnp.bfloat16
everywhere = ("nodes", "hid")
whole = pl.BlockSpec(memory_space=pltpu.VMEM)
scalars = pl.BlockSpec(memory_space=pltpu.SMEM)
anywhere = pl.BlockSpec(memory_space=pl.ANY)


def dot(left, right, left_dim, right_dim):
    return lax.dot_general(
        left, right, (((left_dim,), (right_dim,)), ((), ())), preferred_element_type=jnp.float32
    )


def shaped(shape, dtype=low_type):
    return jax.ShapeDtypeStruct(shape, dtype)


def norm_parts(states):
    centred = states - jnp.mean(states, axis=-1, keepdims=True)
    inverse = lax.rsqrt(jnp.mean(centred * centred, axis=-1, keepdims=True) + epsilon)
    return (centred * inverse, inverse)


def norm_back(grad_plain, plain, inverse):
    first_mean = jnp.mean(grad_plain, axis=-1, keepdims=True)
    second_mean = jnp.mean(grad_plain * plain, axis=-1, keepdims=True)
    return inverse * (grad_plain - first_mean - plain * second_mean)


def call(kernel, out_shape, args, specs=None, out_specs=None, scratch=(), flops=0, moved=0):
    single = not isinstance(out_shape, list)
    return pl.pallas_call(
        kernel,
        in_specs=specs or [whole] * len(args),
        out_specs=out_specs or (whole if single else [whole] * len(out_shape)),
        out_shape=out_shape,
        scratch_shapes=list(scratch),
        compiler_params=pltpu.CompilerParams(vmem_limit_bytes=56 * 2**20),
        cost_estimate=pl.CostEstimate(flops=flops, bytes_accessed=moved, transcendentals=0),
    )(*args)


def chosen_rows(send_ref, position, rows, first=0):
    sends = send_ref.shape[1]
    place = lax.broadcasted_iota(jnp.int32, (rows, sends), 0) + first
    return jnp.where(place == send_ref[position : position + 1, :], 1.0, 0.0).astype(low_type)


def prepare_kernel(states_ref, condition_ref, mod_w_ref, send_ref, normed_ref, plain_ref, modulation_ref, *parcel_refs):
    width = states_ref.shape[1]
    mixed = sum(
        condition_ref[i] * mod_w_ref[i : i + 1, :].astype(jnp.float32) for i in range(condition_ref.shape[0])
    )
    for piece in range(4):
        modulation_ref[piece : piece + 1, :] = mixed[:, piece * width : (piece + 1) * width]

    @pl.loop(0, states_ref.shape[0] // ROW_BLOCK)
    def _(step):
        rows = pl.ds(pl.multiple_of(step * ROW_BLOCK, ROW_BLOCK), ROW_BLOCK)
        plain, _ = norm_parts(states_ref[rows, :])
        plain_ref[rows, :] = plain.astype(low_type)
        normed_ref[rows, :] = (plain * (1.0 + modulation_ref[0:1, :]) + modulation_ref[1:2, :]).astype(low_type)

    for position, parcel_ref in enumerate(parcel_refs):
        chosen = chosen_rows(send_ref, position, states_ref.shape[0])
        parcel_ref[...] = dot(chosen, plain_ref[...], 0, 0).astype(low_type)


def count_near(near_ref, cols, groups):
    half = groups // 2
    near = near_ref[:, cols]
    group = near >> 7
    upper = group >= half
    unit = jnp.left_shift(1, 5 * jnp.where(upper, group - half, group))
    low = near & 127
    low_unit = jnp.where(upper, 0, unit)
    high_unit = jnp.where(upper, unit, 0)
    place = lax.broadcasted_iota(jnp.int32, (128, 128), 0)
    low_count = jnp.zeros((128, 128), jnp.int32)
    high_count = low_count
    for n in range(NEIGH):
        same = low[n : n + 1] == place
        low_count = low_count + jnp.where(same, low_unit[n : n + 1], 0)
        high_count = high_count + jnp.where(same, high_unit[n : n + 1], 0)
    return low_count, high_count


def count_bias(packed, position):
    count = (packed >> (5 * position)) & 31
    return jnp.where(count > 0, jnp.log(count.astype(jnp.float32)), -1e30)


def score_pass(key_ref, query, bias, scores, cols, top):
    width = scores.shape[1]
    for g in range(scores.shape[0] // 128):
        part = slice(g * 128, (g + 1) * 128)
        score = dot(key_ref[part, :], query, 1, 1) * score_scale + bias[part, cols]
        scores[part, :] = score
        top = jnp.maximum(top, jnp.max(score.reshape(16, 8, width), axis=0))
    return jnp.max(top, axis=0, keepdims=True)


def raise_pass(scores, top, raised_ref, cols):
    width = scores.shape[1]
    total = jnp.zeros((8, width), jnp.float32)
    for g in range(scores.shape[0] // 128):
        part = slice(g * 128, (g + 1) * 128)
        raised = jnp.exp(scores[part, :] - top)
        total = total + jnp.sum(raised.reshape(16, 8, width), axis=0)
        raised_ref[0, part, cols] = raised.astype(low_type)
    return jnp.sum(total, axis=0, keepdims=True)


def attend_own_kernel(
    groups, normed_ref, near_ref, w_query_ref, w_key_ref, w_value_ref,
    query_ref, key_ref, value_ref, raised_ref, top_ref, total_ref, mixed_ref, packed_ref,
    bias, scores, value_t,
):
    rows = normed_ref.shape[0]
    half = groups // 2

    @pl.when(pl.program_id(0) == 0)
    def _():
        @pl.loop(0, rows // 128)
        def _(step):
            cols = pl.ds(pl.multiple_of(step * 128, 128), 128)
            packed = count_near(near_ref, cols, groups)
            packed_ref[:, cols] = packed[1]
            for g in range(rows // 128):
                bias[g * 128 : (g + 1) * 128, cols] = count_bias(packed[g // half], g % half)

    for weight_ref, out_ref in ((w_query_ref, query_ref), (w_key_ref, key_ref), (w_value_ref, value_ref)):
        out_ref[...] = dot(normed_ref[...], weight_ref[...], 1, 0).astype(low_type)
    value_t[...] = value_ref[...].T
    width = scores.shape[1]

    @pl.loop(0, rows // width)
    def _(step):
        cols = pl.ds(pl.multiple_of(step * width, width), width)
        least = jnp.full((8, width), -jnp.inf, jnp.float32)
        top = score_pass(key_ref, query_ref[cols, :], bias, scores, cols, least)
        top_ref[0, :, cols] = top
        total_ref[0, :, cols] = raise_pass(scores, top, raised_ref, cols)
        mixed_ref[0, :, cols] = dot(value_t[...], raised_ref[0, :, cols], 1, 0)


def attend_own(normed, near, w_query, w_key, w_value, far_rows):
    rows, width = normed.shape
    groups = (rows + far_rows) // 128
    by_row = pl.BlockSpec((rows, HEAD_DIM), lambda h: (0, h))
    by_weight = pl.BlockSpec((width, HEAD_DIM), lambda h: (0, h))
    by_head = pl.BlockSpec((1, 1, rows), lambda h: (h, 0, 0))
    return pl.pallas_call(
        functools.partial(attend_own_kernel, groups),
        grid=(HEADS,),
        in_specs=[pl.BlockSpec((rows, width), lambda h: (0, 0)), pl.BlockSpec((NEIGH, rows), lambda h: (0, 0))]
        + [by_weight] * 3,
        out_specs=[
            by_row,
            by_row,
            by_row,
            pl.BlockSpec((1, rows, rows), lambda h: (h, 0, 0)),
            by_head,
            by_head,
            pl.BlockSpec((1, HEAD_DIM, rows), lambda h: (h, 0, 0)),
            pl.BlockSpec((128, rows), lambda h: (0, 0)),
        ],
        out_shape=[shaped((rows, width))] * 3
        + [
            shaped((HEADS, rows, rows)),
            shaped((HEADS, 1, rows), jnp.float32),
            shaped((HEADS, 1, rows), jnp.float32),
            shaped((HEADS, HEAD_DIM, rows), jnp.float32),
            shaped((128, rows), jnp.int32),
        ],
        scratch_shapes=[
            pltpu.VMEM((rows, rows), jnp.float32),
            pltpu.VMEM((rows, BLOCK), jnp.float32),
            pltpu.VMEM((HEAD_DIM, rows), low_type),
        ],
        compiler_params=pltpu.CompilerParams(vmem_limit_bytes=48 * 2**20),
        cost_estimate=pl.CostEstimate(flops=2**34, bytes_accessed=2**24, transcendentals=0),
    )(normed, near, w_query, w_key, w_value)


def fetch(parts, to_ref, sems):
    copies, lower = [], 0
    for position, part in enumerate(parts):
        upper = lower + part.shape[0]
        copies.append(pltpu.make_async_copy(part, to_ref.at[lower:upper, :], sems.at[position]))
        copies[-1].start()
        lower = upper
    return copies


def attend_far_kernel(
    skip, modulation_ref, query_ref, w_key_ref, w_value_ref, packed_ref, top_ref, total_ref, mixed_ref, *refs
):
    landed_refs, refs = refs[:4], refs[4:]
    attended_ref, raised_ref, spread_own_ref, spread_far_ref, key_ref, value_ref, plain_ref, normed_ref, *refs = refs
    bias, scores, value_t, sems = refs
    far, rows = bias.shape

    @pl.when(pl.program_id(0) == 0)
    def _():
        copies = fetch(landed_refs, plain_ref, sems)

        @pl.loop(0, rows // 128)
        def _(step):
            cols = pl.ds(pl.multiple_of(step * 128, 128), 128)
            for g in range(far // 128):
                bias[g * 128 : (g + 1) * 128, cols] = count_bias(packed_ref[:, cols], g + skip)

        for copy in copies:
            copy.wait()
        plain = plain_ref[...].astype(jnp.float32)
        normed_ref[...] = (plain * (1.0 + modulation_ref[0:1, :]) + modulation_ref[1:2, :]).astype(low_type)

    key_ref[...] = dot(normed_ref[...], w_key_ref[...], 1, 0).astype(low_type)
    value_ref[...] = dot(normed_ref[...], w_value_ref[...], 1, 0).astype(low_type)
    value_t[...] = value_ref[...].T
    width = scores.shape[1]

    @pl.loop(0, rows // width)
    def _(step):
        cols = pl.ds(pl.multiple_of(step * width, width), width)
        own_top = top_ref[0, :, cols]
        least = jnp.broadcast_to(own_top, (8, width))
        top = score_pass(key_ref, query_ref[cols, :], bias, scores, cols, least)
        factor = jnp.exp(own_top - top)
        total = raise_pass(scores, top, raised_ref, cols) + total_ref[0, :, cols] * factor
        inverse = 1.0 / total
        own_inverse = inverse * factor
        spread_far_ref[cols, :] = jnp.broadcast_to(inverse, (HEAD_DIM, width)).T
        spread_own_ref[cols, :] = jnp.broadcast_to(own_inverse, (HEAD_DIM, width)).T
        mixed = dot(value_t[...], raised_ref[0, :, cols], 1, 0) * inverse + mixed_ref[0, :, cols] * own_inverse
        attended_ref[cols, :] = mixed.T.astype(low_type)


def attend_far(modulation, queries, w_key, w_value, packed, top, total, mixed, landed):
    rows, width = queries.shape
    far = sum(part.shape[0] for part in landed)
    by_row = pl.BlockSpec((rows, HEAD_DIM), lambda h: (0, h))
    by_far = pl.BlockSpec((far, HEAD_DIM), lambda h: (0, h))
    by_weight = pl.BlockSpec((width, HEAD_DIM), lambda h: (0, h))
    by_head = pl.BlockSpec((1, 1, rows), lambda h: (h, 0, 0))
    groups = (rows + far) // 128
    return pl.pallas_call(
        functools.partial(attend_far_kernel, rows // 128 - groups // 2),
        grid=(HEADS,),
        in_specs=[
            pl.BlockSpec(modulation.shape, lambda h: (0, 0)),
            by_row,
            by_weight,
            by_weight,
            pl.BlockSpec(packed.shape, lambda h: (0, 0)),
            by_head,
            by_head,
            pl.BlockSpec((1, HEAD_DIM, rows), lambda h: (h, 0, 0)),
        ]
        + [anywhere] * len(landed),
        out_specs=[by_row, pl.BlockSpec((1, far, rows), lambda h: (h, 0, 0)), by_row, by_row, by_far, by_far]
        + [pl.BlockSpec((far, width), lambda h: (0, 0))] * 2,
        out_shape=[
            shaped((rows, width)),
            shaped((HEADS, far, rows)),
            shaped((rows, width), jnp.float32),
            shaped((rows, width), jnp.float32),
            shaped((far, width)),
            shaped((far, width)),
            shaped((far, width)),
            shaped((far, width)),
        ],
        scratch_shapes=[
            pltpu.VMEM((far, rows), jnp.float32),
            pltpu.VMEM((far, BLOCK), jnp.float32),
            pltpu.VMEM((HEAD_DIM, far), low_type),
            pltpu.SemaphoreType.DMA((len(landed),)),
        ],
        compiler_params=pltpu.CompilerParams(vmem_limit_bytes=48 * 2**20),
        cost_estimate=pl.CostEstimate(flops=2**33, bytes_accessed=2**23, transcendentals=0),
    )(modulation, queries, w_key, w_value, packed, top, total, mixed, *landed)


def attend_back_kernel(query_ref, attended_ref, *refs):
    sides, refs = (refs[:4], refs[4:8]), refs[8:]
    grad_query_ref, refs = refs[0], refs[1:]
    grads, scratch = (refs[0:2], refs[2:4]), (refs[4:6], refs[6:8])
    rows = query_ref.shape[0]
    for (key_ref, *_), (_, key_t) in zip(sides, scratch):
        key_t[...] = key_ref[...].T

    @pl.loop(0, rows // BLOCK)
    def _(step):
        cols = pl.ds(pl.multiple_of(step * BLOCK, BLOCK), BLOCK)
        attended = attended_ref[cols, :].astype(jnp.float32)
        total = 0.0
        for (_, value_ref, grad_ref, raised_ref), (low, key_t) in zip(sides, scratch):
            grad = grad_ref[cols, :]
            mean = jnp.sum((grad.astype(jnp.float32) * attended).T, axis=0, keepdims=True)
            for g in range(value_ref.shape[0] // 128):
                part = slice(g * 128, (g + 1) * 128)
                term = dot(value_ref[part, :], grad, 1, 1) - mean
                low[part, cols] = (term * raised_ref[0, part, cols].astype(jnp.float32)).astype(low_type)
            total = total + dot(key_t[...], low[:, cols], 1, 0)
        grad_query_ref[cols, :] = (total * score_scale).T.astype(low_type)

    for (_, _, grad_ref, raised_ref), (low, _), (grad_key_ref, grad_value_ref) in zip(sides, scratch, grads):
        grad_value_ref[...] = dot(raised_ref[0], grad_ref[...], 1, 0).astype(low_type)
        grad_key_ref[...] = (dot(low[...], query_ref[...], 1, 0) * score_scale).astype(low_type)


def attend_back(first, heads, queries, attended, own, far):
    rows = queries.shape[0]
    by_row = pl.BlockSpec((rows, HEAD_DIM), lambda h: (0, h + first))
    in_specs, out_specs, out_shape, scratch = [], [], [], []
    for keys, _, _, raised in (own, far):
        count = keys.shape[0]
        by_count = pl.BlockSpec((count, HEAD_DIM), lambda h: (0, h + first))
        in_specs += [by_count, by_count, by_row, pl.BlockSpec((1, count, rows), lambda h: (h + first, 0, 0))]
        out_specs += [pl.BlockSpec((count, HEAD_DIM), lambda h: (0, h))] * 2
        out_shape += [shaped((count, heads * HEAD_DIM))] * 2
        scratch += [pltpu.VMEM((count, rows), low_type), pltpu.VMEM((HEAD_DIM, count), low_type)]
    return pl.pallas_call(
        attend_back_kernel,
        grid=(heads,),
        in_specs=[by_row, by_row] + in_specs,
        out_specs=[pl.BlockSpec((rows, HEAD_DIM), lambda h: (0, h))] + out_specs,
        out_shape=[shaped((rows, heads * HEAD_DIM))] + out_shape,
        scratch_shapes=scratch,
        compiler_params=pltpu.CompilerParams(vmem_limit_bytes=48 * 2**20),
        cost_estimate=pl.CostEstimate(flops=heads * 2**33, bytes_accessed=2**22, transcendentals=0),
    )(queries, attended, *own, *far)


def live_rows(count_ref, start, rows):
    place = lax.broadcasted_iota(jnp.int32, (rows, 1), 0) + start
    return (place < count_ref[0]).astype(jnp.float32)


class Mover:
    def __init__(self, sems):
        self.sems, self.used, self.open = sems, 0, []

    def start(self, source, target):
        copy = pltpu.make_async_copy(source, target, self.sems.at[self.used])
        self.used += 1
        copy.start()
        return copy

    def send(self, source, target):
        self.open.append(self.start(source, target))

    def finish(self):
        for copy in self.open:
            copy.wait()


def feed_chunk(weight_ref, second_ref, branch_ref, out_ref, grad_ref, hidden, grad_gate, grad_up, store, fresh, done):
    units = weight_ref.shape[0] // 3
    gate_rows, up_rows, down_rows = (slice(i * units, (i + 1) * units) for i in range(3))
    for step in range(second_ref.shape[0] // ROW_BLOCK):
        rows = slice(step * ROW_BLOCK, (step + 1) * ROW_BLOCK)
        second = second_ref[rows, :]
        gate = dot(second, weight_ref[gate_rows, :], 1, 0)
        up = dot(second, weight_ref[up_rows, :], 1, 0)
        sigmoid = 1.0 / (1.0 + jnp.exp(-gate))
        activated = gate * sigmoid
        hidden[rows, :] = (activated * up).astype(low_type)
        back = dot(branch_ref[rows, :], weight_ref[down_rows, :], 1, 1)
        grad_gate[rows, :] = (back * up * (sigmoid + activated * (1.0 - sigmoid))).astype(low_type)
        grad_up[rows, :] = (back * activated).astype(low_type)
        out = dot(hidden[rows, :], weight_ref[down_rows, :], 1, 0)
        grad = dot(grad_gate[rows, :], weight_ref[gate_rows, :], 1, 1) + dot(
            grad_up[rows, :], weight_ref[up_rows, :], 1, 1
        )
        if fresh:
            out_ref[rows, :] = out
            grad_ref[rows, :] = grad
        else:
            out_ref[rows, :] += out
            grad_ref[rows, :] += grad
        if done is not None:
            done(rows)

    one, two = store
    half = units // 2
    one[:units, :] = dot(second_ref[...], grad_gate[...], 0, 0).astype(low_type)
    grad_up_weight = dot(second_ref[...], grad_up[...], 0, 0).astype(low_type)
    one[units:, :] = grad_up_weight[:half, :]
    two[:half, :] = grad_up_weight[half:, :]
    two[half : half + units, :] = dot(hidden[...], branch_ref[...], 0, 0).astype(low_type)


def feed_first_kernel(
    count_ref, modulation_ref, states_in, cotangent_in, attended_in, w_out_in, core_in, own_in,
    middle_out, second_out, branch_out, out_out, grad_out, core_one_out, core_two_out, own_one_out, own_two_out,
    states, cotangent, attended, w_out, core, own, second, branch, out, grad,
    core_one, core_two, own_one, own_two, hidden, grad_gate, grad_up, in_sems, out_sems,
):
    come, go = Mover(in_sems), Mover(out_sems)
    w_out_copy = come.start(w_out_in, w_out)
    blocks = [slice(lower, lower + ROW_BLOCK) for lower in range(0, states.shape[0], ROW_BLOCK)]
    row_copies = [
        [come.start(source.at[rows, :], target.at[rows, :])
         for source, target in ((attended_in, attended), (states_in, states), (cotangent_in, cotangent))]
        for rows in blocks
    ]
    weight_copies = [come.start(core_in, core), come.start(own_in, own)]
    w_out_copy.wait()
    for rows, copies in zip(blocks, row_copies):
        for copy in copies:
            copy.wait()
        live = live_rows(count_ref, rows.start, ROW_BLOCK)
        middle = states[rows, :] + live * dot(attended[rows, :], w_out[...], 1, 0)
        states[rows, :] = middle
        plain, _ = norm_parts(middle)
        second[rows, :] = (plain * (1.0 + modulation_ref[2:3, :]) + modulation_ref[3:4, :]).astype(low_type)
        branch[rows, :] = (live * cotangent[rows, :]).astype(low_type)
        for source, target in ((states, middle_out), (second, second_out), (branch, branch_out)):
            go.send(source.at[rows, :], target.at[rows, :])

    def done(rows):
        go.send(out.at[rows, :], out_out.at[rows, :])
        go.send(grad.at[rows, :], grad_out.at[rows, :])

    scratch = (hidden, grad_gate, grad_up)
    weight_copies[0].wait()
    feed_chunk(core, second, branch, out, grad, *scratch, (core_one, core_two), True, None)
    go.send(core_one, core_one_out)
    go.send(core_two, core_two_out)
    weight_copies[1].wait()
    feed_chunk(own, second, branch, out, grad, *scratch, (own_one, own_two), False, done)
    go.send(own_one, own_one_out)
    go.send(own_two, own_two_out)
    go.finish()


def feed_last_kernel(
    count_ref, core_ref, modulation_ref, cotangent_in, attended_in, w_out_in, spread_own_in, spread_far_in,
    middle_in, second_in, branch_in, out_in, grad_in, cross_in, far_in,
    output_out, grad_middle_out, grad_own_out, grad_far_out, mod_grad_ref,
    cross_one_out, cross_two_out, far_one_out, far_two_out,
    cotangent, attended, w_out, spread_own, spread_far, middle, second, branch, out, grad, cross, far,
    grad_own, grad_far, cross_one, cross_two, far_one, far_two, w_out_grad,
    hidden, grad_gate, grad_up, in_sems, out_sems,
):
    come, go = Mover(in_sems), Mover(out_sems)
    first_copies = [
        come.start(source, target)
        for source, target in ((second_in, second), (cross_in, cross), (branch_in, branch), (out_in, out), (grad_in, grad))
    ]
    late_copies = [
        come.start(source, target)
        for source, target in (
            (far_in, far), (w_out_in, w_out), (middle_in, middle), (cotangent_in, cotangent),
            (spread_own_in, spread_own), (spread_far_in, spread_far), (attended_in, attended),
        )
    ]
    scratch = (hidden, grad_gate, grad_up)
    for copy in first_copies:
        copy.wait()
    feed_chunk(cross, second, branch, out, grad, *scratch, (cross_one, cross_two), False, None)
    go.send(cross_one, cross_one_out)
    for copy in late_copies:
        copy.wait()
    feed_chunk(far, second, branch, out, grad, *scratch, (far_one, far_two), False, None)
    go.send(far_one, far_one_out)
    low_grad = hidden
    scale, bias = 0.0, 0.0
    for lower in range(0, middle.shape[0], ROW_BLOCK):
        rows = slice(lower, lower + ROW_BLOCK)
        live = live_rows(count_ref, lower, ROW_BLOCK)
        block = middle[rows, :]
        plain, inverse = norm_parts(block)
        middle[rows, :] = block + live * out[rows, :]
        go.send(middle.at[rows, :], output_out.at[rows, :])
        grad_second = grad[rows, :]
        scale += jnp.sum(grad_second * plain, axis=0, keepdims=True)
        bias += jnp.sum(grad_second, axis=0, keepdims=True)
        grad_middle = cotangent[rows, :] + norm_back(grad_second * (1.0 + modulation_ref[2:3, :]), plain, inverse)
        cotangent[rows, :] = grad_middle
        go.send(cotangent.at[rows, :], grad_middle_out.at[rows, :])
        low_grad[rows, :] = (live * grad_middle).astype(low_type)
        grad_attended = dot(low_grad[rows, :], w_out[...], 1, 1)
        grad_own[rows, :] = (grad_attended * spread_own[rows, :]).astype(low_type)
        grad_far[rows, :] = (grad_attended * spread_far[rows, :]).astype(low_type)
        go.send(grad_own.at[rows, :], grad_own_out.at[rows, :])
        go.send(grad_far.at[rows, :], grad_far_out.at[rows, :])
    mod_grad_ref[0:1, :] = scale
    mod_grad_ref[1:2, :] = bias

    half = w_out_grad.shape[0] // 2
    w_out_grad[...] = dot(attended[...], low_grad[...], 0, 0).astype(low_type)
    for two, two_out, side_of in ((far_two, far_two_out, core_ref[0]), (cross_two, cross_two_out, 1 - core_ref[0])):
        start = pl.multiple_of(side_of * half, half)
        two[two.shape[0] - half :, :] = w_out_grad[pl.ds(start, half), :]
        go.send(two, two_out)
    go.finish()


def return_kernel(parts, w_key_ref, w_value_ref, *refs):
    plain_ref, *refs = refs
    pieces, (*parcel_refs, mod_grad_ref) = refs[: 2 * parts], refs[2 * parts :]
    cols = w_key_ref.shape[1] // parts
    scale, bias = 0.0, 0.0
    for position, parcel_ref in enumerate(parcel_refs):
        sends = parcel_ref.shape[0]
        part_rows = slice(position * sends, (position + 1) * sends)
        grad = sum(
            dot(pieces[part * 2 + kind][part_rows, :], weight_ref[:, part * cols : (part + 1) * cols], 1, 1)
            for part in range(parts)
            for kind, weight_ref in enumerate((w_key_ref, w_value_ref))
        )
        scale += jnp.sum(grad * plain_ref[part_rows, :].astype(jnp.float32), axis=0, keepdims=True)
        bias += jnp.sum(grad, axis=0, keepdims=True)
        parcel_ref[...] = grad.astype(low_type)
    mod_grad_ref[0:1, :] = scale
    mod_grad_ref[1:2, :] = bias


def project_back_kernel(
    parts, normed_ref, plain_ref, normed_far_ref, mod_far_ref, mod_two_ref, w_query_ref, w_key_ref, w_value_ref, *refs
):
    pieces, refs = refs[: 5 * parts], refs[5 * parts :]
    weight_grad_ref, grad_normed_ref, mod_grad_ref = refs
    rows, width = normed_ref.shape
    cols = width // parts
    for kind in range(3):
        for part in range(parts):
            grad = dot(normed_ref[...], pieces[part * 5 + kind][...], 0, 0)
            if kind:
                grad += dot(normed_far_ref[...], pieces[part * 5 + kind + 2][...], 0, 0)
            weight_grad_ref[kind, :, part * cols : (part + 1) * cols] = grad.astype(low_type)
    mod_grad_ref[0:2, :] = mod_far_ref[...]
    mod_grad_ref[2:4, :] = mod_two_ref[...]

    @pl.loop(0, rows // ROW_BLOCK)
    def _(step):
        block = pl.ds(pl.multiple_of(step * ROW_BLOCK, ROW_BLOCK), ROW_BLOCK)
        grad = sum(
            dot(pieces[part * 5 + kind][block, :], weight_ref[:, part * cols : (part + 1) * cols], 1, 1)
            for part in range(parts)
            for kind, weight_ref in enumerate((w_query_ref, w_key_ref, w_value_ref))
        )
        grad_normed_ref[block, :] = grad
        mod_grad_ref[0:1, :] += jnp.sum(grad * plain_ref[block, :].astype(jnp.float32), axis=0, keepdims=True)
        mod_grad_ref[1:2, :] += jnp.sum(grad, axis=0, keepdims=True)


def finish_kernel(states_ref, grad_normed_ref, grad_middle_ref, modulation_ref, send_ref, *refs):
    returned_refs, (grad_states_ref, returned, sems) = refs[:4], refs[4:]

    @pl.when(pl.program_id(0) == 0)
    def _():
        for copy in fetch(returned_refs, returned, sems):
            copy.wait()

    rows = states_ref.shape[0]
    sends = send_ref.shape[1]
    grad = grad_normed_ref[...]
    for position in range(len(returned_refs)):
        chosen = chosen_rows(send_ref, position, rows, pl.program_id(0) * rows)
        grad += dot(chosen, returned[position * sends : (position + 1) * sends, :], 1, 0)
    plain, inverse = norm_parts(states_ref[...])
    grad_states_ref[...] = grad_middle_ref[...] + norm_back(grad * (1.0 + modulation_ref[0:1, :]), plain, inverse)


def finish(states, grad_normed, grad_middle, modulation, send_list, returned):
    rows, width = states.shape
    by_block = pl.BlockSpec((ROW_BLOCK, width), lambda i: (i, 0))
    return pl.pallas_call(
        finish_kernel,
        grid=(rows // ROW_BLOCK,),
        in_specs=[by_block] * 3
        + [pl.BlockSpec(modulation.shape, lambda i: (0, 0)), pl.BlockSpec(send_list.shape, lambda i: (0, 0))]
        + [anywhere] * len(returned),
        out_specs=by_block,
        out_shape=shaped((rows, width), jnp.float32),
        scratch_shapes=[
            pltpu.VMEM((sum(part.shape[0] for part in returned), width), low_type),
            pltpu.SemaphoreType.DMA((len(returned),)),
        ],
        compiler_params=pltpu.CompilerParams(vmem_limit_bytes=32 * 2**20),
        cost_estimate=pl.CostEstimate(flops=2**31, bytes_accessed=2**23, transcendentals=0),
    )(states, grad_normed, grad_middle, modulation, send_list, *returned)


def from_behind(block, axis, distance):
    devices = range(lax.axis_size(axis))
    route = [((i - distance) % len(devices), i) for i in devices]
    return lax.ppermute(block, axis, route)


def swap(block, mask):
    count = lax.axis_size("nodes") * lax.axis_size("hid")
    return lax.ppermute(block, everywhere, [(i, i ^ mask) for i in range(count)])


def place():
    return lax.axis_index("nodes") * lax.axis_size("hid") + lax.axis_index("hid")


def side(link):
    return (place() >> link) & 1


def pieces_of(block, count, index):
    size = block.shape[1] // count
    return lax.dynamic_slice_in_dim(block, index * size, size, 1)


def half_sum(block, link):
    return pieces_of(block, 2, side(link)) + swap(pieces_of(block, 2, 1 - side(link)), 1 << link)


def half_join(block, link):
    other = swap(block, 1 << link)
    return jnp.where(
        side(link) == 0, jnp.concatenate([block, other], axis=1), jnp.concatenate([other, block], axis=1)
    )


def pack_wide(values):
    high = lax.reduce_precision(values, 8, 7)
    both = jnp.concatenate([high, values - high]).astype(low_type)
    return jnp.concatenate([both, jnp.zeros((16 - both.shape[0], both.shape[1]), low_type)])


def unpack_wide(packed, count):
    packed = packed.astype(jnp.float32)
    return packed[:count] + packed[count : 2 * count]


def group_sum(block, wide, links):
    count = 1 << len(links)
    here = sum(side(link) << i for i, link in enumerate(links))
    total = pieces_of(block, count, here).astype(jnp.float32)
    shape = total.shape
    packed = pack_wide(wide)
    for mask in range(1, count):
        sent = pieces_of(block, count, here ^ mask).reshape(-1, shape[-1])
        come = swap(jnp.concatenate([sent, packed]), sum(((mask >> i) & 1) << link for i, link in enumerate(links)))
        total = total + come[: -packed.shape[0]].reshape(shape).astype(jnp.float32)
        wide = wide + unpack_wide(come[-packed.shape[0] :], wide.shape[0])
    return total.astype(low_type), wide


def group_join(block, links):
    found = [block]
    for mask in range(1, 1 << len(links)):
        found.append(swap(block, sum(((mask >> i) & 1) << link for i, link in enumerate(links))))
    for i, link in enumerate(links):
        turned = [found[k ^ (1 << i)] for k in range(len(found))]
        found = [jnp.where(side(link) == 0, kept, other) for kept, other in zip(found, turned)]
    return jnp.concatenate(found, axis=1)


def after(values, previous):
    return lax.optimization_barrier((values, previous))


def body(
    states,
    condition,
    mod_w,
    w_query,
    w_key,
    w_value,
    w_out,
    w_gate,
    w_up,
    w_down,
    counts,
    send_rows,
    neighbours,
    cotangent,
):
    rows, width = states.shape
    sends = send_rows.shape[2]
    ext = rows + len(halo_steps) * sends
    f32 = jnp.float32
    parcel = shaped((sends, width))
    send_list = send_rows[0]

    links = (lax.axis_size("nodes") * lax.axis_size("hid")).bit_length() - 1
    core, across, *around = range(links)

    normed, plain, modulation, *parcels = call(
        prepare_kernel,
        [shaped((rows, width)), shaped((rows, width)), shaped((4, width), f32)] + [parcel] * 4,
        (states, condition, mod_w, send_list),
        specs=[whole, scalars, whole, whole],
        flops=2**30,
        moved=2**22,
    )
    landed = [from_behind(part, everywhere, hop) for part, hop in zip(parcels, halo_steps)]
    shard = jnp.concatenate([w_gate, w_up, w_down])
    far_shard = swap(shard, 1 << across)
    core_shard = swap(shard, 1 << core)

    queries, own_keys, own_values, own_raised, top, total, mixed, packed = attend_own(
        normed, neighbours.T, w_query, w_key, w_value, ext - rows
    )
    attended, far_raised, spread_own, spread_far, far_keys, far_values, plain_far, normed_far = attend_far(
        modulation, queries, w_key, w_value, packed, top, total, mixed, landed
    )
    far_shard, attended = after(far_shard, attended)
    cross_shard = swap(far_shard, 1 << core)

    low_rows = shaped((rows, width))
    wide_rows = shaped((rows, width), f32)
    shard_rows = shard.shape[0]
    half_grad = shaped((shard_rows // 2, width))
    joint_grad = shaped((shard_rows // 2 + width // 2, width))

    def room(*shapes):
        return [pltpu.VMEM(one.shape, one.dtype) for one in shapes]

    middle, second, branch, out, grad, core_one, core_two, own_one, own_two = call(
        feed_first_kernel,
        [wide_rows, low_rows, low_rows, wide_rows, wide_rows] + [half_grad] * 4,
        (counts, modulation, states, cotangent, attended, w_out, core_shard, shard),
        specs=[scalars, whole] + [anywhere] * 6,
        out_specs=[anywhere] * 9,
        scratch=room(wide_rows, wide_rows, low_rows, w_out, shard, shard, low_rows, low_rows, wide_rows, wide_rows)
        + room(*[half_grad] * 4, *[low_rows] * 3)
        + [pltpu.SemaphoreType.DMA((3 + 3 * rows // ROW_BLOCK,)), pltpu.SemaphoreType.DMA((4 + 5 * rows // ROW_BLOCK,))],
        flops=2**34,
        moved=2**24,
    )
    core_index = lax.axis_index("hid")[None] & 1
    output, grad_middle, grad_own, grad_far, mod_two, cross_one, cross_two, far_one, far_two = call(
        feed_last_kernel,
        [wide_rows, wide_rows, low_rows, low_rows, shaped((2, width), f32)] + [half_grad, joint_grad] * 2,
        (counts, core_index, modulation, cotangent, attended, w_out, spread_own, spread_far)
        + (middle, second, branch, out, grad, cross_shard, far_shard),
        specs=[scalars, scalars, whole] + [anywhere] * 12,
        out_specs=[anywhere] * 4 + [whole] + [anywhere] * 4,
        scratch=room(wide_rows, low_rows, w_out, wide_rows, wide_rows, wide_rows, low_rows, low_rows)
        + room(wide_rows, wide_rows, shard, shard, low_rows, low_rows, half_grad, joint_grad, half_grad, joint_grad)
        + room(w_out, *[low_rows] * 3)
        + [pltpu.SemaphoreType.DMA((12,)), pltpu.SemaphoreType.DMA((4 + 4 * rows // ROW_BLOCK,))],
        flops=2**34,
        moved=2**24,
    )

    fold = (-1, width // 2, width)

    def over_cores(kept, sent):
        return (kept + swap(sent, 1 << core)).reshape(fold)

    one_own, two_own = over_cores(own_one, core_one), over_cores(own_two, core_two)
    one_far, two_far = over_cores(far_one, cross_one), over_cores(far_two, cross_two)
    kept = one_own.shape[0]
    first, second_link, *rest = around

    own = (own_keys, own_values, grad_own, own_raised)
    far = (far_keys, far_values, grad_far, far_raised)
    parts = 2
    heads = HEADS // parts
    pieces = [attend_back(0, heads, queries, attended, own, far)]
    own, (one_own, one_far, two_own, two_far) = after(own, (one_own, one_far, two_own, two_far))
    one = one_own + swap(one_far, 1 << across)
    here = side(second_link)
    come = swap(
        jnp.concatenate([pieces_of(two_own, 2, 1 - here), pieces_of(two_far, 2, 1 - here)]), 1 << second_link
    )
    two_own = pieces_of(two_own, 2, here) + come[:kept]
    two_far = pieces_of(two_far, 2, here) + come[kept:]
    pieces.append(attend_back(heads, heads, queries, attended, own, far))
    far_pieces = [piece for found in pieces for piece in found[3:]]
    *parcels, mod_far = call(
        functools.partial(return_kernel, parts),
        [parcel] * 4 + [shaped((2, width), f32)],
        (w_key, w_value, plain_far, *far_pieces),
        flops=2**30,
        moved=2**22,
    )
    returned = [from_behind(part, everywhere, -hop) for part, hop in zip(parcels, halo_steps)]
    (one, two_own, two_far), pieces = after((one, two_own, two_far), pieces)
    attn_grad, grad_normed, mod_grad = call(
        functools.partial(project_back_kernel, parts),
        [shaped((3, width, width)), wide_rows, shaped((4, width), f32)],
        (normed, plain, normed_far, mod_far, mod_two, w_query, w_key, w_value)
        + tuple(piece for found in pieces for piece in found),
        flops=2**33,
        moved=2**23,
    )

    one = half_sum(one, first)
    come = swap(two_far, 1 << across)
    two = jnp.concatenate([two_own + come[:kept], two_far[kept:] + come[kept:]])
    one = half_sum(one, second_link)
    two = half_sum(two, first)
    both = jnp.concatenate([one, two])
    for link in rest:
        both = half_sum(both, link)
    for link in reversed(rest):
        both = half_join(both, link)
    one, two = half_join(both[:kept], second_link), half_join(both[kept:], first)
    one, two = half_join(one, first), half_join(two, second_link)
    shard_grad = jnp.concatenate([one, two[:kept]]).reshape(-1, width).astype(f32)
    grad_w_gate, grad_w_up, grad_w_down = jnp.split(shard_grad, 3)

    groups = [[across, first]] + [around[i : i + 2] for i in range(1, len(around), 2)]
    attn_grad, mod_grad = group_sum(attn_grad, mod_grad, [core])
    for group in groups:
        attn_grad, mod_grad = group_sum(attn_grad, mod_grad, group)
    for group in reversed(groups):
        attn_grad = group_join(attn_grad, group)
    attn_grad = half_join(attn_grad, core).astype(f32)
    grad_w_query, grad_w_key, grad_w_value = attn_grad
    grad_w_out = half_join(two[kept:], core)[0].astype(f32)

    grad_states = finish(states, grad_normed, grad_middle, modulation, send_list, returned)
    mod_grad = mod_grad.reshape(-1)
    grad_mod_w = condition[:, None] * mod_grad[None, :]
    grad_condition = jnp.sum(mod_w.astype(f32) * mod_grad[None, :], axis=1)
    return (
        output,
        grad_states,
        grad_condition,
        grad_mod_w,
        grad_w_query,
        grad_w_key,
        grad_w_value,
        grad_w_out,
        grad_w_gate,
        grad_w_up,
        grad_w_down,
    )


def solution(mesh):
    rows = P(everywhere, None)
    placed = (
        rows,
        P(),
        P(),
        P(),
        P(),
        P(),
        P(),
        P(None, "hid"),
        P(None, "hid"),
        P("hid", None),
        P(everywhere),
        P(everywhere, None, None),
        rows,
        rows,
    )
    return jax.shard_map(
        body,
        mesh=mesh,
        in_specs=placed,
        out_specs=(rows, rows, P(), P(), P(), P(), P(), P(), P(None, "hid"), P(None, "hid"), P("hid", None)),
        check_vma=False,
    )
```

```python
import functools

import jax
import jax.numpy as jnp
from jax import lax
from jax.experimental import pallas as pl
from jax.experimental.pallas import tpu as pltpu
from jax.sharding import PartitionSpec as P

HEADS = 4
HEAD_DIM = 128
NEIGH = 16
BLOCK = 1024
ROW_BLOCK = 256
BACK_GRANT = 56

epsilon = 1e-06
halo_steps = (1, -1, 2, -2)
highest = lax.Precision.HIGHEST
score_scale = HEAD_DIM ** (-0.5)
low_type = jnp.bfloat16
everywhere = ("nodes", "hid")
whole = pl.BlockSpec(memory_space=pltpu.VMEM)
scalars = pl.BlockSpec(memory_space=pltpu.SMEM)
anywhere = pl.BlockSpec(memory_space=pl.ANY)


def dot(left, right, left_dim, right_dim):
    return lax.dot_general(
        left, right, (((left_dim,), (right_dim,)), ((), ())), preferred_element_type=jnp.float32
    )


def shaped(shape, dtype=low_type):
    return jax.ShapeDtypeStruct(shape, dtype)


def norm_parts(states):
    centred = states - jnp.mean(states, axis=-1, keepdims=True)
    inverse = lax.rsqrt(jnp.mean(centred * centred, axis=-1, keepdims=True) + epsilon)
    return (centred * inverse, inverse)


def norm_back(grad_plain, plain, inverse):
    first_mean = jnp.mean(grad_plain, axis=-1, keepdims=True)
    second_mean = jnp.mean(grad_plain * plain, axis=-1, keepdims=True)
    return inverse * (grad_plain - first_mean - plain * second_mean)


def call(kernel, out_shape, args, specs=None, out_specs=None, scratch=(), flops=0, moved=0, grant=60):
    single = not isinstance(out_shape, list)
    return pl.pallas_call(
        kernel,
        in_specs=specs or [whole] * len(args),
        out_specs=out_specs or (whole if single else [whole] * len(out_shape)),
        out_shape=out_shape,
        scratch_shapes=list(scratch),
        compiler_params=pltpu.CompilerParams(vmem_limit_bytes=grant * 2**20),
        cost_estimate=pl.CostEstimate(flops=flops, bytes_accessed=moved, transcendentals=0),
    )(*args)


def chosen_rows(send_ref, position, rows, first=0):
    sends = send_ref.shape[1]
    place = lax.broadcasted_iota(jnp.int32, (rows, sends), 0) + first
    return jnp.where(place == send_ref[position : position + 1, :], 1.0, 0.0).astype(low_type)


def prepare_kernel(states_ref, condition_ref, mod_w_ref, send_ref, normed_ref, plain_ref, modulation_ref, *parcel_refs):
    width = states_ref.shape[1]
    mixed = sum(
        condition_ref[i] * mod_w_ref[i : i + 1, :].astype(jnp.float32) for i in range(condition_ref.shape[0])
    )
    for piece in range(4):
        modulation_ref[piece : piece + 1, :] = mixed[:, piece * width : (piece + 1) * width]

    @pl.loop(0, states_ref.shape[0] // ROW_BLOCK)
    def _(step):
        rows = pl.ds(pl.multiple_of(step * ROW_BLOCK, ROW_BLOCK), ROW_BLOCK)
        plain, _ = norm_parts(states_ref[rows, :])
        plain_ref[rows, :] = plain.astype(low_type)
        normed_ref[rows, :] = (plain * (1.0 + modulation_ref[0:1, :]) + modulation_ref[1:2, :]).astype(low_type)

    for position, parcel_ref in enumerate(parcel_refs):
        chosen = chosen_rows(send_ref, position, states_ref.shape[0])
        parcel_ref[...] = dot(chosen, plain_ref[...], 0, 0).astype(low_type)


def count_near(near_ref, cols, groups):
    half = groups // 2
    near = near_ref[:, cols]
    group = near >> 7
    upper = group >= half
    unit = jnp.left_shift(1, 5 * jnp.where(upper, group - half, group))
    low = near & 127
    low_unit = jnp.where(upper, 0, unit)
    high_unit = jnp.where(upper, unit, 0)
    place = lax.broadcasted_iota(jnp.int32, (128, 128), 0)
    low_count = jnp.zeros((128, 128), jnp.int32)
    high_count = low_count
    for n in range(NEIGH):
        same = low[n : n + 1] == place
        low_count = low_count + jnp.where(same, low_unit[n : n + 1], 0)
        high_count = high_count + jnp.where(same, high_unit[n : n + 1], 0)
    return low_count, high_count


def count_bias(packed, position):
    count = (packed >> (5 * position)) & 31
    return jnp.where(count > 0, jnp.log(count.astype(jnp.float32)), -1e30)


def score_pass(key_ref, query, bias, scores, cols, top):
    width = scores.shape[1]
    for g in range(scores.shape[0] // 128):
        part = slice(g * 128, (g + 1) * 128)
        score = dot(key_ref[part, :], query, 1, 1) * score_scale + bias[part, cols]
        scores[part, :] = score
        top = jnp.maximum(top, jnp.max(score.reshape(16, 8, width), axis=0))
    return jnp.max(top, axis=0, keepdims=True)


def raise_pass(scores, top, raised_ref, cols):
    width = scores.shape[1]
    total = jnp.zeros((8, width), jnp.float32)
    for g in range(scores.shape[0] // 128):
        part = slice(g * 128, (g + 1) * 128)
        raised = jnp.exp(scores[part, :] - top)
        total = total + jnp.sum(raised.reshape(16, 8, width), axis=0)
        raised_ref[0, part, cols] = raised.astype(low_type)
    return jnp.sum(total, axis=0, keepdims=True)


def attend_own_kernel(
    groups, normed_ref, near_ref, w_query_ref, w_key_ref, w_value_ref,
    query_ref, key_ref, value_ref, raised_ref, top_ref, total_ref, mixed_ref, packed_ref,
    bias, scores, value_t,
):
    rows = normed_ref.shape[0]
    half = groups // 2

    @pl.when(pl.program_id(0) == 0)
    def _():
        @pl.loop(0, rows // 128)
        def _(step):
            cols = pl.ds(pl.multiple_of(step * 128, 128), 128)
            packed = count_near(near_ref, cols, groups)
            packed_ref[:, cols] = packed[1]
            for g in range(rows // 128):
                bias[g * 128 : (g + 1) * 128, cols] = count_bias(packed[g // half], g % half)

    for weight_ref, out_ref in ((w_query_ref, query_ref), (w_key_ref, key_ref), (w_value_ref, value_ref)):
        out_ref[...] = dot(normed_ref[...], weight_ref[...], 1, 0).astype(low_type)
    value_t[...] = value_ref[...].T
    width = scores.shape[1]

    @pl.loop(0, rows // width)
    def _(step):
        cols = pl.ds(pl.multiple_of(step * width, width), width)
        least = jnp.full((8, width), -jnp.inf, jnp.float32)
        top = score_pass(key_ref, query_ref[cols, :], bias, scores, cols, least)
        top_ref[0, :, cols] = top
        total_ref[0, :, cols] = raise_pass(scores, top, raised_ref, cols)
        mixed_ref[0, :, cols] = dot(value_t[...], raised_ref[0, :, cols], 1, 0)


def attend_own(normed, near, w_query, w_key, w_value, far_rows):
    rows, width = normed.shape
    groups = (rows + far_rows) // 128
    by_row = pl.BlockSpec((rows, HEAD_DIM), lambda h: (0, h))
    by_weight = pl.BlockSpec((width, HEAD_DIM), lambda h: (0, h))
    by_head = pl.BlockSpec((1, 1, rows), lambda h: (h, 0, 0))
    return pl.pallas_call(
        functools.partial(attend_own_kernel, groups),
        grid=(HEADS,),
        in_specs=[pl.BlockSpec((rows, width), lambda h: (0, 0)), pl.BlockSpec((NEIGH, rows), lambda h: (0, 0))]
        + [by_weight] * 3,
        out_specs=[
            by_row,
            by_row,
            by_row,
            pl.BlockSpec((1, rows, rows), lambda h: (h, 0, 0)),
            by_head,
            by_head,
            pl.BlockSpec((1, HEAD_DIM, rows), lambda h: (h, 0, 0)),
            pl.BlockSpec((128, rows), lambda h: (0, 0)),
        ],
        out_shape=[shaped((rows, width))] * 3
        + [
            shaped((HEADS, rows, rows)),
            shaped((HEADS, 1, rows), jnp.float32),
            shaped((HEADS, 1, rows), jnp.float32),
            shaped((HEADS, HEAD_DIM, rows), jnp.float32),
            shaped((128, rows), jnp.int32),
        ],
        scratch_shapes=[
            pltpu.VMEM((rows, rows), jnp.float32),
            pltpu.VMEM((rows, BLOCK), jnp.float32),
            pltpu.VMEM((HEAD_DIM, rows), low_type),
        ],
        compiler_params=pltpu.CompilerParams(vmem_limit_bytes=60 * 2**20),
        cost_estimate=pl.CostEstimate(flops=2**34, bytes_accessed=2**24, transcendentals=0),
    )(normed, near, w_query, w_key, w_value)


def fetch(parts, to_ref, sems):
    copies, lower = [], 0
    for position, part in enumerate(parts):
        upper = lower + part.shape[0]
        copies.append(pltpu.make_async_copy(part, to_ref.at[lower:upper, :], sems.at[position]))
        copies[-1].start()
        lower = upper
    return copies


def attend_far_kernel(
    skip, modulation_ref, query_ref, w_key_ref, w_value_ref, packed_ref, top_ref, total_ref, mixed_ref, *refs
):
    landed_refs, refs = refs[:4], refs[4:]
    attended_ref, raised_ref, spread_own_ref, spread_far_ref, key_ref, value_ref, plain_ref, normed_ref, *refs = refs
    bias, scores, value_t, sems = refs
    far, rows = bias.shape

    @pl.when(pl.program_id(0) == 0)
    def _():
        copies = fetch(landed_refs, plain_ref, sems)

        @pl.loop(0, rows // 128)
        def _(step):
            cols = pl.ds(pl.multiple_of(step * 128, 128), 128)
            for g in range(far // 128):
                bias[g * 128 : (g + 1) * 128, cols] = count_bias(packed_ref[:, cols], g + skip)

        for copy in copies:
            copy.wait()
        plain = plain_ref[...].astype(jnp.float32)
        normed_ref[...] = (plain * (1.0 + modulation_ref[0:1, :]) + modulation_ref[1:2, :]).astype(low_type)

    key_ref[...] = dot(normed_ref[...], w_key_ref[...], 1, 0).astype(low_type)
    value_ref[...] = dot(normed_ref[...], w_value_ref[...], 1, 0).astype(low_type)
    value_t[...] = value_ref[...].T
    width = scores.shape[1]

    @pl.loop(0, rows // width)
    def _(step):
        cols = pl.ds(pl.multiple_of(step * width, width), width)
        own_top = top_ref[0, :, cols]
        least = jnp.broadcast_to(own_top, (8, width))
        top = score_pass(key_ref, query_ref[cols, :], bias, scores, cols, least)
        factor = jnp.exp(own_top - top)
        total = raise_pass(scores, top, raised_ref, cols) + total_ref[0, :, cols] * factor
        inverse = 1.0 / total
        own_inverse = inverse * factor
        spread_far_ref[cols, :] = jnp.broadcast_to(inverse, (HEAD_DIM, width)).T
        spread_own_ref[cols, :] = jnp.broadcast_to(own_inverse, (HEAD_DIM, width)).T
        mixed = dot(value_t[...], raised_ref[0, :, cols], 1, 0) * inverse + mixed_ref[0, :, cols] * own_inverse
        attended_ref[cols, :] = mixed.T.astype(low_type)


def attend_far(modulation, queries, w_key, w_value, packed, top, total, mixed, landed):
    rows, width = queries.shape
    far = sum(part.shape[0] for part in landed)
    by_row = pl.BlockSpec((rows, HEAD_DIM), lambda h: (0, h))
    by_far = pl.BlockSpec((far, HEAD_DIM), lambda h: (0, h))
    by_weight = pl.BlockSpec((width, HEAD_DIM), lambda h: (0, h))
    by_head = pl.BlockSpec((1, 1, rows), lambda h: (h, 0, 0))
    groups = (rows + far) // 128
    return pl.pallas_call(
        functools.partial(attend_far_kernel, rows // 128 - groups // 2),
        grid=(HEADS,),
        in_specs=[
            pl.BlockSpec(modulation.shape, lambda h: (0, 0)),
            by_row,
            by_weight,
            by_weight,
            pl.BlockSpec(packed.shape, lambda h: (0, 0)),
            by_head,
            by_head,
            pl.BlockSpec((1, HEAD_DIM, rows), lambda h: (h, 0, 0)),
        ]
        + [anywhere] * len(landed),
        out_specs=[by_row, pl.BlockSpec((1, far, rows), lambda h: (h, 0, 0)), by_row, by_row, by_far, by_far]
        + [pl.BlockSpec((far, width), lambda h: (0, 0))] * 2,
        out_shape=[
            shaped((rows, width)),
            shaped((HEADS, far, rows)),
            shaped((rows, width), jnp.float32),
            shaped((rows, width), jnp.float32),
            shaped((far, width)),
            shaped((far, width)),
            shaped((far, width)),
            shaped((far, width)),
        ],
        scratch_shapes=[
            pltpu.VMEM((far, rows), jnp.float32),
            pltpu.VMEM((far, BLOCK), jnp.float32),
            pltpu.VMEM((HEAD_DIM, far), low_type),
            pltpu.SemaphoreType.DMA((len(landed),)),
        ],
        compiler_params=pltpu.CompilerParams(vmem_limit_bytes=60 * 2**20),
        cost_estimate=pl.CostEstimate(flops=2**33, bytes_accessed=2**23, transcendentals=0),
    )(modulation, queries, w_key, w_value, packed, top, total, mixed, *landed)


def attend_back_kernel(has_partial, query_ref, attended_ref, key_ref, value_ref, grad_ref, raised_ref, *refs):
    if has_partial:
        partial_ref, *refs = refs
    else:
        w_key_ref, w_value_ref, plain_ref, *refs = refs
    grad_query_ref, grad_key_ref, grad_value_ref, *refs = refs
    if not has_partial:
        *parcel_refs, mod_grad_ref, low, key_t, grad_normed = refs
    else:
        low, key_t = refs
    rows = query_ref.shape[0]
    key_t[...] = key_ref[...].T

    @pl.loop(0, rows // BLOCK)
    def _(step):
        cols = pl.ds(pl.multiple_of(step * BLOCK, BLOCK), BLOCK)
        attended = attended_ref[cols, :].astype(jnp.float32)
        grad = grad_ref[cols, :]
        mean = jnp.sum((grad.astype(jnp.float32) * attended).T, axis=0, keepdims=True)
        for g in range(value_ref.shape[0] // 128):
            part = slice(g * 128, (g + 1) * 128)
            term = dot(value_ref[part, :], grad, 1, 1) - mean
            low[part, cols] = (term * raised_ref[0, part, cols].astype(jnp.float32)).astype(low_type)
        total = dot(key_t[...], low[:, cols], 1, 0)
        if has_partial:
            total = (total + partial_ref[0, :, cols]) * score_scale
            grad_query_ref[cols, :] = total.T.astype(low_type)
        else:
            grad_query_ref[0, :, cols] = total

    grad_value_ref[...] = dot(raised_ref[0], grad_ref[...], 1, 0).astype(low_type)
    grad_key_ref[...] = (dot(low[...], query_ref[...], 1, 0) * score_scale).astype(low_type)
    if has_partial:
        return

    back = dot(grad_key_ref[...], w_key_ref[...], 1, 1) + dot(grad_value_ref[...], w_value_ref[...], 1, 1)

    @pl.when(pl.program_id(0) == 0)
    def _():
        grad_normed[...] = back

    @pl.when(pl.program_id(0) > 0)
    def _():
        grad_normed[...] += back

    @pl.when(pl.program_id(0) == HEADS - 1)
    def _():
        grad = grad_normed[...]
        mod_grad_ref[0:1, :] = jnp.sum(grad * plain_ref[...].astype(jnp.float32), axis=0, keepdims=True)
        mod_grad_ref[1:2, :] = jnp.sum(grad, axis=0, keepdims=True)
        for position, parcel_ref in enumerate(parcel_refs):
            sends = parcel_ref.shape[0]
            parcel_ref[...] = grad[position * sends : (position + 1) * sends, :].astype(low_type)


def attend_back(queries, attended, keys, values, grads, raised, partial=None, returns=None):
    rows, width = queries.shape
    count = keys.shape[0]
    by_row = pl.BlockSpec((rows, HEAD_DIM), lambda h: (0, h))
    by_count = pl.BlockSpec((count, HEAD_DIM), lambda h: (0, h))
    by_head = pl.BlockSpec((1, HEAD_DIM, rows), lambda h: (h, 0, 0))
    in_specs = [by_row, by_row, by_count, by_count, by_row, pl.BlockSpec((1, count, rows), lambda h: (h, 0, 0))]
    out_specs = [by_row if returns is None else by_head, by_count, by_count]
    out_shape = [
        shaped((rows, width)) if returns is None else shaped((HEADS, HEAD_DIM, rows), jnp.float32),
        shaped((count, width)),
        shaped((count, width)),
    ]
    scratch = [pltpu.VMEM((count, rows), low_type), pltpu.VMEM((HEAD_DIM, count), low_type)]
    if returns is None:
        in_specs.append(by_head)
    else:
        by_weight = pl.BlockSpec((width, HEAD_DIM), lambda h: (0, h))
        in_specs += [by_weight, by_weight, pl.BlockSpec((count, width), lambda h: (0, 0))]
        sends = count // len(halo_steps)
        out_specs += [pl.BlockSpec((sends, width), lambda h: (0, 0))] * len(halo_steps)
        out_shape += [shaped((sends, width))] * len(halo_steps)
        out_specs.append(pl.BlockSpec((2, width), lambda h: (0, 0)))
        out_shape.append(shaped((2, width), jnp.float32))
        scratch.append(pltpu.VMEM((count, width), jnp.float32))
    return pl.pallas_call(
        functools.partial(attend_back_kernel, returns is None),
        grid=(HEADS,),
        in_specs=in_specs,
        out_specs=out_specs,
        out_shape=out_shape,
        scratch_shapes=scratch,
        compiler_params=pltpu.CompilerParams(vmem_limit_bytes=BACK_GRANT * 2**20),
        cost_estimate=pl.CostEstimate(flops=count * 2**22, bytes_accessed=2**22, transcendentals=0),
    )(queries, attended, keys, values, grads, raised, *([partial] if returns is None else returns))


def live_rows(count_ref, start, rows):
    place = lax.broadcasted_iota(jnp.int32, (rows, 1), 0) + start
    return (place < count_ref[0]).astype(jnp.float32)


class Mover:
    def __init__(self, sems):
        self.sems, self.used, self.open = sems, 0, []

    def start(self, source, target):
        copy = pltpu.make_async_copy(source, target, self.sems.at[self.used])
        self.used += 1
        copy.start()
        return copy

    def send(self, source, target):
        self.open.append(self.start(source, target))

    def finish(self):
        for copy in self.open:
            copy.wait()


def feed_chunk(weight_ref, second_ref, branch_ref, out_ref, grad_ref, hidden, grad_gate, grad_up, store, fresh, done, ready=None):
    units = weight_ref.shape[0] // 3
    gate_rows, up_rows, down_rows = (slice(i * units, (i + 1) * units) for i in range(3))
    for step in range(second_ref.shape[0] // ROW_BLOCK):
        rows = slice(step * ROW_BLOCK, (step + 1) * ROW_BLOCK)
        second = second_ref[rows, :]
        gate = dot(second, weight_ref[gate_rows, :], 1, 0)
        up = dot(second, weight_ref[up_rows, :], 1, 0)
        sigmoid = 1.0 / (1.0 + jnp.exp(-gate))
        activated = gate * sigmoid
        hidden[rows, :] = (activated * up).astype(low_type)
        back = dot(branch_ref[rows, :], weight_ref[down_rows, :], 1, 1)
        grad_gate[rows, :] = (back * up * (sigmoid + activated * (1.0 - sigmoid))).astype(low_type)
        grad_up[rows, :] = (back * activated).astype(low_type)
        out = dot(hidden[rows, :], weight_ref[down_rows, :], 1, 0)
        grad = dot(grad_gate[rows, :], weight_ref[gate_rows, :], 1, 1) + dot(
            grad_up[rows, :], weight_ref[up_rows, :], 1, 1
        )
        if step == 0 and ready is not None:
            ready()
        if fresh:
            out_ref[rows, :] = out
            grad_ref[rows, :] = grad
        else:
            out_ref[rows, :] += out
            grad_ref[rows, :] += grad
        if done is not None:
            done(rows)

    one, two = store
    half = units // 2
    one[:units, :] = dot(second_ref[...], grad_gate[...], 0, 0).astype(low_type)
    grad_up_weight = dot(second_ref[...], grad_up[...], 0, 0).astype(low_type)
    one[units:, :] = grad_up_weight[:half, :]
    two[:half, :] = grad_up_weight[half:, :]
    two[half : half + units, :] = dot(hidden[...], branch_ref[...], 0, 0).astype(low_type)


def feed_first_kernel(
    count_ref, modulation_ref, states_in, cotangent_in, attended_in, w_out_in,
    core_gate_in, core_up_in, core_down_in, own_gate_in, own_up_in, own_down_in,
    middle_out, second_out, branch_out, out_out, grad_out, core_one_out, core_two_out, own_one_out, own_two_out,
    states, cotangent, attended, w_out, core, own, second, branch, out, grad,
    core_one, core_two, own_one, own_two, hidden, grad_gate, grad_up, in_sems, out_sems,
):
    come, go = Mover(in_sems), Mover(out_sems)
    w_out_copy = come.start(w_out_in, w_out)
    blocks = [slice(lower, lower + ROW_BLOCK) for lower in range(0, states.shape[0], ROW_BLOCK)]
    units = own_gate_in.shape[0]

    def start_rows(rows):
        pairs = ((attended_in, attended), (states_in, states), (cotangent_in, cotangent))
        return [come.start(source.at[rows, :], target.at[rows, :]) for source, target in pairs]

    def start_units(sources, target):
        return [come.start(source, target.at[i * units : (i + 1) * units, :]) for i, source in enumerate(sources)]

    row_copies = [start_rows(rows) for rows in blocks]
    weight_copies = [start_units((core_gate_in, core_up_in, core_down_in), core)]
    weight_copies.append(start_units((own_gate_in, own_up_in, own_down_in), own))
    w_out_copy.wait()
    for index, rows in enumerate(blocks):
        for copy in row_copies[index]:
            copy.wait()
        live = live_rows(count_ref, rows.start, ROW_BLOCK)
        middle = states[rows, :] + live * dot(attended[rows, :], w_out[...], 1, 0)
        states[rows, :] = middle
        plain, _ = norm_parts(middle)
        second[rows, :] = (plain * (1.0 + modulation_ref[2:3, :]) + modulation_ref[3:4, :]).astype(low_type)
        branch[rows, :] = (live * cotangent[rows, :]).astype(low_type)
        for source, target in ((states, middle_out), (second, second_out), (branch, branch_out)):
            go.send(source.at[rows, :], target.at[rows, :])

    def done(rows):
        go.send(out.at[rows, :], out_out.at[rows, :])
        go.send(grad.at[rows, :], grad_out.at[rows, :])

    scratch = (hidden, grad_gate, grad_up)
    for copy in weight_copies[0]:
        copy.wait()
    feed_chunk(core, second, branch, out, grad, *scratch, (core_one, core_two), True, None)
    go.send(core_one, core_one_out)
    go.send(core_two, core_two_out)
    for copy in weight_copies[1]:
        copy.wait()
    feed_chunk(own, second, branch, out, grad, *scratch, (own_one, own_two), False, done)
    go.send(own_one, own_one_out)
    go.send(own_two, own_two_out)
    go.finish()


def feed_last_kernel(
    count_ref, core_ref, modulation_ref, cotangent_in, attended_in, w_out_in, spread_own_in, spread_far_in,
    middle_in, second_in, branch_in, out_in, grad_in, cross_half_in, cross_rest_in, far_half_in, far_rest_in,
    output_out, grad_middle_out, grad_own_out, grad_far_out, mod_grad_ref,
    cross_one_out, cross_two_out, far_one_out, far_two_out,
    cotangent, attended, w_out, spread_own, spread_far, middle, second, branch, out, grad, cross, far,
    grad_own, grad_far, cross_one, cross_two, far_one, far_two, w_out_grad,
    hidden, grad_gate, grad_up, in_sems, out_sems,
):
    come, go = Mover(in_sems), Mover(out_sems)
    half = far_half_in.shape[0] // 3

    def halves(half_in, rest_in, target):
        return [
            (source.at[i * half : (i + 1) * half, :], target.at[pl.ds(pl.multiple_of((2 * i + which) * half, half), half), :])
            for source, which in ((half_in, core_ref[1]), (rest_in, 1 - core_ref[1]))
            for i in range(3)
        ]


    def start_all(pairs):
        return [come.start(source, target) for source, target in pairs]

    first_copies = start_all([(second_in, second), *halves(far_half_in, far_rest_in, far), (branch_in, branch)])
    scratch = (hidden, grad_gate, grad_up)
    for copy in first_copies:
        copy.wait()
    sum_copies = start_all([(out_in, out), (grad_in, grad)])
    late_copies = []

    def ready():
        for copy in sum_copies:
            copy.wait()
        late_copies.extend(
            start_all(
                [
                    *halves(cross_half_in, cross_rest_in, cross), (w_out_in, w_out), (middle_in, middle),
                    (cotangent_in, cotangent), (spread_own_in, spread_own), (spread_far_in, spread_far),
                    (attended_in, attended),
                ]
            )
        )

    feed_chunk(far, second, branch, out, grad, *scratch, (far_one, far_two), False, None, ready)
    go.send(far_one, far_one_out)
    for copy in late_copies:
        copy.wait()
    feed_chunk(cross, second, branch, out, grad, *scratch, (cross_one, cross_two), False, None)
    go.send(cross_one, cross_one_out)
    low_grad = hidden
    scale, bias = 0.0, 0.0
    for lower in range(0, middle.shape[0], ROW_BLOCK):
        rows = slice(lower, lower + ROW_BLOCK)
        live = live_rows(count_ref, lower, ROW_BLOCK)
        block = middle[rows, :]
        plain, inverse = norm_parts(block)
        middle[rows, :] = block + live * out[rows, :]
        go.send(middle.at[rows, :], output_out.at[rows, :])
        grad_second = grad[rows, :]
        scale += jnp.sum(grad_second * plain, axis=0, keepdims=True)
        bias += jnp.sum(grad_second, axis=0, keepdims=True)
        grad_middle = cotangent[rows, :] + norm_back(grad_second * (1.0 + modulation_ref[2:3, :]), plain, inverse)
        cotangent[rows, :] = grad_middle
        go.send(cotangent.at[rows, :], grad_middle_out.at[rows, :])
        low_grad[rows, :] = (live * grad_middle).astype(low_type)
        grad_attended = dot(low_grad[rows, :], w_out[...], 1, 1)
        grad_own[rows, :] = (grad_attended * spread_own[rows, :]).astype(low_type)
        grad_far[rows, :] = (grad_attended * spread_far[rows, :]).astype(low_type)
        go.send(grad_own.at[rows, :], grad_own_out.at[rows, :])
        go.send(grad_far.at[rows, :], grad_far_out.at[rows, :])
    mod_grad_ref[0:1, :] = scale
    mod_grad_ref[1:2, :] = bias

    half = w_out_grad.shape[0] // 2
    w_out_grad[...] = dot(attended[...], low_grad[...], 0, 0).astype(low_type)
    for two, two_out, side_of in ((far_two, far_two_out, core_ref[0]), (cross_two, cross_two_out, 1 - core_ref[0])):
        start = pl.multiple_of(side_of * half, half)
        two[two.shape[0] - half :, :] = w_out_grad[pl.ds(start, half), :]
        go.send(two, two_out)
    go.finish()


def project_back_kernel(
    core_ref, mod_far_ref, mod_two_ref, normed_in, query_in, key_in, normed_far_in, far_key_in, value_in, far_value_in,
    w_query_in, w_key_in, w_value_in, plain_in,
    kept_out, sent_out, grad_normed_out, mod_grad_ref,
    normed, query, key, normed_far, far_key, value, far_value, w_query, w_key, w_value, plain,
    weight_grad, grad_normed, packed, in_sems, out_sems,
):
    come, go = Mover(in_sems), Mover(out_sems)
    half = weight_grad.shape[1] // 2
    own_half = pl.ds(pl.multiple_of(core_ref[0] * half, half), half)
    other_half = pl.ds(pl.multiple_of((1 - core_ref[0]) * half, half), half)
    groups = (
        ((normed_in, normed), (query_in, query)),
        ((key_in, key), (normed_far_in, normed_far), (far_key_in, far_key)),
        ((value_in, value), (far_value_in, far_value)),
        ((w_query_in, w_query), (w_key_in, w_key), (w_value_in, w_value), (plain_in, plain)),
    )
    copies = [[come.start(source, target) for source, target in group] for group in groups]
    for kind, (own, far) in enumerate(((query, None), (key, far_key), (value, far_value))):
        for copy in copies[kind]:
            copy.wait()
        grad = dot(normed[...], own[...], 0, 0)
        if far is not None:
            grad += dot(normed_far[...], far[...], 0, 0)
        weight_grad[kind] = grad.astype(low_type)
        go.send(weight_grad.at[kind, own_half, :], kept_out.at[kind])
        go.send(weight_grad.at[kind, other_half, :], sent_out.at[kind * half : (kind + 1) * half, :])
    for copy in copies[3]:
        copy.wait()
    scale, bias = 0.0, 0.0
    for lower in range(0, normed.shape[0], ROW_BLOCK):
        rows = slice(lower, lower + ROW_BLOCK)
        grad = sum(dot(own[rows, :], weight[...], 1, 1) for own, weight in ((query, w_query), (key, w_key), (value, w_value)))
        grad_normed[rows, :] = grad
        go.send(grad_normed.at[rows, :], grad_normed_out.at[rows, :])
        scale += jnp.sum(grad * plain[rows, :].astype(jnp.float32), axis=0, keepdims=True)
        bias += jnp.sum(grad, axis=0, keepdims=True)
    mod_grad_ref[0:1, :] = mod_far_ref[0:1, :] + scale
    mod_grad_ref[1:2, :] = mod_far_ref[1:2, :] + bias
    mod_grad_ref[2:4, :] = mod_two_ref[...]
    mod_grad = mod_grad_ref[...]
    high = mod_grad.astype(low_type).astype(jnp.float32)
    packed[...] = jnp.concatenate([high, mod_grad - high, jnp.zeros((8, high.shape[1]), jnp.float32)]).astype(low_type)
    go.send(packed, sent_out.at[3 * half : 3 * half + 16, :])
    go.finish()


def small(work, out_shapes, scalar_args, args, grant=16):
    def kernel(scalar_ref, *refs):
        for out_ref, value in zip(refs[len(args) :], work(scalar_ref, *refs[: len(args)])):
            out_ref[...] = value.astype(out_ref.dtype)

    return call(
        kernel, list(out_shapes), (scalar_args, *args), specs=[scalars] + [whole] * len(args), grant=grant, flops=2**29
    )


def half_of(ref, which):
    half = ref.shape[1] // 2
    return ref[:, pl.ds(pl.multiple_of(which * half, half), half), :].astype(jnp.float32)


def halves_of(side_of, *refs):
    return sum(half_of(ref, 1 - side_of) for ref in refs), sum(half_of(ref, side_of) for ref in refs)


def finish_kernel(states_ref, grad_normed_ref, grad_middle_ref, modulation_ref, send_ref, *refs):
    returned_refs, (grad_states_ref, returned, sems) = refs[:4], refs[4:]

    @pl.when(pl.program_id(0) == 0)
    def _():
        for copy in fetch(returned_refs, returned, sems):
            copy.wait()

    rows = states_ref.shape[0]
    sends = send_ref.shape[1]
    grad = grad_normed_ref[...]
    for position in range(len(returned_refs)):
        chosen = chosen_rows(send_ref, position, rows, pl.program_id(0) * rows)
        grad += dot(chosen, returned[position * sends : (position + 1) * sends, :], 1, 0)
    plain, inverse = norm_parts(states_ref[...])
    grad_states_ref[...] = grad_middle_ref[...] + norm_back(grad * (1.0 + modulation_ref[0:1, :]), plain, inverse)


def finish(states, grad_normed, grad_middle, modulation, send_list, returned):
    rows, width = states.shape
    by_block = pl.BlockSpec((ROW_BLOCK, width), lambda i: (i, 0))
    return pl.pallas_call(
        finish_kernel,
        grid=(rows // ROW_BLOCK,),
        in_specs=[by_block] * 3
        + [pl.BlockSpec(modulation.shape, lambda i: (0, 0)), pl.BlockSpec(send_list.shape, lambda i: (0, 0))]
        + [anywhere] * len(returned),
        out_specs=by_block,
        out_shape=shaped((rows, width), jnp.float32),
        scratch_shapes=[
            pltpu.VMEM((sum(part.shape[0] for part in returned), width), low_type),
            pltpu.SemaphoreType.DMA((len(returned),)),
        ],
        compiler_params=pltpu.CompilerParams(vmem_limit_bytes=24 * 2**20),
        cost_estimate=pl.CostEstimate(flops=2**31, bytes_accessed=2**23, transcendentals=0),
    )(states, grad_normed, grad_middle, modulation, send_list, *returned)


def from_behind(block, axis, distance):
    devices = range(lax.axis_size(axis))
    route = [((i - distance) % len(devices), i) for i in devices]
    return lax.ppermute(block, axis, route)


def swap(block, mask):
    count = lax.axis_size("nodes") * lax.axis_size("hid")
    return lax.ppermute(block, everywhere, [(i, i ^ mask) for i in range(count)])


def place():
    return lax.axis_index("nodes") * lax.axis_size("hid") + lax.axis_index("hid")


def side(link):
    return (place() >> link) & 1


def added(parts):
    return sum(part.astype(jnp.float32) for part in parts).astype(low_type)


def pieces_of(block, count, index):
    size = block.shape[1] // count
    return lax.dynamic_slice_in_dim(block, index * size, size, 1)


def half_sum(block, link):
    return pieces_of(block, 2, side(link)) + swap(pieces_of(block, 2, 1 - side(link)), 1 << link)


def half_join(block, link):
    other = swap(block, 1 << link)
    return jnp.where(
        side(link) == 0, jnp.concatenate([block, other], axis=1), jnp.concatenate([other, block], axis=1)
    )


def pack_wide(values):
    high = lax.reduce_precision(values, 8, 7)
    both = jnp.concatenate([high, values - high]).astype(low_type)
    return jnp.concatenate([both, jnp.zeros((16 - both.shape[0], both.shape[1]), low_type)])


def unpack_wide(packed, count):
    packed = packed.astype(jnp.float32)
    return packed[:count] + packed[count : 2 * count]


def group_sum(block, wide, links):
    count = 1 << len(links)
    here = sum(side(link) << i for i, link in enumerate(links))
    total = pieces_of(block, count, here).astype(jnp.float32)
    shape = total.shape
    packed = pack_wide(wide)
    for mask in range(1, count):
        sent = pieces_of(block, count, here ^ mask).reshape(-1, shape[-1])
        come = swap(jnp.concatenate([sent, packed]), sum(((mask >> i) & 1) << link for i, link in enumerate(links)))
        total = total + come[: -packed.shape[0]].reshape(shape).astype(jnp.float32)
        wide = wide + unpack_wide(come[-packed.shape[0] :], wide.shape[0])
    return total.astype(low_type), wide


def group_join(block, links):
    found = [block]
    for mask in range(1, 1 << len(links)):
        found.append(swap(block, sum(((mask >> i) & 1) << link for i, link in enumerate(links))))
    for i, link in enumerate(links):
        turned = [found[k ^ (1 << i)] for k in range(len(found))]
        found = [jnp.where(side(link) == 0, kept, other) for kept, other in zip(found, turned)]
    return jnp.concatenate(found, axis=1)


def after(values, previous):
    return lax.optimization_barrier((values, previous))


def body(
    states,
    condition,
    mod_w,
    w_query,
    w_key,
    w_value,
    w_out,
    w_gate,
    w_up,
    w_down,
    counts,
    send_rows,
    neighbours,
    cotangent,
):
    rows, width = states.shape
    sends = send_rows.shape[2]
    ext = rows + len(halo_steps) * sends
    f32 = jnp.float32
    parcel = shaped((sends, width))
    send_list = send_rows[0]

    links = (lax.axis_size("nodes") * lax.axis_size("hid")).bit_length() - 1
    core, across, *around = range(links)

    normed, plain, modulation, *parcels = call(
        prepare_kernel,
        [shaped((rows, width)), shaped((rows, width)), shaped((4, width), f32)] + [parcel] * 4,
        (states, condition, mod_w, send_list),
        specs=[whole, scalars, whole, whole],
        flops=2**30,
        moved=2**22,
    )
    landed = [from_behind(part, everywhere, hop) for part, hop in zip(parcels, halo_steps)]
    normed, plain, modulation, *parcels = call(
        prepare_kernel,
        [shaped((rows, width)), shaped((rows, width)), shaped((4, width), f32)] + [parcel] * 4,
        (states, condition, mod_w, send_list),
        specs=[whole, scalars, whole, whole],
        flops=2**30,
        moved=2**22,
    )
    landed = [from_behind(part, everywhere, hop) for part, hop in zip(parcels, halo_steps)]
    shard, normed = after((w_gate, w_up, w_down), normed)
    near_half = side(around[0])
    far_half = jnp.concatenate([pieces_of(weight[None], 2, near_half)[0] for weight in shard])
    far_half = swap(far_half, 1 << across)

    queries, own_keys, own_values, own_raised, top, total, mixed, packed = attend_own(
        normed, neighbours.T, w_query, w_key, w_value, ext - rows
    )
    queries, far_half, landed, shard = lax.optimization_barrier((queries, far_half, landed, shard))
    core_shard = [swap(weight, 1 << core) for weight in shard]
    far_rest = swap(far_half, 1 << around[0])
    cross_half = swap(far_half, 1 << core)
    attended, far_raised, spread_own, spread_far, far_keys, far_values, plain_far, normed_far = attend_far(
        modulation, queries, w_key, w_value, packed, top, total, mixed, landed
    )

    low_rows = shaped((rows, width))
    wide_rows = shaped((rows, width), f32)
    shard_rows = sum(weight.size for weight in shard) // width
    all_units = shaped((shard_rows, width))
    half_grad = shaped((shard_rows // 2, width))
    joint_grad = shaped((shard_rows // 2 + width // 2, width))

    def room(*shapes):
        return [pltpu.VMEM(one.shape, one.dtype) for one in shapes]

    middle, second, branch, out, grad, core_one, core_two, own_one, own_two = call(
        feed_first_kernel,
        [wide_rows, low_rows, low_rows, wide_rows, wide_rows] + [half_grad] * 4,
        (counts, modulation, states, cotangent, attended, w_out, *core_shard, *shard),
        specs=[scalars, whole] + [anywhere] * 10,
        out_specs=[anywhere] * 9,
        scratch=room(wide_rows, wide_rows, low_rows, w_out, all_units, all_units, low_rows, low_rows)
        + room(wide_rows, wide_rows)
        + room(*[half_grad] * 4, *[low_rows] * 3)
        + [pltpu.SemaphoreType.DMA((7 + 3 * rows // ROW_BLOCK,)), pltpu.SemaphoreType.DMA((4 + 5 * rows // ROW_BLOCK,))],
        flops=2**34,
        moved=2**24,
    )
    core_index = jnp.stack([lax.axis_index("hid") & 1, near_half])
    (cross_half, far_rest), grad = after((cross_half, far_rest), grad)
    cross_rest = swap(far_rest, 1 << core)
    fold = (-1, width // 2, width)

    def over_cores(*grads):
        return [[kept.reshape(fold), swap(sent, 1 << core).reshape(fold)] for kept, sent in grads]

    first, second_link, *rest = around
    sides = jnp.stack([side(first), side(second_link)])

    def lines(blocks, count):
        return shaped((blocks, count, width))

    def first_halves(side_ref, one, one_come, two, two_come):
        return *halves_of(side_ref[0], one, one_come), *halves_of(side_ref[1], two, two_come)

    own_sums = over_cores((own_one, core_one), (own_two, core_two))
    kept = own_sums[0][0].shape[0]
    eighth = fold[1] // 2
    quarter = eighth // 2
    one_sent, one_own, two_sent, two_own = small(
        first_halves, [lines(kept, eighth)] * 4, sides, (*own_sums[0], *own_sums[1])
    )
    (one_sent, two_sent), cross_rest = after((one_sent, two_sent), cross_rest)
    own_come = swap(one_sent, 1 << first), swap(two_sent, 1 << second_link)
    output, grad_middle, grad_own, grad_far, mod_two, cross_one, cross_two, far_one, far_two = call(
        feed_last_kernel,
        [wide_rows, wide_rows, low_rows, low_rows, shaped((2, width), f32)] + [half_grad, joint_grad] * 2,
        (counts, core_index, modulation, cotangent, attended, w_out, spread_own, spread_far)
        + (middle, second, branch, out, grad, cross_half, cross_rest, far_half, far_rest),
        specs=[scalars, scalars, whole] + [anywhere] * 14,
        out_specs=[anywhere] * 4 + [whole] + [anywhere] * 4,
        scratch=room(wide_rows, low_rows, w_out, wide_rows, wide_rows, wide_rows, low_rows, low_rows)
        + room(wide_rows, wide_rows, all_units, all_units, low_rows, low_rows)
        + room(half_grad, joint_grad, half_grad, joint_grad)
        + room(w_out, *[low_rows] * 3)
        + [pltpu.SemaphoreType.DMA((22,)), pltpu.SemaphoreType.DMA((4 + 4 * rows // ROW_BLOCK,))],
        flops=2**34,
        moved=2**24,
    )

    (cross_one, cross_two), own_come = after((cross_one, cross_two), own_come)
    far_sums = over_cores((far_one, cross_one), (far_two, cross_two))
    one_sent, one_far, two_sent, two_far = small(
        first_halves,
        [lines(kept, eighth)] * 2 + [lines(kept + 1, eighth)] * 2,
        sides,
        (*far_sums[0], *far_sums[1]),
    )
    grad_far, (one_sent, two_sent) = after(grad_far, (one_sent, two_sent))
    far_come = swap(one_sent, 1 << first), swap(two_sent, 1 << second_link)
    partial, *far_pieces = attend_back(
        queries, attended, far_keys, far_values, grad_far, far_raised, returns=(w_key, w_value, plain_far)
    )
    *far_pieces, mod_far = far_pieces
    far_pieces, parcels = far_pieces[:2], far_pieces[2:]
    far_come, (grad_own, parcels, partial) = after(far_come, (grad_own, parcels, partial))

    def second_halves(side_ref, one_own, one_own_come, one_far, one_far_come, two_own, two_own_come, two_far, two_far_come):
        own_sent, own_kept = halves_of(side_ref[1], one_own, one_own_come)
        far_sent, far_kept = halves_of(side_ref[1], one_far, one_far_come)
        two_kept = two_own[...].astype(f32) + two_own_come[...].astype(f32)
        two_sent = two_far[...].astype(f32) + two_far_come[...].astype(f32)
        return jnp.concatenate([own_sent, far_sent]), own_kept, far_kept, two_kept, two_sent

    one_sent, one_own, one_far, two_own, two_sent = small(
        second_halves,
        [lines(2 * kept, quarter), lines(kept, quarter), lines(kept, quarter), lines(kept, eighth), lines(kept + 1, eighth)],
        sides,
        (one_own, own_come[0], one_far, far_come[0], two_own, own_come[1], two_far, far_come[1]),
    )
    (one_sent, two_sent), grad_own = after((one_sent, two_sent), grad_own)
    one_come, two_come = swap(one_sent, 1 << second_link), swap(two_sent, 1 << across)
    pieces = attend_back(queries, attended, own_keys, own_values, grad_own, own_raised, partial)
    (one_come, two_come), pieces = after((one_come, two_come), pieces)

    def third_halves(side_ref, one_own, one_far, one_come, two_own, two_last, two_come):
        one_kept = one_own[...].astype(f32) + one_come[:kept].astype(f32)
        one_sent = one_far[...].astype(f32) + one_come[kept:].astype(f32)
        here = side_ref[0]
        own_sent, own_kept = halves_of(here, two_own, two_come.at[:kept])
        last_sent, last_kept = halves_of(here, two_last.at[kept:], two_come.at[kept:])
        return one_sent, one_kept, jnp.concatenate([own_sent, last_sent]), jnp.concatenate([own_kept, last_kept])

    one_sent, one_kept, two_sent, two_kept = small(
        third_halves,
        [lines(kept, quarter)] * 2 + [lines(kept + 1, quarter)] * 2,
        sides,
        (one_own, one_far, one_come, two_own, two_sent, two_come),
    )
    (one_sent, two_sent), pieces = after((one_sent, two_sent), pieces)
    one_come, two_come = swap(one_sent, 1 << across), swap(two_sent, 1 << first)
    returned = [from_behind(part, everywhere, -hop) for part, hop in zip(parcels[:3], halo_steps)]
    far_low = shaped((ext - rows, width))
    attn_kept, attn_sent, grad_normed, mod_grad = call(
        project_back_kernel,
        [shaped((3, width // 2, width)), shaped((3 * width // 2 + 16, width)), wide_rows, shaped((4, width), f32)],
        (core_index, mod_far, mod_two, normed, pieces[0], pieces[1], normed_far, far_pieces[0], pieces[2], far_pieces[1])
        + (w_query, w_key, w_value, plain),
        specs=[scalars, whole, whole] + [anywhere] * 11,
        out_specs=[anywhere, anywhere, anywhere, whole],
        scratch=room(low_rows, low_rows, low_rows, far_low, far_low, low_rows, far_low, w_query, w_key, w_value, low_rows)
        + room(shaped((3, width, width)), wide_rows, shaped((16, width)))
        + [pltpu.SemaphoreType.DMA((11,)), pltpu.SemaphoreType.DMA((7 + rows // ROW_BLOCK,))],
        flops=2**32,
        moved=2**23,
    )

    def on_both(step, link):
        def run(one, two):
            both = step(jnp.concatenate([one, two]), link)
            return both[:kept], both[kept:]

        return run

    shard_steps = [on_both(half_sum, link) for link in rest]
    shard_steps += [on_both(half_join, link) for link in reversed(rest)]
    shard_steps.append(lambda one, two: (half_join(one, second_link), half_join(two, first)))
    shard_steps.append(lambda one, two: (half_join(one, first), half_join(two, second_link)))

    groups = [[across, first]] + [around[i : i + 2] for i in range(1, len(around), 2)]
    def over_attn_cores(kept, wide):
        come = swap(attn_sent, 1 << core)
        total = kept.astype(f32) + come[:-16].reshape(kept.shape).astype(f32)
        return total.astype(low_type), wide + unpack_wide(come[-16:], wide.shape[0])

    attn_steps = [over_attn_cores] + [functools.partial(group_sum, links=group) for group in groups]
    attn_steps += [lambda grad, wide, group=group: (group_join(grad, group), wide) for group in reversed(groups)]

    returned, (one_come, two_come), parcels, attn_sent = lax.optimization_barrier(
        (returned, (one_come, two_come), parcels, attn_sent)
    )
    returned.append(from_behind(parcels[3], everywhere, -halo_steps[3]))
    shard_state = added([one_kept, one_come]), added([two_kept, two_come])
    attn_state = attn_kept, mod_grad
    for index in range(max(len(shard_steps), len(attn_steps))):
        if index < len(shard_steps):
            shard_state = shard_steps[index](*shard_state)
        if index < len(attn_steps):
            attn_state = attn_steps[index](*attn_state)
        if index == 0:
            returned, attn_state = after(returned, attn_state)
        if index == 1:
            grad_states = finish(states, grad_normed, grad_middle, modulation, send_list, returned)
            grad_states, attn_state = after(grad_states, attn_state)
        if index + 1 == len(shard_steps):
            one, two = shard_state
            shard_grad = jnp.concatenate([one, two[:kept]]).reshape(-1, width)
            shard_grad, two, attn_state = lax.optimization_barrier((shard_grad, two, attn_state))
            shard_grad = jnp.split(shard_grad.astype(f32), 3)
            shard_state = shard_grad, two
        shard_state, attn_state = after(shard_state, attn_state)
    (shard_grad, two), (attn_grad, mod_grad) = shard_state, attn_state
    grad_w_gate, grad_w_up, grad_w_down = shard_grad
    grad_w_query, grad_w_key, grad_w_value = half_join(attn_grad, core).astype(f32)
    grad_w_out = half_join(two[kept:], core)[0].astype(f32)
    mod_grad = mod_grad.reshape(-1)
    grad_mod_w = condition[:, None] * mod_grad[None, :]
    grad_condition = jnp.sum(mod_w.astype(f32) * mod_grad[None, :], axis=1)
    return (
        output,
        grad_states,
        grad_condition,
        grad_mod_w,
        grad_w_query,
        grad_w_key,
        grad_w_value,
        grad_w_out,
        grad_w_gate,
        grad_w_up,
        grad_w_down,
    )


def solution(mesh):
    rows = P(everywhere, None)
    placed = (
        rows,
        P(),
        P(),
        P(),
        P(),
        P(),
        P(),
        P(None, "hid"),
        P(None, "hid"),
        P("hid", None),
        P(everywhere),
        P(everywhere, None, None),
        rows,
        rows,
    )
    return jax.shard_map(
        body,
        mesh=mesh,
        in_specs=placed,
        out_specs=(rows, rows, P(), P(), P(), P(), P(), P(), P(None, "hid"), P(None, "hid"), P("hid", None)),
        check_vma=False,
    )
```

```python
import functools

import jax
import jax.numpy as jnp
from jax import lax
from jax.experimental import pallas as pl
from jax.experimental.pallas import tpu as pltpu
from jax.sharding import PartitionSpec as P

HEADS = 4
HEAD_DIM = 128
NEIGH = 16
BLOCK = 1024
ROW_BLOCK = 256
BACK_GRANT = 56
RAISED_PARTS = 1

epsilon = 1e-06
halo_steps = (1, -1, 2, -2)
highest = lax.Precision.HIGHEST
score_scale = HEAD_DIM ** (-0.5)
LOG2_E = 1.4426950408889634
low_type = jnp.bfloat16
everywhere = ("nodes", "hid")
whole = pl.BlockSpec(memory_space=pltpu.VMEM)
scalars = pl.BlockSpec(memory_space=pltpu.SMEM)
anywhere = pl.BlockSpec(memory_space=pl.ANY)


def dot(left, right, left_dim, right_dim):
    return lax.dot_general(
        left, right, (((left_dim,), (right_dim,)), ((), ())), preferred_element_type=jnp.float32
    )


def shaped(shape, dtype=low_type):
    return jax.ShapeDtypeStruct(shape, dtype)


def norm_parts(states):
    centred = states - jnp.mean(states, axis=-1, keepdims=True)
    inverse = lax.rsqrt(jnp.mean(centred * centred, axis=-1, keepdims=True) + epsilon)
    return (centred * inverse, inverse)


def norm_back(grad_plain, plain, inverse):
    first_mean = jnp.mean(grad_plain, axis=-1, keepdims=True)
    second_mean = jnp.mean(grad_plain * plain, axis=-1, keepdims=True)
    return inverse * (grad_plain - first_mean - plain * second_mean)


def call(kernel, out_shape, args, specs=None, out_specs=None, scratch=(), flops=0, moved=0, grant=60):
    single = not isinstance(out_shape, list)
    return pl.pallas_call(
        kernel,
        in_specs=specs or [whole] * len(args),
        out_specs=out_specs or (whole if single else [whole] * len(out_shape)),
        out_shape=out_shape,
        scratch_shapes=list(scratch),
        compiler_params=pltpu.CompilerParams(vmem_limit_bytes=grant * 2**20),
        cost_estimate=pl.CostEstimate(flops=flops, bytes_accessed=moved, transcendentals=0),
    )(*args)


def chosen_rows(send_ref, position, rows, first=0):
    sends = send_ref.shape[1]
    place = lax.broadcasted_iota(jnp.int32, (rows, sends), 0) + first
    return jnp.where(place == send_ref[position : position + 1, :], 1.0, 0.0).astype(low_type)


def prepare_kernel(
    states_ref, condition_ref, mod_w_ref, send_ref, normed_ref, plain_ref, modulation_ref, *refs
):
    *parcel_refs, plain = refs
    step, (block, width) = pl.program_id(0), states_ref.shape

    @pl.when(step == 0)
    def _():
        mixed = sum(
            condition_ref[i] * mod_w_ref[i : i + 1, :].astype(jnp.float32) for i in range(condition_ref.shape[0])
        )
        for piece in range(4):
            modulation_ref[piece : piece + 1, :] = mixed[:, piece * width : (piece + 1) * width]

    values, _ = norm_parts(states_ref[...])
    plain_ref[...] = values.astype(low_type)
    plain[pl.ds(pl.multiple_of(step * block, block), block), :] = plain_ref[...]
    normed_ref[...] = (values * (1.0 + modulation_ref[0:1, :]) + modulation_ref[1:2, :]).astype(low_type)

    @pl.when(step == pl.num_programs(0) - 1)
    def _():
        for position, parcel_ref in enumerate(parcel_refs):
            chosen = chosen_rows(send_ref, position, plain.shape[0])
            parcel_ref[...] = dot(chosen, plain[...], 0, 0).astype(low_type)


def prepare(states, condition, mod_w, send_list):
    rows, width = states.shape
    by_block = pl.BlockSpec((2 * ROW_BLOCK, width), lambda i: (i, 0))

    def once(*shape):
        return pl.BlockSpec(shape, lambda i: (0,) * len(shape))

    count, sends = send_list.shape
    return pl.pallas_call(
        prepare_kernel,
        grid=(rows // ROW_BLOCK // 2,),
        in_specs=[by_block, scalars, once(*mod_w.shape), once(*send_list.shape)],
        out_specs=[by_block, by_block, once(4, width)] + [once(sends, width)] * count,
        out_shape=[shaped((rows, width)), shaped((rows, width)), shaped((4, width), jnp.float32)]
        + [shaped((sends, width))] * count,
        scratch_shapes=[pltpu.VMEM((rows, width), low_type)],
        compiler_params=pltpu.CompilerParams(vmem_limit_bytes=60 * 2**20),
        cost_estimate=pl.CostEstimate(flops=2**30, bytes_accessed=2**22, transcendentals=0),
    )(states, condition, mod_w, send_list)


def count_near(near_ref, cols, groups):
    half = groups // 2
    near = near_ref[:, cols]
    group = near >> 7
    upper = group >= half
    unit = jnp.left_shift(1, 5 * jnp.where(upper, group - half, group))
    low = near & 127
    low_unit = jnp.where(upper, 0, unit)
    high_unit = jnp.where(upper, unit, 0)
    place = lax.broadcasted_iota(jnp.int32, (128, 128), 0)
    low_count = jnp.zeros((128, 128), jnp.int32)
    high_count = low_count
    for n in range(NEIGH):
        same = low[n : n + 1] == place
        low_count = low_count + jnp.where(same, low_unit[n : n + 1], 0)
        high_count = high_count + jnp.where(same, high_unit[n : n + 1], 0)
    return low_count, high_count


def count_bias(packed, position):
    count = (packed >> (5 * position)) & 31
    return jnp.where(count > 0, jnp.log2(count.astype(jnp.float32)), -1e30)


def score_pass(key_ref, query, bias, scores, cols, top):
    width = scores.shape[1]
    for g in range(scores.shape[0] // 128):
        part = slice(g * 128, (g + 1) * 128)
        score = dot(key_ref[part, :], query, 1, 1) * (score_scale * LOG2_E) + bias[part, cols]
        scores[part, :] = score
        top = jnp.maximum(top, jnp.max(score.reshape(16, 8, width), axis=0))
    return jnp.max(top, axis=0, keepdims=True)


def raise_pass(scores, top, raised_refs, cols):
    width = scores.shape[1]
    size = raised_refs[0].shape[1]
    total = jnp.zeros((8, width), jnp.float32)
    for g in range(scores.shape[0] // 128):
        part = slice(g * 128, (g + 1) * 128)
        raised = jnp.exp2(scores[part, :] - top)
        total = total + jnp.sum(raised.reshape(16, 8, width), axis=0)
        lower = g * 128 % size
        raised_refs[g * 128 // size][0, lower : lower + 128, cols] = raised.astype(low_type)
    return jnp.sum(total, axis=0, keepdims=True)


def mix(value_t, raised_refs, cols):
    size = raised_refs[0].shape[1]
    return sum(
        dot(value_t[:, i * size : (i + 1) * size], raised_ref[0, :, cols], 1, 0)
        for i, raised_ref in enumerate(raised_refs)
    )


def raised_parts(count, rows):
    size = count // RAISED_PARTS
    return (
        [pl.BlockSpec((1, size, rows), lambda h: (h, 0, 0))] * RAISED_PARTS,
        [shaped((HEADS, size, rows))] * RAISED_PARTS,
    )


def attend_own_kernel(
    groups, normed_ref, near_ref, w_query_ref, w_key_ref, w_value_ref,
    query_ref, key_ref, value_ref, *refs,
):
    raised_refs, refs = refs[:RAISED_PARTS], refs[RAISED_PARTS:]
    top_ref, total_ref, mixed_ref, packed_ref, bias, scores, value_t = refs
    rows = normed_ref.shape[0]
    half = groups // 2

    @pl.when(pl.program_id(0) == 0)
    def _():
        @pl.loop(0, rows // 128)
        def _(step):
            cols = pl.ds(pl.multiple_of(step * 128, 128), 128)
            packed = count_near(near_ref, cols, groups)
            packed_ref[:, cols] = packed[1]
            for g in range(rows // 128):
                bias[g * 128 : (g + 1) * 128, cols] = count_bias(packed[g // half], g % half)

    for weight_ref, out_ref in ((w_query_ref, query_ref), (w_key_ref, key_ref), (w_value_ref, value_ref)):
        out_ref[...] = dot(normed_ref[...], weight_ref[...], 1, 0).astype(low_type)
    value_t[...] = value_ref[...].T
    width = scores.shape[1]

    @pl.loop(0, rows // width)
    def _(step):
        cols = pl.ds(pl.multiple_of(step * width, width), width)
        least = jnp.full((8, width), -jnp.inf, jnp.float32)
        top = score_pass(key_ref, query_ref[cols, :], bias, scores, cols, least)
        top_ref[0, :, cols] = top
        total_ref[0, :, cols] = raise_pass(scores, top, raised_refs, cols)
        mixed_ref[0, :, cols] = mix(value_t, raised_refs, cols)


def attend_own(normed, near, w_query, w_key, w_value, far_rows):
    rows, width = normed.shape
    groups = (rows + far_rows) // 128
    by_row = pl.BlockSpec((rows, HEAD_DIM), lambda h: (0, h))
    by_weight = pl.BlockSpec((width, HEAD_DIM), lambda h: (0, h))
    by_head = pl.BlockSpec((1, 1, rows), lambda h: (h, 0, 0))
    return pl.pallas_call(
        functools.partial(attend_own_kernel, groups),
        grid=(HEADS,),
        in_specs=[pl.BlockSpec((rows, width), lambda h: (0, 0)), pl.BlockSpec((NEIGH, rows), lambda h: (0, 0))]
        + [by_weight] * 3,
        out_specs=[
            by_row,
            by_row,
            by_row,
            *raised_parts(rows, rows)[0],
            by_head,
            by_head,
            pl.BlockSpec((1, HEAD_DIM, rows), lambda h: (h, 0, 0)),
            pl.BlockSpec((128, rows), lambda h: (0, 0)),
        ],
        out_shape=[shaped((rows, width))] * 3
        + [
            *raised_parts(rows, rows)[1],
            shaped((HEADS, 1, rows), jnp.float32),
            shaped((HEADS, 1, rows), jnp.float32),
            shaped((HEADS, HEAD_DIM, rows), jnp.float32),
            shaped((128, rows), jnp.int32),
        ],
        scratch_shapes=[
            pltpu.VMEM((rows, rows), jnp.float32),
            pltpu.VMEM((rows, BLOCK), jnp.float32),
            pltpu.VMEM((HEAD_DIM, rows), low_type),
        ],
        compiler_params=pltpu.CompilerParams(vmem_limit_bytes=60 * 2**20),
        cost_estimate=pl.CostEstimate(flops=2**34, bytes_accessed=2**24, transcendentals=0),
    )(normed, near, w_query, w_key, w_value)


def fetch(parts, to_ref, sems):
    copies, lower = [], 0
    for position, part in enumerate(parts):
        upper = lower + part.shape[0]
        copies.append(pltpu.make_async_copy(part, to_ref.at[lower:upper, :], sems.at[position]))
        copies[-1].start()
        lower = upper
    return copies


def attend_far_kernel(
    skip, modulation_ref, query_ref, w_key_ref, w_value_ref, packed_ref, top_ref, total_ref, mixed_ref, *refs
):
    landed_refs, refs = refs[:4], refs[4:]
    raised_refs, refs = refs[:RAISED_PARTS], refs[RAISED_PARTS:]
    attended_ref, spread_own_ref, spread_far_ref, key_ref, value_ref, plain_ref, *refs = refs
    bias, scores, value_t, normed_ref, sems = refs
    far, rows = bias.shape

    @pl.when(pl.program_id(0) == 0)
    def _():
        copies = fetch(landed_refs, plain_ref, sems)

        @pl.loop(0, rows // 128)
        def _(step):
            cols = pl.ds(pl.multiple_of(step * 128, 128), 128)
            for g in range(far // 128):
                bias[g * 128 : (g + 1) * 128, cols] = count_bias(packed_ref[:, cols], g + skip)

        for copy in copies:
            copy.wait()
        plain = plain_ref[...].astype(jnp.float32)
        normed_ref[...] = (plain * (1.0 + modulation_ref[0:1, :]) + modulation_ref[1:2, :]).astype(low_type)

    key_ref[...] = dot(normed_ref[...], w_key_ref[...], 1, 0).astype(low_type)
    value_ref[...] = dot(normed_ref[...], w_value_ref[...], 1, 0).astype(low_type)
    value_t[...] = value_ref[...].T
    width = scores.shape[1]

    @pl.loop(0, rows // width)
    def _(step):
        cols = pl.ds(pl.multiple_of(step * width, width), width)
        own_top = top_ref[0, :, cols]
        least = jnp.broadcast_to(own_top, (8, width))
        top = score_pass(key_ref, query_ref[cols, :], bias, scores, cols, least)
        factor = jnp.exp2(own_top - top)
        total = raise_pass(scores, top, raised_refs, cols) + total_ref[0, :, cols] * factor
        inverse = 1.0 / total
        own_inverse = inverse * factor
        spread_far_ref[cols, :] = jnp.broadcast_to(inverse, (HEAD_DIM, width)).T
        spread_own_ref[cols, :] = jnp.broadcast_to(own_inverse, (HEAD_DIM, width)).T
        mixed = mix(value_t, raised_refs, cols) * inverse + mixed_ref[0, :, cols] * own_inverse
        attended_ref[cols, :] = mixed.T.astype(low_type)


def attend_far(modulation, queries, w_key, w_value, packed, top, total, mixed, landed):
    rows, width = queries.shape
    far = sum(part.shape[0] for part in landed)
    by_row = pl.BlockSpec((rows, HEAD_DIM), lambda h: (0, h))
    by_far = pl.BlockSpec((far, HEAD_DIM), lambda h: (0, h))
    by_weight = pl.BlockSpec((width, HEAD_DIM), lambda h: (0, h))
    by_head = pl.BlockSpec((1, 1, rows), lambda h: (h, 0, 0))
    groups = (rows + far) // 128
    return pl.pallas_call(
        functools.partial(attend_far_kernel, rows // 128 - groups // 2),
        grid=(HEADS,),
        in_specs=[
            pl.BlockSpec(modulation.shape, lambda h: (0, 0)),
            by_row,
            by_weight,
            by_weight,
            pl.BlockSpec(packed.shape, lambda h: (0, 0)),
            by_head,
            by_head,
            pl.BlockSpec((1, HEAD_DIM, rows), lambda h: (h, 0, 0)),
        ]
        + [anywhere] * len(landed),
        out_specs=[*raised_parts(far, rows)[0], by_row, by_row, by_row, by_far, by_far]
        + [pl.BlockSpec((far, width), lambda h: (0, 0))],
        out_shape=[
            *raised_parts(far, rows)[1],
            shaped((rows, width)),
            shaped((rows, width), jnp.float32),
            shaped((rows, width), jnp.float32),
            shaped((far, width)),
            shaped((far, width)),
            shaped((far, width)),
        ],
        scratch_shapes=[
            pltpu.VMEM((far, rows), jnp.float32),
            pltpu.VMEM((far, BLOCK), jnp.float32),
            pltpu.VMEM((HEAD_DIM, far), low_type),
            pltpu.VMEM((far, width), low_type),
            pltpu.SemaphoreType.DMA((len(landed),)),
        ],
        compiler_params=pltpu.CompilerParams(vmem_limit_bytes=60 * 2**20),
        cost_estimate=pl.CostEstimate(flops=2**33, bytes_accessed=2**23, transcendentals=0),
    )(modulation, queries, w_key, w_value, packed, top, total, mixed, *landed)


def attend_back_kernel(has_partial, query_ref, attended_ref, key_ref, value_ref, grad_ref, *refs):
    raised_refs, refs = refs[:RAISED_PARTS], refs[RAISED_PARTS:]
    size = raised_refs[0].shape[1]
    if has_partial:
        partial_ref, *refs = refs
    else:
        w_key_ref, w_value_ref, *refs = refs
    grad_query_ref, grad_key_ref, grad_value_ref, *refs = refs
    if not has_partial:
        *parcel_refs, low, key_t, grad_normed = refs
    else:
        low, key_t = refs
    rows = query_ref.shape[0]
    key_t[...] = key_ref[...].T

    @pl.loop(0, rows // BLOCK)
    def _(step):
        cols = pl.ds(pl.multiple_of(step * BLOCK, BLOCK), BLOCK)
        attended = attended_ref[cols, :].astype(jnp.float32)
        grad = grad_ref[cols, :]
        mean = jnp.sum((grad.astype(jnp.float32) * attended).T, axis=0, keepdims=True)
        for g in range(value_ref.shape[0] // 128):
            part = slice(g * 128, (g + 1) * 128)
            term = dot(value_ref[part, :], grad, 1, 1) - mean
            lower = g * 128 % size
            raised = raised_refs[g * 128 // size][0, lower : lower + 128, cols]
            low[part, cols] = (term * raised.astype(jnp.float32)).astype(low_type)
        total = dot(key_t[...], low[:, cols], 1, 0)
        if has_partial:
            total = (total + partial_ref[0, :, cols]) * score_scale
            grad_query_ref[cols, :] = total.T.astype(low_type)
        else:
            grad_query_ref[0, :, cols] = total

    for i, raised_ref in enumerate(raised_refs):
        grad_value_ref[i * size : (i + 1) * size, :] = dot(raised_ref[0], grad_ref[...], 1, 0).astype(low_type)
    grad_key_ref[...] = (dot(low[...], query_ref[...], 1, 0) * score_scale).astype(low_type)
    if has_partial:
        return

    back = dot(grad_key_ref[...], w_key_ref[...], 1, 1) + dot(grad_value_ref[...], w_value_ref[...], 1, 1)

    @pl.when(pl.program_id(0) == 0)
    def _():
        grad_normed[...] = back

    @pl.when(pl.program_id(0) > 0)
    def _():
        grad_normed[...] += back

    @pl.when(pl.program_id(0) == HEADS - 1)
    def _():
        grad = grad_normed[...]
        for position, parcel_ref in enumerate(parcel_refs):
            sends = parcel_ref.shape[0]
            parcel_ref[...] = grad[position * sends : (position + 1) * sends, :].astype(low_type)


def attend_back(queries, attended, keys, values, grads, raised, partial=None, returns=None):
    rows, width = queries.shape
    count = keys.shape[0]
    by_row = pl.BlockSpec((rows, HEAD_DIM), lambda h: (0, h))
    by_count = pl.BlockSpec((count, HEAD_DIM), lambda h: (0, h))
    by_head = pl.BlockSpec((1, HEAD_DIM, rows), lambda h: (h, 0, 0))
    in_specs = [by_row, by_row, by_count, by_count, by_row, *raised_parts(count, rows)[0]]
    out_specs = [by_row if returns is None else by_head, by_count, by_count]
    out_shape = [
        shaped((rows, width)) if returns is None else shaped((HEADS, HEAD_DIM, rows), jnp.float32),
        shaped((count, width)),
        shaped((count, width)),
    ]
    scratch = [pltpu.VMEM((count, rows), low_type), pltpu.VMEM((HEAD_DIM, count), low_type)]
    if returns is None:
        in_specs.append(by_head)
    else:
        by_weight = pl.BlockSpec((width, HEAD_DIM), lambda h: (0, h))
        in_specs += [by_weight, by_weight]
        sends = count // len(halo_steps)
        out_specs += [pl.BlockSpec((sends, width), lambda h: (0, 0))] * len(halo_steps)
        out_shape += [shaped((sends, width))] * len(halo_steps)
        scratch.append(pltpu.VMEM((count, width), jnp.float32))
    return pl.pallas_call(
        functools.partial(attend_back_kernel, returns is None),
        grid=(HEADS,),
        in_specs=in_specs,
        out_specs=out_specs,
        out_shape=out_shape,
        scratch_shapes=scratch,
        compiler_params=pltpu.CompilerParams(vmem_limit_bytes=BACK_GRANT * 2**20),
        cost_estimate=pl.CostEstimate(flops=count * 2**22, bytes_accessed=2**22, transcendentals=0),
    )(queries, attended, keys, values, grads, *raised, *([partial] if returns is None else returns))


def live_rows(count_ref, start, rows):
    place = lax.broadcasted_iota(jnp.int32, (rows, 1), 0) + start
    return (place < count_ref[0]).astype(jnp.float32)


class Mover:
    def __init__(self, sems):
        self.sems, self.used, self.open = sems, 0, []

    def start(self, source, target):
        copy = pltpu.make_async_copy(source, target, self.sems.at[self.used])
        self.used += 1
        copy.start()
        return copy

    def send(self, source, target):
        self.open.append(self.start(source, target))

    def finish(self):
        for copy in self.open:
            copy.wait()


def feed_chunk(weight_ref, second_ref, branch_ref, out_ref, grad_ref, hidden, grad_gate, grad_up, store, fresh, done, ready=None):
    units = weight_ref.shape[0] // 3
    gate_rows, up_rows, down_rows = (slice(i * units, (i + 1) * units) for i in range(3))
    for step in range(second_ref.shape[0] // ROW_BLOCK):
        rows = slice(step * ROW_BLOCK, (step + 1) * ROW_BLOCK)
        second = second_ref[rows, :]
        gate = dot(second, weight_ref[gate_rows, :], 1, 0)
        up = dot(second, weight_ref[up_rows, :], 1, 0)
        sigmoid = 1.0 / (1.0 + jnp.exp(-gate))
        activated = gate * sigmoid
        hidden[rows, :] = (activated * up).astype(low_type)
        back = dot(branch_ref[rows, :], weight_ref[down_rows, :], 1, 1)
        grad_gate[rows, :] = (back * up * (sigmoid + activated * (1.0 - sigmoid))).astype(low_type)
        grad_up[rows, :] = (back * activated).astype(low_type)
        out = dot(hidden[rows, :], weight_ref[down_rows, :], 1, 0)
        grad = dot(grad_gate[rows, :], weight_ref[gate_rows, :], 1, 1) + dot(
            grad_up[rows, :], weight_ref[up_rows, :], 1, 1
        )
        if step == 0 and ready is not None:
            ready()
        if fresh:
            out_ref[rows, :] = out
            grad_ref[rows, :] = grad
        else:
            out_ref[rows, :] += out
            grad_ref[rows, :] += grad
        if done is not None:
            done(rows)

    one, two = store
    half = units // 2
    one[:units, :] = dot(second_ref[...], grad_gate[...], 0, 0).astype(low_type)
    grad_up_weight = dot(second_ref[...], grad_up[...], 0, 0).astype(low_type)
    one[units:, :] = grad_up_weight[:half, :]
    two[:half, :] = grad_up_weight[half:, :]
    two[half : half + units, :] = dot(hidden[...], branch_ref[...], 0, 0).astype(low_type)


def feed_first_kernel(
    count_ref, modulation_ref, states_in, cotangent_in, attended_in, w_out_in,
    core_gate_in, core_up_in, core_down_in, own_gate_in, own_up_in, own_down_in,
    middle_out, second_out, branch_out, out_out, grad_out, core_one_out, core_two_out, own_one_out, own_two_out,
    states, cotangent, attended, w_out, core, own, second, branch, out, grad,
    core_one, core_two, own_one, own_two, hidden, grad_gate, grad_up, in_sems, out_sems,
):
    come, go = Mover(in_sems), Mover(out_sems)
    w_out_copy = come.start(w_out_in, w_out)
    blocks = [slice(lower, lower + ROW_BLOCK) for lower in range(0, states.shape[0], ROW_BLOCK)]
    pairs = [slice(lower, lower + 2 * ROW_BLOCK) for lower in range(0, states.shape[0], 2 * ROW_BLOCK)]
    units = own_gate_in.shape[0]

    def start_rows(rows):
        pairs = ((attended_in, attended), (states_in, states), (cotangent_in, cotangent))
        return [come.start(source.at[rows, :], target.at[rows, :]) for source, target in pairs]

    def start_units(sources, target):
        return [come.start(source, target.at[i * units : (i + 1) * units, :]) for i, source in enumerate(sources)]

    row_copies = [start_rows(rows) for rows in pairs]
    weight_copies = [start_units((core_gate_in, core_up_in, core_down_in), core)]
    weight_copies.append(start_units((own_gate_in, own_up_in, own_down_in), own))
    w_out_copy.wait()
    for index, rows in enumerate(blocks):
        if index % 2 == 0:
            for copy in row_copies[index // 2]:
                copy.wait()
        live = live_rows(count_ref, rows.start, ROW_BLOCK)
        middle = states[rows, :] + live * dot(attended[rows, :], w_out[...], 1, 0)
        states[rows, :] = middle
        plain, _ = norm_parts(middle)
        second[rows, :] = (plain * (1.0 + modulation_ref[2:3, :]) + modulation_ref[3:4, :]).astype(low_type)
        branch[rows, :] = (live * cotangent[rows, :]).astype(low_type)

    for source, target in ((states, middle_out), (second, second_out), (branch, branch_out)):
        go.send(source, target)

    def done(rows):
        if rows.stop == out.shape[0]:
            go.send(out, out_out)
            go.send(grad, grad_out)

    scratch = (hidden, grad_gate, grad_up)
    for copy in weight_copies[0]:
        copy.wait()
    feed_chunk(core, second, branch, out, grad, *scratch, (core_one, core_two), True, None)
    go.send(core_one, core_one_out)
    go.send(core_two, core_two_out)
    for copy in weight_copies[1]:
        copy.wait()
    feed_chunk(own, second, branch, out, grad, *scratch, (own_one, own_two), False, done)
    go.send(own_one, own_one_out)
    go.send(own_two, own_two_out)
    go.finish()


def feed_last_kernel(
    count_ref, core_ref, modulation_ref, cotangent_in, attended_in, w_out_in, spread_own_in, spread_far_in,
    middle_in, second_in, branch_in, out_in, grad_in, cross_half_in, cross_rest_in, far_half_in, far_rest_in,
    output_out, grad_middle_out, grad_own_out, grad_far_out, mod_grad_ref,
    cross_one_out, cross_two_out, far_one_out, far_two_out,
    cotangent, attended, w_out, spread_own, spread_far, middle, second, branch, out, grad, cross, far,
    grad_own, grad_far, cross_one, cross_two, far_one, far_two, w_out_grad,
    hidden, grad_gate, grad_up, in_sems, out_sems,
):
    come, go = Mover(in_sems), Mover(out_sems)
    half_rows = far_half_in.shape[0]

    def halves(half_in, rest_in, target):
        return [
            (source, target.at[pl.ds(pl.multiple_of(which * half_rows, half_rows), half_rows), :])
            for source, which in ((half_in, core_ref[1]), (rest_in, 1 - core_ref[1]))
        ]

    def start_all(pairs):
        return [come.start(source, target) for source, target in pairs]

    first_copies = start_all([(second_in, second), *halves(far_half_in, far_rest_in, far), (branch_in, branch)])
    scratch = (hidden, grad_gate, grad_up)
    for copy in first_copies:
        copy.wait()
    sum_copies = start_all([(out_in, out), (grad_in, grad)])
    late_copies = []

    def ready():
        for copy in sum_copies:
            copy.wait()
        late_copies.extend(
            start_all(
                [
                    *halves(cross_half_in, cross_rest_in, cross), (w_out_in, w_out), (middle_in, middle),
                    (cotangent_in, cotangent), (spread_own_in, spread_own), (spread_far_in, spread_far),
                    (attended_in, attended),
                ]
            )
        )

    feed_chunk(far, second, branch, out, grad, *scratch, (far_one, far_two), False, None, ready)
    go.send(far_one, far_one_out)
    for copy in late_copies:
        copy.wait()
    feed_chunk(cross, second, branch, out, grad, *scratch, (cross_one, cross_two), False, None)
    go.send(cross_one, cross_one_out)
    low_grad = hidden
    scale, bias = 0.0, 0.0
    for lower in range(0, middle.shape[0], ROW_BLOCK):
        rows = slice(lower, lower + ROW_BLOCK)
        live = live_rows(count_ref, lower, ROW_BLOCK)
        block = middle[rows, :]
        plain, inverse = norm_parts(block)
        middle[rows, :] = block + live * out[rows, :]
        grad_second = grad[rows, :]
        scale += jnp.sum(grad_second * plain, axis=0, keepdims=True)
        bias += jnp.sum(grad_second, axis=0, keepdims=True)
        grad_middle = cotangent[rows, :] + norm_back(grad_second * (1.0 + modulation_ref[2:3, :]), plain, inverse)
        cotangent[rows, :] = grad_middle
        low_grad[rows, :] = (live * grad_middle).astype(low_type)
        grad_attended = dot(low_grad[rows, :], w_out[...], 1, 1)
        grad_own[rows, :] = (grad_attended * spread_own[rows, :]).astype(low_type)
        grad_far[rows, :] = (grad_attended * spread_far[rows, :]).astype(low_type)
        if lower // ROW_BLOCK % 2:
            pair = slice(lower - ROW_BLOCK, lower + ROW_BLOCK)
            for source, target in (
                (middle, output_out), (cotangent, grad_middle_out), (grad_own, grad_own_out), (grad_far, grad_far_out),
            ):
                go.send(source.at[pair, :], target.at[pair, :])
    mod_grad_ref[0:1, :] = scale
    mod_grad_ref[1:2, :] = bias

    half = w_out_grad.shape[0] // 2
    w_out_grad[...] = dot(attended[...], low_grad[...], 0, 0).astype(low_type)
    for two, two_out, side_of in ((far_two, far_two_out, core_ref[0]), (cross_two, cross_two_out, 1 - core_ref[0])):
        start = pl.multiple_of(side_of * half, half)
        two[two.shape[0] - half :, :] = w_out_grad[pl.ds(start, half), :]
        go.send(two, two_out)
    go.finish()


def project_back_kernel(
    core_ref, modulation_ref, mod_two_ref, plain_in, query_in, plain_far_in, key_in, far_key_in, value_in, far_value_in,
    w_query_in, w_key_in, w_value_in,
    kept_out, sent_out, mod_grad_ref,
    plain, query, plain_far, key, far_key, value, far_value, w_query, w_key, w_value,
    weight_grad, packed, in_sems, out_sems,
):
    come, go = Mover(in_sems), Mover(out_sems)
    width = weight_grad.shape[2]
    half = width // 2
    own_half = pl.ds(pl.multiple_of(core_ref[0] * half, half), half)
    other_half = pl.ds(pl.multiple_of((1 - core_ref[0]) * half, half), half)
    groups = (
        ((plain_in, plain), (query_in, query), (w_query_in, w_query)),
        ((key_in, key), (plain_far_in, plain_far), (far_key_in, far_key), (w_key_in, w_key)),
        ((value_in, value), (far_value_in, far_value), (w_value_in, w_value)),
    )
    copies = [[come.start(source, target) for source, target in group] for group in groups]
    gain = (1.0 + modulation_ref[0:1, :]).T
    shift = modulation_ref[1:2, :].T
    scale, bias = 0.0, 0.0
    for kind, (own, far, weight) in enumerate(
        ((query, None, w_query), (key, far_key, w_key), (value, far_value, w_value))
    ):
        for copy in copies[kind]:
            copy.wait()
        grad = dot(plain[...], own[...], 0, 0)
        total = jnp.sum(own[...].astype(jnp.float32), axis=0, keepdims=True)
        if far is not None:
            grad += dot(plain_far[...], far[...], 0, 0)
            total += jnp.sum(far[...].astype(jnp.float32), axis=0, keepdims=True)
        matrix = weight[...].astype(jnp.float32)
        scale += jnp.sum(grad * matrix, axis=1, keepdims=True)
        bias += jnp.sum(matrix * total, axis=1, keepdims=True)
        weight_grad[kind] = (grad * gain + shift * total).astype(low_type)
        go.send(weight_grad.at[kind, own_half, :], kept_out.at[kind])
        go.send(weight_grad.at[kind, other_half, :], sent_out.at[kind * half : (kind + 1) * half, :])
    mod_grad_ref[0:1, :] = scale.T
    mod_grad_ref[1:2, :] = bias.T
    mod_grad_ref[2:4, :] = mod_two_ref[...]
    mod_grad = mod_grad_ref[...]
    high = mod_grad.astype(low_type).astype(jnp.float32)
    packed[...] = jnp.concatenate([high, mod_grad - high, jnp.zeros((8, high.shape[1]), jnp.float32)]).astype(low_type)
    go.send(packed, sent_out.at[3 * half : 3 * half + 16, :])
    go.finish()


def small(work, out_shapes, scalar_args, args, grant=16):
    def kernel(scalar_ref, *refs):
        for out_ref, value in zip(refs[len(args) :], work(scalar_ref, *refs[: len(args)])):
            out_ref[...] = value.astype(out_ref.dtype)

    return call(
        kernel, list(out_shapes), (scalar_args, *args), specs=[scalars] + [whole] * len(args), grant=grant, flops=2**29
    )


def half_of(ref, which):
    half = ref.shape[1] // 2
    return ref[:, pl.ds(pl.multiple_of(which * half, half), half), :].astype(jnp.float32)


def halves_of(side_of, *refs):
    return sum(half_of(ref, 1 - side_of) for ref in refs), sum(half_of(ref, side_of) for ref in refs)


def finish_kernel(
    states_ref, grad_middle_ref, query_ref, key_ref, value_ref, modulation_ref, send_ref, w_query_ref, w_key_ref, w_value_ref, *refs
):
    returned_refs, (grad_states_ref, returned, sems) = refs[:4], refs[4:]

    @pl.when(pl.program_id(0) == 0)
    def _():
        for copy in fetch(returned_refs, returned, sems):
            copy.wait()

    rows = states_ref.shape[0]
    sends = send_ref.shape[1]
    grad = sum(
        dot(own_ref[...], weight_ref[...], 1, 1)
        for own_ref, weight_ref in ((query_ref, w_query_ref), (key_ref, w_key_ref), (value_ref, w_value_ref))
    )
    for position in range(len(returned_refs)):
        chosen = chosen_rows(send_ref, position, rows, pl.program_id(0) * rows)
        grad += dot(chosen, returned[position * sends : (position + 1) * sends, :], 1, 0)
    plain, inverse = norm_parts(states_ref[...])
    grad_states_ref[...] = grad_middle_ref[...] + norm_back(grad * (1.0 + modulation_ref[0:1, :]), plain, inverse)


def finish(states, grad_middle, grads, modulation, send_list, weights, returned):
    rows, width = states.shape
    by_block = pl.BlockSpec((ROW_BLOCK, width), lambda i: (i, 0))
    once = [pl.BlockSpec(part.shape, lambda i: (0, 0)) for part in (modulation, send_list, *weights)]
    return pl.pallas_call(
        finish_kernel,
        grid=(rows // ROW_BLOCK,),
        in_specs=[by_block] * 5 + once + [anywhere] * len(returned),
        out_specs=by_block,
        out_shape=shaped((rows, width), jnp.float32),
        scratch_shapes=[
            pltpu.VMEM((sum(part.shape[0] for part in returned), width), low_type),
            pltpu.SemaphoreType.DMA((len(returned),)),
        ],
        compiler_params=pltpu.CompilerParams(vmem_limit_bytes=24 * 2**20),
        cost_estimate=pl.CostEstimate(flops=2**31, bytes_accessed=2**23, transcendentals=0),
    )(states, grad_middle, *grads, modulation, send_list, *weights, *returned)


def from_behind(block, axis, distance):
    devices = range(lax.axis_size(axis))
    route = [((i - distance) % len(devices), i) for i in devices]
    return lax.ppermute(block, axis, route)


def swap(block, mask):
    count = lax.axis_size("nodes") * lax.axis_size("hid")
    return lax.ppermute(block, everywhere, [(i, i ^ mask) for i in range(count)])


def place():
    return lax.axis_index("nodes") * lax.axis_size("hid") + lax.axis_index("hid")


def side(link):
    return (place() >> link) & 1


def added(parts):
    return sum(part.astype(jnp.float32) for part in parts).astype(low_type)


def pieces_of(block, count, index):
    size = block.shape[1] // count
    return lax.dynamic_slice_in_dim(block, index * size, size, 1)


def half_sum(block, link):
    return pieces_of(block, 2, side(link)) + swap(pieces_of(block, 2, 1 - side(link)), 1 << link)


def half_join(block, link):
    other = swap(block, 1 << link)
    return jnp.where(
        side(link) == 0, jnp.concatenate([block, other], axis=1), jnp.concatenate([other, block], axis=1)
    )


def pack_wide(values):
    high = lax.reduce_precision(values, 8, 7)
    both = jnp.concatenate([high, values - high]).astype(low_type)
    return jnp.concatenate([both, jnp.zeros((16 - both.shape[0], both.shape[1]), low_type)])


def unpack_wide(packed, count):
    packed = packed.astype(jnp.float32)
    return packed[:count] + packed[count : 2 * count]


def group_sum(block, wide, links):
    count = 1 << len(links)
    here = sum(side(link) << i for i, link in enumerate(links))
    total = pieces_of(block, count, here).astype(jnp.float32)
    shape = total.shape
    packed = pack_wide(wide)
    for mask in range(1, count):
        sent = pieces_of(block, count, here ^ mask).reshape(-1, shape[-1])
        come = swap(jnp.concatenate([sent, packed]), sum(((mask >> i) & 1) << link for i, link in enumerate(links)))
        total = total + come[: -packed.shape[0]].reshape(shape).astype(jnp.float32)
        wide = wide + unpack_wide(come[-packed.shape[0] :], wide.shape[0])
    return total.astype(low_type), wide


def group_join(block, links):
    found = [block]
    for mask in range(1, 1 << len(links)):
        found.append(swap(block, sum(((mask >> i) & 1) << link for i, link in enumerate(links))))
    for i, link in enumerate(links):
        turned = [found[k ^ (1 << i)] for k in range(len(found))]
        found = [jnp.where(side(link) == 0, kept, other) for kept, other in zip(found, turned)]
    return jnp.concatenate(found, axis=1)


def after(values, previous):
    return lax.optimization_barrier((values, previous))


def body(
    states,
    condition,
    mod_w,
    w_query,
    w_key,
    w_value,
    w_out,
    w_gate,
    w_up,
    w_down,
    counts,
    send_rows,
    neighbours,
    cotangent,
):
    rows, width = states.shape
    sends = send_rows.shape[2]
    ext = rows + len(halo_steps) * sends
    f32 = jnp.float32
    parcel = shaped((sends, width))
    send_list = send_rows[0]

    links = (lax.axis_size("nodes") * lax.axis_size("hid")).bit_length() - 1
    core, across, *around = range(links)

    normed, plain, modulation, *parcels = prepare(states, condition, mod_w, send_list)
    landed = [from_behind(part, everywhere, hop) for part, hop in zip(parcels, halo_steps)]
    shard, normed = after((w_gate, w_up, w_down), normed)
    near_half = side(around[0])
    middle_row = shard[1].shape[0] // 2
    far_half = jnp.where(
        near_half == 0,
        jnp.concatenate([shard[0], shard[1][:middle_row]]),
        jnp.concatenate([shard[1][middle_row:], shard[2]]),
    )
    far_half = swap(far_half, 1 << across)

    queries, own_keys, own_values, *own_raised, top, total, mixed, packed = attend_own(
        normed, neighbours.T, w_query, w_key, w_value, ext - rows
    )
    queries, far_half, landed, shard = lax.optimization_barrier((queries, far_half, landed, shard))
    core_shard = [swap(weight, 1 << core) for weight in shard]
    far_rest = swap(far_half, 1 << around[0])
    cross_half = swap(far_half, 1 << core)
    *far_raised, attended, spread_own, spread_far, far_keys, far_values, plain_far = attend_far(
        modulation, queries, w_key, w_value, packed, top, total, mixed, landed
    )

    low_rows = shaped((rows, width))
    wide_rows = shaped((rows, width), f32)
    shard_rows = sum(weight.size for weight in shard) // width
    all_units = shaped((shard_rows, width))
    half_grad = shaped((shard_rows // 2, width))
    joint_grad = shaped((shard_rows // 2 + width // 2, width))

    def room(*shapes):
        return [pltpu.VMEM(one.shape, one.dtype) for one in shapes]

    middle, second, branch, out, grad, core_one, core_two, own_one, own_two = call(
        feed_first_kernel,
        [wide_rows, low_rows, low_rows, wide_rows, wide_rows] + [half_grad] * 4,
        (counts, modulation, states, cotangent, attended, w_out, *core_shard, *shard),
        specs=[scalars, whole] + [anywhere] * 10,
        out_specs=[anywhere] * 9,
        scratch=room(wide_rows, wide_rows, low_rows, w_out, all_units, all_units, low_rows, low_rows)
        + room(wide_rows, wide_rows)
        + room(*[half_grad] * 4, *[low_rows] * 3)
        + [pltpu.SemaphoreType.DMA((13,)), pltpu.SemaphoreType.DMA((9,))],
        flops=2**34,
        moved=2**24,
    )
    core_index = jnp.stack([lax.axis_index("hid") & 1, near_half])
    (cross_half, far_rest), grad = after((cross_half, far_rest), grad)
    cross_rest = swap(far_rest, 1 << core)
    fold = (-1, width // 2, width)

    def over_cores(*grads):
        return [[kept.reshape(fold), swap(sent, 1 << core).reshape(fold)] for kept, sent in grads]

    first, second_link, *rest = around
    sides = jnp.stack([side(first), side(second_link)])

    def lines(blocks, count):
        return shaped((blocks, count, width))

    def first_halves(side_ref, one, one_come, two, two_come):
        return *halves_of(side_ref[0], one, one_come), *halves_of(side_ref[1], two, two_come)

    own_sums = over_cores((own_one, core_one), (own_two, core_two))
    kept = own_sums[0][0].shape[0]
    eighth = fold[1] // 2
    quarter = eighth // 2
    one_sent, one_own, two_sent, two_own = small(
        first_halves, [lines(kept, eighth)] * 4, sides, (*own_sums[0], *own_sums[1])
    )
    (one_sent, two_sent), cross_rest = after((one_sent, two_sent), cross_rest)
    own_come = swap(one_sent, 1 << first), swap(two_sent, 1 << second_link)
    output, grad_middle, grad_own, grad_far, mod_two, cross_one, cross_two, far_one, far_two = call(
        feed_last_kernel,
        [wide_rows, wide_rows, low_rows, low_rows, shaped((2, width), f32)] + [half_grad, joint_grad] * 2,
        (counts, core_index, modulation, cotangent, attended, w_out, spread_own, spread_far)
        + (middle, second, branch, out, grad, cross_half, cross_rest, far_half, far_rest),
        specs=[scalars, scalars, whole] + [anywhere] * 14,
        out_specs=[anywhere] * 4 + [whole] + [anywhere] * 4,
        scratch=room(wide_rows, low_rows, w_out, wide_rows, wide_rows, wide_rows, low_rows, low_rows)
        + room(wide_rows, wide_rows, all_units, all_units, low_rows, low_rows)
        + room(half_grad, joint_grad, half_grad, joint_grad)
        + room(w_out, *[low_rows] * 3)
        + [pltpu.SemaphoreType.DMA((14,)), pltpu.SemaphoreType.DMA((12,))],
        flops=2**34,
        moved=2**24,
    )

    (cross_one, cross_two), own_come = after((cross_one, cross_two), own_come)
    far_sums = over_cores((far_one, cross_one), (far_two, cross_two))
    one_sent, one_far, two_sent, two_far = small(
        first_halves,
        [lines(kept, eighth)] * 2 + [lines(kept + 1, eighth)] * 2,
        sides,
        (*far_sums[0], *far_sums[1]),
    )
    grad_far, (one_sent, two_sent) = after(grad_far, (one_sent, two_sent))
    far_come = swap(one_sent, 1 << first), swap(two_sent, 1 << second_link)
    partial, *far_pieces = attend_back(
        queries, attended, far_keys, far_values, grad_far, far_raised, returns=(w_key, w_value)
    )
    far_pieces, parcels = far_pieces[:2], far_pieces[2:]
    far_come, (grad_own, parcels, partial) = after(far_come, (grad_own, parcels, partial))

    def second_halves(side_ref, one_own, one_own_come, one_far, one_far_come, two_own, two_own_come, two_far, two_far_come):
        own_sent, own_kept = halves_of(side_ref[1], one_own, one_own_come)
        far_sent, far_kept = halves_of(side_ref[1], one_far, one_far_come)
        two_kept = two_own[...].astype(f32) + two_own_come[...].astype(f32)
        two_sent = two_far[...].astype(f32) + two_far_come[...].astype(f32)
        return jnp.concatenate([own_sent, far_sent]), own_kept, far_kept, two_kept, two_sent

    one_sent, one_own, one_far, two_own, two_sent = small(
        second_halves,
        [lines(2 * kept, quarter), lines(kept, quarter), lines(kept, quarter), lines(kept, eighth), lines(kept + 1, eighth)],
        sides,
        (one_own, own_come[0], one_far, far_come[0], two_own, own_come[1], two_far, far_come[1]),
    )
    (one_sent, two_sent), grad_own = after((one_sent, two_sent), grad_own)
    one_come, two_come = swap(one_sent, 1 << second_link), swap(two_sent, 1 << across)
    pieces = attend_back(queries, attended, own_keys, own_values, grad_own, own_raised, partial)
    (one_come, two_come), pieces = after((one_come, two_come), pieces)

    def third_halves(side_ref, one_own, one_far, one_come, two_own, two_last, two_come):
        one_kept = one_own[...].astype(f32) + one_come[:kept].astype(f32)
        one_sent = one_far[...].astype(f32) + one_come[kept:].astype(f32)
        here = side_ref[0]
        own_sent, own_kept = halves_of(here, two_own, two_come.at[:kept])
        last_sent, last_kept = halves_of(here, two_last.at[kept:], two_come.at[kept:])
        return one_sent, one_kept, jnp.concatenate([own_sent, last_sent]), jnp.concatenate([own_kept, last_kept])

    one_sent, one_kept, two_sent, two_kept = small(
        third_halves,
        [lines(kept, quarter)] * 2 + [lines(kept + 1, quarter)] * 2,
        sides,
        (one_own, one_far, one_come, two_own, two_sent, two_come),
    )
    (one_sent, two_sent), pieces = after((one_sent, two_sent), pieces)
    one_come, two_come = swap(one_sent, 1 << across), swap(two_sent, 1 << first)
    returned = [from_behind(part, everywhere, -hop) for part, hop in zip(parcels[:3], halo_steps)]
    far_low = shaped((ext - rows, width))
    attn_kept, attn_sent, mod_grad = call(
        project_back_kernel,
        [shaped((3, width // 2, width)), shaped((3 * width // 2 + 16, width)), shaped((4, width), f32)],
        (core_index, modulation, mod_two, plain, pieces[0], plain_far, pieces[1], far_pieces[0], pieces[2], far_pieces[1])
        + (w_query, w_key, w_value),
        specs=[scalars, whole, whole] + [anywhere] * 10,
        out_specs=[anywhere, anywhere, whole],
        scratch=room(low_rows, low_rows, far_low, low_rows, far_low, low_rows, far_low, w_query, w_key, w_value)
        + room(shaped((3, width, width)), shaped((16, width)))
        + [pltpu.SemaphoreType.DMA((10,)), pltpu.SemaphoreType.DMA((7,))],
        flops=2**32,
        moved=2**23,
    )

    def on_both(step, link):
        def run(one, two):
            both = step(jnp.concatenate([one, two]), link)
            return both[:kept], both[kept:]

        return run

    shard_steps = [on_both(half_sum, link) for link in rest]
    shard_steps += [on_both(half_join, link) for link in reversed(rest)]
    shard_steps.append(lambda one, two: (half_join(one, second_link), half_join(two, first)))
    shard_steps.append(lambda one, two: (half_join(one, first), half_join(two, second_link)))

    groups = [[across, first]] + [around[i : i + 2] for i in range(1, len(around), 2)]
    def over_attn_cores(kept, wide):
        come = swap(attn_sent, 1 << core)
        total = kept.astype(f32) + come[:-16].reshape(kept.shape).astype(f32)
        return total.astype(low_type), wide + unpack_wide(come[-16:], wide.shape[0])

    attn_steps = [over_attn_cores] + [functools.partial(group_sum, links=group) for group in groups]
    attn_steps += [lambda grad, wide, group=group: (group_join(grad, group), wide) for group in reversed(groups)]

    returned, (one_come, two_come), parcels, attn_sent = lax.optimization_barrier(
        (returned, (one_come, two_come), parcels, attn_sent)
    )
    returned.append(from_behind(parcels[3], everywhere, -halo_steps[3]))
    shard_state = added([one_kept, one_come]), added([two_kept, two_come])
    attn_state = attn_kept, mod_grad
    shard_turns = [[]] + [[step] for step in shard_steps]
    for index in range(max(len(shard_turns), len(attn_steps))):
        for step in shard_turns[index] if index < len(shard_turns) else []:
            shard_state = step(*shard_state)
        if index < len(attn_steps):
            attn_state = attn_steps[index](*attn_state)
        if index == 1:
            returned, attn_state = after(returned, attn_state)
        if index == 2:
            grad_states = finish(
                states, grad_middle, pieces, modulation, send_list, (w_query, w_key, w_value), returned
            )
            grad_states, attn_state = after(grad_states, attn_state)
        if index == len(shard_steps):
            one, two = shard_state
            shard_grad = jnp.concatenate([one, two[:kept]]).reshape(-1, width)
            shard_grad, two, attn_state = lax.optimization_barrier((shard_grad, two, attn_state))
            shard_grad = jnp.split(shard_grad.astype(f32), 3)
            shard_state = shard_grad, two
        if index % 2:
            shard_state, attn_state = after(shard_state, attn_state)
    (shard_grad, two), (attn_grad, mod_grad) = shard_state, attn_state
    grad_w_gate, grad_w_up, grad_w_down = shard_grad
    grad_w_query, grad_w_key, grad_w_value = half_join(attn_grad, core).astype(f32)
    grad_w_out = half_join(two[kept:], core)[0].astype(f32)
    mod_grad = mod_grad.reshape(-1)
    grad_mod_w = condition[:, None] * mod_grad[None, :]
    grad_condition = jnp.sum(mod_w.astype(f32) * mod_grad[None, :], axis=1)
    return (
        output,
        grad_states,
        grad_condition,
        grad_mod_w,
        grad_w_query,
        grad_w_key,
        grad_w_value,
        grad_w_out,
        grad_w_gate,
        grad_w_up,
        grad_w_down,
    )


def solution(mesh):
    rows = P(everywhere, None)
    placed = (
        rows,
        P(),
        P(),
        P(),
        P(),
        P(),
        P(),
        P(None, "hid"),
        P(None, "hid"),
        P("hid", None),
        P(everywhere),
        P(everywhere, None, None),
        rows,
        rows,
    )
    return jax.shard_map(
        body,
        mesh=mesh,
        in_specs=placed,
        out_specs=(rows, rows, P(), P(), P(), P(), P(), P(), P(None, "hid"), P(None, "hid"), P("hid", None)),
        check_vma=False,
    )
```

```python
import functools

import jax
import jax.numpy as jnp
from jax import lax
from jax.experimental import pallas as pl
from jax.experimental.pallas import tpu as pltpu
from jax.sharding import PartitionSpec as P

HEADS = 4
HEAD_DIM = 128
NEIGH = 16
BLOCK = 1024
ROW_BLOCK = 256
BACK_GRANT = 56
RAISED_PARTS = 1

epsilon = 1e-06
halo_steps = (1, -1, 2, -2)
highest = lax.Precision.HIGHEST
score_scale = HEAD_DIM ** (-0.5)
LOG2_E = 1.4426950408889634
low_type = jnp.bfloat16
everywhere = ("nodes", "hid")
whole = pl.BlockSpec(memory_space=pltpu.VMEM)
scalars = pl.BlockSpec(memory_space=pltpu.SMEM)
anywhere = pl.BlockSpec(memory_space=pl.ANY)


def dot(left, right, left_dim, right_dim):
    return lax.dot_general(
        left, right, (((left_dim,), (right_dim,)), ((), ())), preferred_element_type=jnp.float32
    )


def shaped(shape, dtype=low_type):
    return jax.ShapeDtypeStruct(shape, dtype)


def norm_parts(states):
    centred = states - jnp.mean(states, axis=-1, keepdims=True)
    inverse = lax.rsqrt(jnp.mean(centred * centred, axis=-1, keepdims=True) + epsilon)
    return (centred * inverse, inverse)


def norm_back(grad_plain, plain, inverse):
    first_mean = jnp.mean(grad_plain, axis=-1, keepdims=True)
    second_mean = jnp.mean(grad_plain * plain, axis=-1, keepdims=True)
    return inverse * (grad_plain - first_mean - plain * second_mean)


def call(kernel, out_shape, args, specs=None, out_specs=None, scratch=(), flops=0, moved=0, grant=60):
    single = not isinstance(out_shape, list)
    return pl.pallas_call(
        kernel,
        in_specs=specs or [whole] * len(args),
        out_specs=out_specs or (whole if single else [whole] * len(out_shape)),
        out_shape=out_shape,
        scratch_shapes=list(scratch),
        compiler_params=pltpu.CompilerParams(vmem_limit_bytes=grant * 2**20),
        cost_estimate=pl.CostEstimate(flops=flops, bytes_accessed=moved, transcendentals=0),
    )(*args)


def chosen_rows(send_ref, position, rows, first=0):
    sends = send_ref.shape[1]
    place = lax.broadcasted_iota(jnp.int32, (rows, sends), 0) + first
    return jnp.where(place == send_ref[position : position + 1, :], 1.0, 0.0).astype(low_type)


def prepare_kernel(
    states_ref, condition_ref, mod_w_ref, send_ref, normed_ref, plain_ref, modulation_ref, *refs
):
    *parcel_refs, plain = refs
    step, (block, width) = pl.program_id(0), states_ref.shape

    @pl.when(step == 0)
    def _():
        mixed = sum(
            condition_ref[i] * mod_w_ref[i : i + 1, :].astype(jnp.float32) for i in range(condition_ref.shape[0])
        )
        for piece in range(4):
            modulation_ref[piece : piece + 1, :] = mixed[:, piece * width : (piece + 1) * width]

    values, _ = norm_parts(states_ref[...])
    plain_ref[...] = values.astype(low_type)
    plain[pl.ds(pl.multiple_of(step * block, block), block), :] = plain_ref[...]
    normed_ref[...] = (values * (1.0 + modulation_ref[0:1, :]) + modulation_ref[1:2, :]).astype(low_type)

    @pl.when(step == pl.num_programs(0) - 1)
    def _():
        for position, parcel_ref in enumerate(parcel_refs):
            chosen = chosen_rows(send_ref, position, plain.shape[0])
            parcel_ref[...] = dot(chosen, plain[...], 0, 0).astype(low_type)


def prepare(states, condition, mod_w, send_list):
    rows, width = states.shape
    by_block = pl.BlockSpec((2 * ROW_BLOCK, width), lambda i: (i, 0))

    def once(*shape):
        return pl.BlockSpec(shape, lambda i: (0,) * len(shape))

    count, sends = send_list.shape
    return pl.pallas_call(
        prepare_kernel,
        grid=(rows // ROW_BLOCK // 2,),
        in_specs=[by_block, scalars, once(*mod_w.shape), once(*send_list.shape)],
        out_specs=[by_block, by_block, once(4, width)] + [once(sends, width)] * count,
        out_shape=[shaped((rows, width)), shaped((rows, width)), shaped((4, width), jnp.float32)]
        + [shaped((sends, width))] * count,
        scratch_shapes=[pltpu.VMEM((rows, width), low_type)],
        compiler_params=pltpu.CompilerParams(vmem_limit_bytes=60 * 2**20),
        cost_estimate=pl.CostEstimate(flops=2**30, bytes_accessed=2**22, transcendentals=0),
    )(states, condition, mod_w, send_list)


def count_near(near_ref, cols, groups):
    half = groups // 2
    near = near_ref[:, cols]
    group = near >> 7
    upper = group >= half
    unit = jnp.left_shift(1, 5 * jnp.where(upper, group - half, group))
    low = near & 127
    low_unit = jnp.where(upper, 0, unit)
    high_unit = jnp.where(upper, unit, 0)
    place = lax.broadcasted_iota(jnp.int32, (128, 128), 0)
    low_count = jnp.zeros((128, 128), jnp.int32)
    high_count = low_count
    for n in range(NEIGH):
        same = low[n : n + 1] == place
        low_count = low_count + jnp.where(same, low_unit[n : n + 1], 0)
        high_count = high_count + jnp.where(same, high_unit[n : n + 1], 0)
    return low_count, high_count


def count_bias(packed, position):
    count = (packed >> (5 * position)) & 31
    return jnp.where(count > 0, jnp.log2(count.astype(jnp.float32)), -1e30)


def score_pass(key_ref, query, bias, scores, cols, top):
    width = scores.shape[1]
    for g in range(scores.shape[0] // 128):
        part = slice(g * 128, (g + 1) * 128)
        score = dot(key_ref[part, :], query, 1, 1) * (score_scale * LOG2_E) + bias[part, cols]
        scores[part, :] = score
        top = jnp.maximum(top, jnp.max(score.reshape(16, 8, width), axis=0))
    return jnp.max(top, axis=0, keepdims=True)


def raise_pass(scores, top, raised_refs, cols):
    width = scores.shape[1]
    size = raised_refs[0].shape[1]
    total = jnp.zeros((8, width), jnp.float32)
    for g in range(scores.shape[0] // 128):
        part = slice(g * 128, (g + 1) * 128)
        raised = jnp.exp2(scores[part, :] - top)
        total = total + jnp.sum(raised.reshape(16, 8, width), axis=0)
        lower = g * 128 % size
        raised_refs[g * 128 // size][0, lower : lower + 128, cols] = raised.astype(low_type)
    return jnp.sum(total, axis=0, keepdims=True)


def mix(value_t, raised_refs, cols):
    size = raised_refs[0].shape[1]
    return sum(
        dot(value_t[:, i * size : (i + 1) * size], raised_ref[0, :, cols], 1, 0)
        for i, raised_ref in enumerate(raised_refs)
    )


def raised_parts(count, rows):
    size = count // RAISED_PARTS
    return (
        [pl.BlockSpec((1, size, rows), lambda h: (h, 0, 0))] * RAISED_PARTS,
        [shaped((HEADS, size, rows))] * RAISED_PARTS,
    )


def attend_own_kernel(
    groups, normed_ref, near_ref, w_query_ref, w_key_ref, w_value_ref,
    query_ref, key_ref, value_ref, *refs,
):
    raised_refs, refs = refs[:RAISED_PARTS], refs[RAISED_PARTS:]
    top_ref, total_ref, mixed_ref, packed_ref, bias, scores, value_t = refs
    rows = normed_ref.shape[0]
    half = groups // 2

    @pl.when(pl.program_id(0) == 0)
    def _():
        @pl.loop(0, rows // 128)
        def _(step):
            cols = pl.ds(pl.multiple_of(step * 128, 128), 128)
            packed = count_near(near_ref, cols, groups)
            packed_ref[:, cols] = packed[1]
            for g in range(rows // 128):
                bias[g * 128 : (g + 1) * 128, cols] = count_bias(packed[g // half], g % half)

    for weight_ref, out_ref in ((w_query_ref, query_ref), (w_key_ref, key_ref), (w_value_ref, value_ref)):
        out_ref[...] = dot(normed_ref[...], weight_ref[...], 1, 0).astype(low_type)
    value_t[...] = value_ref[...].T
    width = scores.shape[1]

    @pl.loop(0, rows // width)
    def _(step):
        cols = pl.ds(pl.multiple_of(step * width, width), width)
        least = jnp.full((8, width), -jnp.inf, jnp.float32)
        top = score_pass(key_ref, query_ref[cols, :], bias, scores, cols, least)
        top_ref[0, :, cols] = top
        total_ref[0, :, cols] = raise_pass(scores, top, raised_refs, cols)
        mixed_ref[0, :, cols] = mix(value_t, raised_refs, cols)


def attend_own(normed, near, w_query, w_key, w_value, far_rows):
    rows, width = normed.shape
    groups = (rows + far_rows) // 128
    by_row = pl.BlockSpec((rows, HEAD_DIM), lambda h: (0, h))
    by_weight = pl.BlockSpec((width, HEAD_DIM), lambda h: (0, h))
    by_head = pl.BlockSpec((1, 1, rows), lambda h: (h, 0, 0))
    return pl.pallas_call(
        functools.partial(attend_own_kernel, groups),
        grid=(HEADS,),
        in_specs=[pl.BlockSpec((rows, width), lambda h: (0, 0)), pl.BlockSpec((NEIGH, rows), lambda h: (0, 0))]
        + [by_weight] * 3,
        out_specs=[
            by_row,
            by_row,
            by_row,
            *raised_parts(rows, rows)[0],
            by_head,
            by_head,
            pl.BlockSpec((1, HEAD_DIM, rows), lambda h: (h, 0, 0)),
            pl.BlockSpec((128, rows), lambda h: (0, 0)),
        ],
        out_shape=[shaped((rows, width))] * 3
        + [
            *raised_parts(rows, rows)[1],
            shaped((HEADS, 1, rows), jnp.float32),
            shaped((HEADS, 1, rows), jnp.float32),
            shaped((HEADS, HEAD_DIM, rows), jnp.float32),
            shaped((128, rows), jnp.int32),
        ],
        scratch_shapes=[
            pltpu.VMEM((rows, rows), jnp.float32),
            pltpu.VMEM((rows, BLOCK), jnp.float32),
            pltpu.VMEM((HEAD_DIM, rows), low_type),
        ],
        compiler_params=pltpu.CompilerParams(vmem_limit_bytes=56 * 2**20),
        cost_estimate=pl.CostEstimate(flops=2**34, bytes_accessed=2**24, transcendentals=0),
    )(normed, near, w_query, w_key, w_value)


def fetch(parts, to_ref, sems):
    copies, lower = [], 0
    for position, part in enumerate(parts):
        upper = lower + part.shape[0]
        copies.append(pltpu.make_async_copy(part, to_ref.at[lower:upper, :], sems.at[position]))
        copies[-1].start()
        lower = upper
    return copies


def attend_far_kernel(
    skip, modulation_ref, query_ref, w_key_ref, w_value_ref, packed_ref, top_ref, total_ref, mixed_ref, *refs
):
    landed_refs, refs = refs[:4], refs[4:]
    raised_refs, refs = refs[:RAISED_PARTS], refs[RAISED_PARTS:]
    attended_ref, spread_own_ref, spread_far_ref, key_ref, value_ref, plain_ref, *refs = refs
    bias, scores, value_t, normed_ref, sems = refs
    far, rows = bias.shape

    @pl.when(pl.program_id(0) == 0)
    def _():
        copies = fetch(landed_refs, plain_ref, sems)

        @pl.loop(0, rows // 128)
        def _(step):
            cols = pl.ds(pl.multiple_of(step * 128, 128), 128)
            for g in range(far // 128):
                bias[g * 128 : (g + 1) * 128, cols] = count_bias(packed_ref[:, cols], g + skip)

        for copy in copies:
            copy.wait()
        plain = plain_ref[...].astype(jnp.float32)
        normed_ref[...] = (plain * (1.0 + modulation_ref[0:1, :]) + modulation_ref[1:2, :]).astype(low_type)

    key_ref[...] = dot(normed_ref[...], w_key_ref[...], 1, 0).astype(low_type)
    value_ref[...] = dot(normed_ref[...], w_value_ref[...], 1, 0).astype(low_type)
    value_t[...] = value_ref[...].T
    width = scores.shape[1]

    @pl.loop(0, rows // width)
    def _(step):
        cols = pl.ds(pl.multiple_of(step * width, width), width)
        own_top = top_ref[0, :, cols]
        least = jnp.broadcast_to(own_top, (8, width))
        top = score_pass(key_ref, query_ref[cols, :], bias, scores, cols, least)
        factor = jnp.exp2(own_top - top)
        total = raise_pass(scores, top, raised_refs, cols) + total_ref[0, :, cols] * factor
        inverse = 1.0 / total
        own_inverse = inverse * factor
        spread_far_ref[cols, :] = jnp.broadcast_to(inverse, (HEAD_DIM, width)).T
        spread_own_ref[cols, :] = jnp.broadcast_to(own_inverse, (HEAD_DIM, width)).T
        mixed = mix(value_t, raised_refs, cols) * inverse + mixed_ref[0, :, cols] * own_inverse
        attended_ref[cols, :] = mixed.T.astype(low_type)


def attend_far(modulation, queries, w_key, w_value, packed, top, total, mixed, landed):
    rows, width = queries.shape
    far = sum(part.shape[0] for part in landed)
    by_row = pl.BlockSpec((rows, HEAD_DIM), lambda h: (0, h))
    by_far = pl.BlockSpec((far, HEAD_DIM), lambda h: (0, h))
    by_weight = pl.BlockSpec((width, HEAD_DIM), lambda h: (0, h))
    by_head = pl.BlockSpec((1, 1, rows), lambda h: (h, 0, 0))
    groups = (rows + far) // 128
    return pl.pallas_call(
        functools.partial(attend_far_kernel, rows // 128 - groups // 2),
        grid=(HEADS,),
        in_specs=[
            pl.BlockSpec(modulation.shape, lambda h: (0, 0)),
            by_row,
            by_weight,
            by_weight,
            pl.BlockSpec(packed.shape, lambda h: (0, 0)),
            by_head,
            by_head,
            pl.BlockSpec((1, HEAD_DIM, rows), lambda h: (h, 0, 0)),
        ]
        + [anywhere] * len(landed),
        out_specs=[*raised_parts(far, rows)[0], by_row, by_row, by_row, by_far, by_far]
        + [pl.BlockSpec((far, width), lambda h: (0, 0))],
        out_shape=[
            *raised_parts(far, rows)[1],
            shaped((rows, width)),
            shaped((rows, width), jnp.float32),
            shaped((rows, width), jnp.float32),
            shaped((far, width)),
            shaped((far, width)),
            shaped((far, width)),
        ],
        scratch_shapes=[
            pltpu.VMEM((far, rows), jnp.float32),
            pltpu.VMEM((far, BLOCK), jnp.float32),
            pltpu.VMEM((HEAD_DIM, far), low_type),
            pltpu.VMEM((far, width), low_type),
            pltpu.SemaphoreType.DMA((len(landed),)),
        ],
        compiler_params=pltpu.CompilerParams(vmem_limit_bytes=56 * 2**20),
        cost_estimate=pl.CostEstimate(flops=2**33, bytes_accessed=2**23, transcendentals=0),
    )(modulation, queries, w_key, w_value, packed, top, total, mixed, *landed)


def attend_back_kernel(has_partial, query_ref, attended_ref, key_ref, value_ref, grad_ref, *refs):
    raised_refs, refs = refs[:RAISED_PARTS], refs[RAISED_PARTS:]
    size = raised_refs[0].shape[1]
    if has_partial:
        partial_ref, *refs = refs
    else:
        w_key_ref, w_value_ref, *refs = refs
    grad_query_ref, grad_key_ref, grad_value_ref, *refs = refs
    if not has_partial:
        *parcel_refs, low, key_t, grad_normed = refs
    else:
        low, key_t = refs
    rows = query_ref.shape[0]
    key_t[...] = key_ref[...].T

    @pl.loop(0, rows // BLOCK)
    def _(step):
        cols = pl.ds(pl.multiple_of(step * BLOCK, BLOCK), BLOCK)
        attended = attended_ref[cols, :].astype(jnp.float32)
        grad = grad_ref[cols, :]
        mean = jnp.sum((grad.astype(jnp.float32) * attended).T, axis=0, keepdims=True)
        for g in range(value_ref.shape[0] // 128):
            part = slice(g * 128, (g + 1) * 128)
            term = dot(value_ref[part, :], grad, 1, 1) - mean
            lower = g * 128 % size
            raised = raised_refs[g * 128 // size][0, lower : lower + 128, cols]
            low[part, cols] = (term * raised.astype(jnp.float32)).astype(low_type)
        total = dot(key_t[...], low[:, cols], 1, 0)
        if has_partial:
            total = (total + partial_ref[0, :, cols]) * score_scale
            grad_query_ref[cols, :] = total.T.astype(low_type)
        else:
            grad_query_ref[0, :, cols] = total

    for i, raised_ref in enumerate(raised_refs):
        grad_value_ref[i * size : (i + 1) * size, :] = dot(raised_ref[0], grad_ref[...], 1, 0).astype(low_type)
    grad_key_ref[...] = (dot(low[...], query_ref[...], 1, 0) * score_scale).astype(low_type)
    if has_partial:
        return

    back = dot(grad_key_ref[...], w_key_ref[...], 1, 1) + dot(grad_value_ref[...], w_value_ref[...], 1, 1)

    @pl.when(pl.program_id(0) == 0)
    def _():
        grad_normed[...] = back

    @pl.when(pl.program_id(0) > 0)
    def _():
        grad_normed[...] += back

    @pl.when(pl.program_id(0) == HEADS - 1)
    def _():
        grad = grad_normed[...]
        for position, parcel_ref in enumerate(parcel_refs):
            sends = parcel_ref.shape[0]
            parcel_ref[...] = grad[position * sends : (position + 1) * sends, :].astype(low_type)


def attend_back(queries, attended, keys, values, grads, raised, partial=None, returns=None):
    rows, width = queries.shape
    count = keys.shape[0]
    by_row = pl.BlockSpec((rows, HEAD_DIM), lambda h: (0, h))
    by_count = pl.BlockSpec((count, HEAD_DIM), lambda h: (0, h))
    by_head = pl.BlockSpec((1, HEAD_DIM, rows), lambda h: (h, 0, 0))
    in_specs = [by_row, by_row, by_count, by_count, by_row, *raised_parts(count, rows)[0]]
    out_specs = [by_row if returns is None else by_head, by_count, by_count]
    out_shape = [
        shaped((rows, width)) if returns is None else shaped((HEADS, HEAD_DIM, rows), jnp.float32),
        shaped((count, width)),
        shaped((count, width)),
    ]
    scratch = [pltpu.VMEM((count, rows), low_type), pltpu.VMEM((HEAD_DIM, count), low_type)]
    if returns is None:
        in_specs.append(by_head)
    else:
        by_weight = pl.BlockSpec((width, HEAD_DIM), lambda h: (0, h))
        in_specs += [by_weight, by_weight]
        sends = count // len(halo_steps)
        out_specs += [pl.BlockSpec((sends, width), lambda h: (0, 0))] * len(halo_steps)
        out_shape += [shaped((sends, width))] * len(halo_steps)
        scratch.append(pltpu.VMEM((count, width), jnp.float32))
    return pl.pallas_call(
        functools.partial(attend_back_kernel, returns is None),
        grid=(HEADS,),
        in_specs=in_specs,
        out_specs=out_specs,
        out_shape=out_shape,
        scratch_shapes=scratch,
        compiler_params=pltpu.CompilerParams(vmem_limit_bytes=BACK_GRANT * 2**20),
        cost_estimate=pl.CostEstimate(flops=count * 2**22, bytes_accessed=2**22, transcendentals=0),
    )(queries, attended, keys, values, grads, *raised, *([partial] if returns is None else returns))


def live_rows(count_ref, start, rows):
    place = lax.broadcasted_iota(jnp.int32, (rows, 1), 0) + start
    return (place < count_ref[0]).astype(jnp.float32)


class Mover:
    def __init__(self, sems):
        self.sems, self.used, self.open = sems, 0, []

    def start(self, source, target):
        copy = pltpu.make_async_copy(source, target, self.sems.at[self.used])
        self.used += 1
        copy.start()
        return copy

    def send(self, source, target):
        self.open.append(self.start(source, target))

    def finish(self):
        for copy in self.open:
            copy.wait()


def feed_chunk(weight_ref, second_ref, branch_ref, out_ref, grad_ref, hidden, grad_gate, grad_up, store, fresh, done, ready=None):
    units = weight_ref.shape[0] // 3
    gate_rows, up_rows, down_rows = (slice(i * units, (i + 1) * units) for i in range(3))
    for step in range(second_ref.shape[0] // ROW_BLOCK):
        rows = slice(step * ROW_BLOCK, (step + 1) * ROW_BLOCK)
        second = second_ref[rows, :]
        gate = dot(second, weight_ref[gate_rows, :], 1, 0)
        up = dot(second, weight_ref[up_rows, :], 1, 0)
        sigmoid = 1.0 / (1.0 + jnp.exp(-gate))
        activated = gate * sigmoid
        hidden[rows, :] = (activated * up).astype(low_type)
        back = dot(branch_ref[rows, :], weight_ref[down_rows, :], 1, 1)
        grad_gate[rows, :] = (back * up * (sigmoid + activated * (1.0 - sigmoid))).astype(low_type)
        grad_up[rows, :] = (back * activated).astype(low_type)
        out = dot(hidden[rows, :], weight_ref[down_rows, :], 1, 0)
        grad = dot(grad_gate[rows, :], weight_ref[gate_rows, :], 1, 1) + dot(
            grad_up[rows, :], weight_ref[up_rows, :], 1, 1
        )
        if step == 0 and ready is not None:
            ready()
        if fresh:
            out_ref[rows, :] = out
            grad_ref[rows, :] = grad
        else:
            out_ref[rows, :] += out
            grad_ref[rows, :] += grad
        if done is not None:
            done(rows)

    one, two = store
    half = units // 2
    one[:units, :] = dot(second_ref[...], grad_gate[...], 0, 0).astype(low_type)
    grad_up_weight = dot(second_ref[...], grad_up[...], 0, 0).astype(low_type)
    one[units:, :] = grad_up_weight[:half, :]
    two[:half, :] = grad_up_weight[half:, :]
    two[half : half + units, :] = dot(hidden[...], branch_ref[...], 0, 0).astype(low_type)


def feed_first_kernel(
    count_ref, modulation_ref, states_in, cotangent_in, attended_in, w_out_in,
    core_gate_in, core_up_in, core_down_in, own_gate_in, own_up_in, own_down_in,
    middle_out, second_out, branch_out, out_out, grad_out, core_one_out, core_two_out, own_one_out, own_two_out,
    states, cotangent, attended, w_out, core, own, second, branch, out, grad,
    core_one, core_two, own_one, own_two, hidden, grad_gate, grad_up, in_sems, out_sems,
):
    come, go = Mover(in_sems), Mover(out_sems)
    w_out_copy = come.start(w_out_in, w_out)
    blocks = [slice(lower, lower + ROW_BLOCK) for lower in range(0, states.shape[0], ROW_BLOCK)]
    pairs = [slice(lower, lower + 2 * ROW_BLOCK) for lower in range(0, states.shape[0], 2 * ROW_BLOCK)]
    units = own_gate_in.shape[0]

    def start_rows(rows):
        pairs = ((attended_in, attended), (states_in, states), (cotangent_in, cotangent))
        return [come.start(source.at[rows, :], target.at[rows, :]) for source, target in pairs]

    def start_units(sources, target):
        return [come.start(source, target.at[i * units : (i + 1) * units, :]) for i, source in enumerate(sources)]

    row_copies = [start_rows(rows) for rows in pairs]
    weight_copies = [start_units((core_gate_in, core_up_in, core_down_in), core)]
    weight_copies.append(start_units((own_gate_in, own_up_in, own_down_in), own))
    w_out_copy.wait()
    for index, rows in enumerate(blocks):
        if index % 2 == 0:
            for copy in row_copies[index // 2]:
                copy.wait()
        live = live_rows(count_ref, rows.start, ROW_BLOCK)
        middle = states[rows, :] + live * dot(attended[rows, :], w_out[...], 1, 0)
        states[rows, :] = middle
        plain, _ = norm_parts(middle)
        second[rows, :] = (plain * (1.0 + modulation_ref[2:3, :]) + modulation_ref[3:4, :]).astype(low_type)
        branch[rows, :] = (live * cotangent[rows, :]).astype(low_type)

    for source, target in ((states, middle_out), (second, second_out), (branch, branch_out)):
        go.send(source, target)

    def done(rows):
        if rows.stop == out.shape[0]:
            go.send(out, out_out)
            go.send(grad, grad_out)

    scratch = (hidden, grad_gate, grad_up)
    for copy in weight_copies[0]:
        copy.wait()
    feed_chunk(core, second, branch, out, grad, *scratch, (core_one, core_two), True, None)
    go.send(core_one, core_one_out)
    go.send(core_two, core_two_out)
    for copy in weight_copies[1]:
        copy.wait()
    feed_chunk(own, second, branch, out, grad, *scratch, (own_one, own_two), False, done)
    go.send(own_one, own_one_out)
    go.send(own_two, own_two_out)
    go.finish()


def feed_last_kernel(
    count_ref, core_ref, modulation_ref, cotangent_in, attended_in, w_out_in, spread_own_in, spread_far_in,
    middle_in, second_in, branch_in, out_in, grad_in, cross_half_in, cross_rest_in, far_half_in, far_rest_in,
    output_out, grad_middle_out, grad_own_out, grad_far_out, mod_grad_ref,
    cross_one_out, cross_two_out, far_one_out, far_two_out,
    cotangent, attended, w_out, spread_own, spread_far, middle, second, branch, out, grad, cross, far,
    grad_own, grad_far, cross_one, cross_two, far_one, far_two, w_out_grad,
    hidden, grad_gate, grad_up, in_sems, out_sems,
):
    come, go = Mover(in_sems), Mover(out_sems)
    half_rows = far_half_in.shape[0]

    def halves(half_in, rest_in, target):
        return [
            (source, target.at[pl.ds(pl.multiple_of(which * half_rows, half_rows), half_rows), :])
            for source, which in ((half_in, core_ref[1]), (rest_in, 1 - core_ref[1]))
        ]

    def start_all(pairs):
        return [come.start(source, target) for source, target in pairs]

    first_copies = start_all([(second_in, second), *halves(far_half_in, far_rest_in, far), (branch_in, branch)])
    scratch = (hidden, grad_gate, grad_up)
    for copy in first_copies:
        copy.wait()
    sum_copies = start_all([(out_in, out), (grad_in, grad)])
    late_copies = []

    def ready():
        for copy in sum_copies:
            copy.wait()
        late_copies.extend(
            start_all(
                [
                    *halves(cross_half_in, cross_rest_in, cross), (w_out_in, w_out), (middle_in, middle),
                    (cotangent_in, cotangent), (spread_own_in, spread_own), (spread_far_in, spread_far),
                    (attended_in, attended),
                ]
            )
        )

    feed_chunk(far, second, branch, out, grad, *scratch, (far_one, far_two), False, None, ready)
    go.send(far_one, far_one_out)
    for copy in late_copies:
        copy.wait()
    feed_chunk(cross, second, branch, out, grad, *scratch, (cross_one, cross_two), False, None)
    go.send(cross_one, cross_one_out)
    low_grad = hidden
    scale, bias = 0.0, 0.0
    for lower in range(0, middle.shape[0], ROW_BLOCK):
        rows = slice(lower, lower + ROW_BLOCK)
        live = live_rows(count_ref, lower, ROW_BLOCK)
        block = middle[rows, :]
        plain, inverse = norm_parts(block)
        middle[rows, :] = block + live * out[rows, :]
        grad_second = grad[rows, :]
        scale += jnp.sum(grad_second * plain, axis=0, keepdims=True)
        bias += jnp.sum(grad_second, axis=0, keepdims=True)
        grad_middle = cotangent[rows, :] + norm_back(grad_second * (1.0 + modulation_ref[2:3, :]), plain, inverse)
        cotangent[rows, :] = grad_middle
        low_grad[rows, :] = (live * grad_middle).astype(low_type)
        grad_attended = dot(low_grad[rows, :], w_out[...], 1, 1)
        grad_own[rows, :] = (grad_attended * spread_own[rows, :]).astype(low_type)
        grad_far[rows, :] = (grad_attended * spread_far[rows, :]).astype(low_type)
        if lower // ROW_BLOCK % 2:
            pair = slice(lower - ROW_BLOCK, lower + ROW_BLOCK)
            for source, target in (
                (middle, output_out), (cotangent, grad_middle_out), (grad_own, grad_own_out), (grad_far, grad_far_out),
            ):
                go.send(source.at[pair, :], target.at[pair, :])
    mod_grad_ref[0:1, :] = scale
    mod_grad_ref[1:2, :] = bias

    half = w_out_grad.shape[0] // 2
    w_out_grad[...] = dot(attended[...], low_grad[...], 0, 0).astype(low_type)
    for two, two_out, side_of in ((far_two, far_two_out, core_ref[0]), (cross_two, cross_two_out, 1 - core_ref[0])):
        start = pl.multiple_of(side_of * half, half)
        two[two.shape[0] - half :, :] = w_out_grad[pl.ds(start, half), :]
        go.send(two, two_out)
    go.finish()


def project_back_kernel(
    core_ref, modulation_ref, mod_two_ref, plain_in, query_in, plain_far_in, key_in, far_key_in, value_in, far_value_in,
    w_query_in, w_key_in, w_value_in,
    kept_out, sent_out, mod_grad_ref,
    plain, query, plain_far, key, far_key, value, far_value, w_query, w_key, w_value,
    weight_grad, packed, in_sems, out_sems,
):
    come, go = Mover(in_sems), Mover(out_sems)
    width = weight_grad.shape[2]
    half = width // 2
    own_half = pl.ds(pl.multiple_of(core_ref[0] * half, half), half)
    other_half = pl.ds(pl.multiple_of((1 - core_ref[0]) * half, half), half)
    groups = (
        ((plain_in, plain), (query_in, query), (w_query_in, w_query)),
        ((key_in, key), (plain_far_in, plain_far), (far_key_in, far_key), (w_key_in, w_key)),
        ((value_in, value), (far_value_in, far_value), (w_value_in, w_value)),
    )
    copies = [[come.start(source, target) for source, target in group] for group in groups]
    gain = (1.0 + modulation_ref[0:1, :]).T
    shift = modulation_ref[1:2, :].T
    scale, bias = 0.0, 0.0
    for kind, (own, far, weight) in enumerate(
        ((query, None, w_query), (key, far_key, w_key), (value, far_value, w_value))
    ):
        for copy in copies[kind]:
            copy.wait()
        grad = dot(plain[...], own[...], 0, 0)
        total = jnp.sum(own[...].astype(jnp.float32), axis=0, keepdims=True)
        if far is not None:
            grad += dot(plain_far[...], far[...], 0, 0)
            total += jnp.sum(far[...].astype(jnp.float32), axis=0, keepdims=True)
        matrix = weight[...].astype(jnp.float32)
        scale += jnp.sum(grad * matrix, axis=1, keepdims=True)
        bias += jnp.sum(matrix * total, axis=1, keepdims=True)
        weight_grad[kind] = (grad * gain + shift * total).astype(low_type)
        go.send(weight_grad.at[kind, own_half, :], kept_out.at[kind])
        go.send(weight_grad.at[kind, other_half, :], sent_out.at[kind * half : (kind + 1) * half, :])
    mod_grad_ref[0:1, :] = scale.T
    mod_grad_ref[1:2, :] = bias.T
    mod_grad_ref[2:4, :] = mod_two_ref[...]
    mod_grad = mod_grad_ref[...]
    high = mod_grad.astype(low_type).astype(jnp.float32)
    packed[...] = jnp.concatenate([high, mod_grad - high, jnp.zeros((8, high.shape[1]), jnp.float32)]).astype(low_type)
    go.send(packed, sent_out.at[3 * half : 3 * half + 16, :])
    go.finish()


def small(work, out_shapes, scalar_args, args, grant=16):
    def kernel(scalar_ref, *refs):
        for out_ref, value in zip(refs[len(args) :], work(scalar_ref, *refs[: len(args)])):
            out_ref[...] = value.astype(out_ref.dtype)

    return call(
        kernel, list(out_shapes), (scalar_args, *args), specs=[scalars] + [whole] * len(args), grant=grant, flops=2**29
    )


def half_of(ref, which):
    half = ref.shape[1] // 2
    return ref[:, pl.ds(pl.multiple_of(which * half, half), half), :].astype(jnp.float32)


def halves_of(side_of, *refs):
    return sum(half_of(ref, 1 - side_of) for ref in refs), sum(half_of(ref, side_of) for ref in refs)


def finish_kernel(
    states_ref, grad_middle_ref, query_ref, key_ref, value_ref, modulation_ref, send_ref, w_query_ref, w_key_ref, w_value_ref, *refs
):
    returned_refs, (grad_states_ref, returned, sems) = refs[:4], refs[4:]

    @pl.when(pl.program_id(0) == 0)
    def _():
        for copy in fetch(returned_refs, returned, sems):
            copy.wait()

    rows = states_ref.shape[0]
    sends = send_ref.shape[1]
    grad = sum(
        dot(own_ref[...], weight_ref[...], 1, 1)
        for own_ref, weight_ref in ((query_ref, w_query_ref), (key_ref, w_key_ref), (value_ref, w_value_ref))
    )
    for position in range(len(returned_refs)):
        chosen = chosen_rows(send_ref, position, rows, pl.program_id(0) * rows)
        grad += dot(chosen, returned[position * sends : (position + 1) * sends, :], 1, 0)
    plain, inverse = norm_parts(states_ref[...])
    grad_states_ref[...] = grad_middle_ref[...] + norm_back(grad * (1.0 + modulation_ref[0:1, :]), plain, inverse)


def finish(states, grad_middle, grads, modulation, send_list, weights, returned):
    rows, width = states.shape
    by_block = pl.BlockSpec((ROW_BLOCK, width), lambda i: (i, 0))
    once = [pl.BlockSpec(part.shape, lambda i: (0, 0)) for part in (modulation, send_list, *weights)]
    return pl.pallas_call(
        finish_kernel,
        grid=(rows // ROW_BLOCK,),
        in_specs=[by_block] * 5 + once + [anywhere] * len(returned),
        out_specs=by_block,
        out_shape=shaped((rows, width), jnp.float32),
        scratch_shapes=[
            pltpu.VMEM((sum(part.shape[0] for part in returned), width), low_type),
            pltpu.SemaphoreType.DMA((len(returned),)),
        ],
        compiler_params=pltpu.CompilerParams(vmem_limit_bytes=24 * 2**20),
        cost_estimate=pl.CostEstimate(flops=2**31, bytes_accessed=2**23, transcendentals=0),
    )(states, grad_middle, *grads, modulation, send_list, *weights, *returned)


def from_behind(block, axis, distance):
    devices = range(lax.axis_size(axis))
    route = [((i - distance) % len(devices), i) for i in devices]
    return lax.ppermute(block, axis, route)


def swap(block, mask):
    count = lax.axis_size("nodes") * lax.axis_size("hid")
    return lax.ppermute(block, everywhere, [(i, i ^ mask) for i in range(count)])


def place():
    return lax.axis_index("nodes") * lax.axis_size("hid") + lax.axis_index("hid")


def side(link):
    return (place() >> link) & 1


def added(parts):
    return sum(part.astype(jnp.float32) for part in parts).astype(low_type)


def pieces_of(block, count, index):
    size = block.shape[1] // count
    return lax.dynamic_slice_in_dim(block, index * size, size, 1)


def half_sum(block, link):
    return pieces_of(block, 2, side(link)) + swap(pieces_of(block, 2, 1 - side(link)), 1 << link)


def half_join(block, link):
    other = swap(block, 1 << link)
    return jnp.where(
        side(link) == 0, jnp.concatenate([block, other], axis=1), jnp.concatenate([other, block], axis=1)
    )


def whole_sum(block, link):
    return block + swap(block, 1 << link)


def pack_wide(values):
    high = lax.reduce_precision(values, 8, 7)
    both = jnp.concatenate([high, values - high]).astype(low_type)
    return jnp.concatenate([both, jnp.zeros((16 - both.shape[0], both.shape[1]), low_type)])


def unpack_wide(packed, count):
    packed = packed.astype(jnp.float32)
    return packed[:count] + packed[count : 2 * count]


def group_sum(block, wide, links):
    count = 1 << len(links)
    here = sum(side(link) << i for i, link in enumerate(links))
    total = pieces_of(block, count, here).astype(jnp.float32)
    shape = total.shape
    packed = pack_wide(wide)
    for mask in range(1, count):
        sent = pieces_of(block, count, here ^ mask).reshape(-1, shape[-1])
        come = swap(jnp.concatenate([sent, packed]), sum(((mask >> i) & 1) << link for i, link in enumerate(links)))
        total = total + come[: -packed.shape[0]].reshape(shape).astype(jnp.float32)
        wide = wide + unpack_wide(come[-packed.shape[0] :], wide.shape[0])
    return total.astype(low_type), wide


def group_join(block, links):
    found = [block]
    for mask in range(1, 1 << len(links)):
        found.append(swap(block, sum(((mask >> i) & 1) << link for i, link in enumerate(links))))
    for i, link in enumerate(links):
        turned = [found[k ^ (1 << i)] for k in range(len(found))]
        found = [jnp.where(side(link) == 0, kept, other) for kept, other in zip(found, turned)]
    return jnp.concatenate(found, axis=1)


def after(values, previous):
    return lax.optimization_barrier((values, previous))


def body(
    states,
    condition,
    mod_w,
    w_query,
    w_key,
    w_value,
    w_out,
    w_gate,
    w_up,
    w_down,
    counts,
    send_rows,
    neighbours,
    cotangent,
):
    rows, width = states.shape
    sends = send_rows.shape[2]
    ext = rows + len(halo_steps) * sends
    f32 = jnp.float32
    parcel = shaped((sends, width))
    send_list = send_rows[0]

    links = (lax.axis_size("nodes") * lax.axis_size("hid")).bit_length() - 1
    core, across, *around = range(links)

    normed, plain, modulation, *parcels = prepare(states, condition, mod_w, send_list)
    landed = [from_behind(part, everywhere, hop) for part, hop in zip(parcels, halo_steps)]
    shard, normed = after((w_gate, w_up, w_down), normed)
    near_half = side(around[0])
    middle_row = shard[1].shape[0] // 2
    far_half = jnp.where(
        near_half == 0,
        jnp.concatenate([shard[0], shard[1][:middle_row]]),
        jnp.concatenate([shard[1][middle_row:], shard[2]]),
    )
    far_half = swap(far_half, 1 << across)

    queries, own_keys, own_values, *own_raised, top, total, mixed, packed = attend_own(
        normed, neighbours.T, w_query, w_key, w_value, ext - rows
    )
    queries, far_half, landed, shard = lax.optimization_barrier((queries, far_half, landed, shard))
    core_shard = [swap(weight, 1 << core) for weight in shard]
    far_rest = swap(far_half, 1 << around[0])
    cross_half = swap(far_half, 1 << core)
    *far_raised, attended, spread_own, spread_far, far_keys, far_values, plain_far = attend_far(
        modulation, queries, w_key, w_value, packed, top, total, mixed, landed
    )

    low_rows = shaped((rows, width))
    wide_rows = shaped((rows, width), f32)
    shard_rows = sum(weight.size for weight in shard) // width
    all_units = shaped((shard_rows, width))
    half_grad = shaped((shard_rows // 2, width))
    joint_grad = shaped((shard_rows // 2 + width // 2, width))

    def room(*shapes):
        return [pltpu.VMEM(one.shape, one.dtype) for one in shapes]

    middle, second, branch, out, grad, core_one, core_two, own_one, own_two = call(
        feed_first_kernel,
        [wide_rows, low_rows, low_rows, wide_rows, wide_rows] + [half_grad] * 4,
        (counts, modulation, states, cotangent, attended, w_out, *core_shard, *shard),
        grant=56,
        specs=[scalars, whole] + [anywhere] * 10,
        out_specs=[anywhere] * 9,
        scratch=room(wide_rows, wide_rows, low_rows, w_out, all_units, all_units, low_rows, low_rows)
        + room(wide_rows, wide_rows)
        + room(*[half_grad] * 4, *[low_rows] * 3)
        + [pltpu.SemaphoreType.DMA((13,)), pltpu.SemaphoreType.DMA((9,))],
        flops=2**34,
        moved=2**24,
    )
    core_index = jnp.stack([lax.axis_index("hid") & 1, near_half])
    (cross_half, far_rest), grad = after((cross_half, far_rest), grad)
    cross_rest = swap(far_rest, 1 << core)
    fold = (-1, width // 2, width)

    def over_cores(*grads):
        return [[kept.reshape(fold), swap(sent, 1 << core).reshape(fold)] for kept, sent in grads]

    first, second_link, *rest = around
    sides = jnp.stack([side(first), side(second_link)])

    def lines(blocks, count):
        return shaped((blocks, count, width))

    def first_halves(side_ref, one, one_come, two, two_come):
        return *halves_of(side_ref[0], one, one_come), *halves_of(side_ref[1], two, two_come)

    own_sums = over_cores((own_one, core_one), (own_two, core_two))
    kept = own_sums[0][0].shape[0]
    eighth = fold[1] // 2
    quarter = eighth // 2
    one_sent, one_own, two_sent, two_own = small(
        first_halves, [lines(kept, eighth)] * 4, sides, (*own_sums[0], *own_sums[1])
    )
    (one_sent, two_sent), cross_rest = after((one_sent, two_sent), cross_rest)
    own_come = swap(one_sent, 1 << first), swap(two_sent, 1 << second_link)
    output, grad_middle, grad_own, grad_far, mod_two, cross_one, cross_two, far_one, far_two = call(
        feed_last_kernel,
        [wide_rows, wide_rows, low_rows, low_rows, shaped((2, width), f32)] + [half_grad, joint_grad] * 2,
        (counts, core_index, modulation, cotangent, attended, w_out, spread_own, spread_far)
        + (middle, second, branch, out, grad, cross_half, cross_rest, far_half, far_rest),
        grant=56,
        specs=[scalars, scalars, whole] + [anywhere] * 14,
        out_specs=[anywhere] * 4 + [whole] + [anywhere] * 4,
        scratch=room(wide_rows, low_rows, w_out, wide_rows, wide_rows, wide_rows, low_rows, low_rows)
        + room(wide_rows, wide_rows, all_units, all_units, low_rows, low_rows)
        + room(half_grad, joint_grad, half_grad, joint_grad)
        + room(w_out, *[low_rows] * 3)
        + [pltpu.SemaphoreType.DMA((14,)), pltpu.SemaphoreType.DMA((12,))],
        flops=2**34,
        moved=2**24,
    )

    (cross_one, cross_two), own_come = after((cross_one, cross_two), own_come)
    far_sums = over_cores((far_one, cross_one), (far_two, cross_two))
    one_sent, one_far, two_sent, two_far = small(
        first_halves,
        [lines(kept, eighth)] * 2 + [lines(kept + 1, eighth)] * 2,
        sides,
        (*far_sums[0], *far_sums[1]),
    )
    grad_far, (one_sent, two_sent) = after(grad_far, (one_sent, two_sent))
    far_come = swap(one_sent, 1 << first), swap(two_sent, 1 << second_link)
    partial, *far_pieces = attend_back(
        queries, attended, far_keys, far_values, grad_far, far_raised, returns=(w_key, w_value)
    )
    far_pieces, parcels = far_pieces[:2], far_pieces[2:]
    far_come, (grad_own, partial) = after(far_come, (grad_own, partial))

    def second_halves(side_ref, one_own, one_own_come, one_far, one_far_come, two_own, two_own_come, two_far, two_far_come):
        own_sent, own_kept = halves_of(side_ref[1], one_own, one_own_come)
        far_sent, far_kept = halves_of(side_ref[1], one_far, one_far_come)
        two_kept = two_own[...].astype(f32) + two_own_come[...].astype(f32)
        two_sent = two_far[...].astype(f32) + two_far_come[...].astype(f32)
        return jnp.concatenate([own_sent, far_sent]), own_kept, far_kept, two_kept, two_sent

    one_sent, one_own, one_far, two_own, two_sent = small(
        second_halves,
        [lines(2 * kept, quarter), lines(kept, quarter), lines(kept, quarter), lines(kept, eighth), lines(kept + 1, eighth)],
        sides,
        (one_own, own_come[0], one_far, far_come[0], two_own, own_come[1], two_far, far_come[1]),
    )
    (one_sent, two_sent), grad_own = after((one_sent, two_sent), grad_own)
    one_come, two_come = swap(one_sent, 1 << second_link), swap(two_sent, 1 << across)
    pieces = attend_back(queries, attended, own_keys, own_values, grad_own, own_raised, partial)
    (one_come, two_come), pieces = after((one_come, two_come), pieces)

    def third_halves(side_ref, one_own, one_far, one_come, two_own, two_last, two_come):
        one_kept = one_own[...].astype(f32) + one_come[:kept].astype(f32)
        one_sent = one_far[...].astype(f32) + one_come[kept:].astype(f32)
        here = side_ref[0]
        own_sent, own_kept = halves_of(here, two_own, two_come.at[:kept])
        last_sent, last_kept = halves_of(here, two_last.at[kept:], two_come.at[kept:])
        return one_sent, one_kept, jnp.concatenate([own_sent, last_sent]), jnp.concatenate([own_kept, last_kept])

    one_sent, one_kept, two_sent, two_kept = small(
        third_halves,
        [lines(kept, quarter)] * 2 + [lines(kept + 1, quarter)] * 2,
        sides,
        (one_own, one_far, one_come, two_own, two_sent, two_come),
    )
    (one_sent, two_sent), pieces = after((one_sent, two_sent), pieces)
    one_come, two_come = swap(one_sent, 1 << across), swap(two_sent, 1 << first)
    returned = [from_behind(part, everywhere, -hop) for part, hop in zip(parcels[:3], halo_steps)]
    far_low = shaped((ext - rows, width))
    attn_kept, attn_sent, mod_grad = call(
        project_back_kernel,
        [shaped((3, width // 2, width)), shaped((3 * width // 2 + 16, width)), shaped((4, width), f32)],
        (core_index, modulation, mod_two, plain, pieces[0], plain_far, pieces[1], far_pieces[0], pieces[2], far_pieces[1])
        + (w_query, w_key, w_value),
        specs=[scalars, whole, whole] + [anywhere] * 10,
        out_specs=[anywhere, anywhere, whole],
        scratch=room(low_rows, low_rows, far_low, low_rows, far_low, low_rows, far_low, w_query, w_key, w_value)
        + room(shaped((3, width, width)), shaped((16, width)))
        + [pltpu.SemaphoreType.DMA((10,)), pltpu.SemaphoreType.DMA((7,))],
        flops=2**32,
        moved=2**23,
    )

    def on_both(step, link):
        def run(one, two):
            both = step(jnp.concatenate([one, two]), link)
            return both[:kept], both[kept:]

        return run

    shard_steps = [on_both(whole_sum, link) for link in rest]
    shard_steps.append(lambda one, two: (half_join(one, second_link), half_join(two, first)))
    shard_steps.append(lambda one, two: (half_join(one, first), half_join(two, second_link)))

    groups = [[across, first]] + [around[i : i + 2] for i in range(1, len(around), 2)]
    def over_attn_cores(kept, wide):
        come = swap(attn_sent, 1 << core)
        total = kept.astype(f32) + come[:-16].reshape(kept.shape).astype(f32)
        return total.astype(low_type), wide + unpack_wide(come[-16:], wide.shape[0])

    attn_steps = [over_attn_cores] + [functools.partial(group_sum, links=group) for group in groups]
    attn_steps += [lambda grad, wide, group=group: (group_join(grad, group), wide) for group in reversed(groups)]

    returned, (one_come, two_come), parcels, attn_sent = lax.optimization_barrier(
        (returned, (one_come, two_come), parcels, attn_sent)
    )
    returned.append(from_behind(parcels[3], everywhere, -halo_steps[3]))
    shard_state = added([one_kept, one_come]), added([two_kept, two_come])
    attn_state = attn_kept, mod_grad
    shard_turns = [[]] + [[step] for step in shard_steps]
    for index in range(max(len(shard_turns), len(attn_steps))):
        for step in shard_turns[index] if index < len(shard_turns) else []:
            shard_state = step(*shard_state)
        if index < len(attn_steps):
            attn_state = attn_steps[index](*attn_state)
        if index == 1:
            returned, attn_state = after(returned, attn_state)
        if index == 2:
            grad_states = finish(
                states, grad_middle, pieces, modulation, send_list, (w_query, w_key, w_value), returned
            )
            grad_states, attn_state = after(grad_states, attn_state)
        if index in (1, 2):
            shard_state, attn_state = after(shard_state, attn_state)
    (one, two), (attn_grad, mod_grad) = shard_state, attn_state
    shard_grad = jnp.concatenate([one, two[:kept]]).reshape(-1, width).astype(f32)
    grad_w_gate, grad_w_up, grad_w_down = jnp.split(shard_grad, 3)
    grad_w_query, grad_w_key, grad_w_value = half_join(attn_grad, core).astype(f32)
    grad_w_out = half_join(two[kept:], core)[0].astype(f32)
    mod_grad = mod_grad.reshape(-1)
    grad_mod_w = condition[:, None] * mod_grad[None, :]
    grad_condition = jnp.sum(mod_w.astype(f32) * mod_grad[None, :], axis=1)
    return (
        output,
        grad_states,
        grad_condition,
        grad_mod_w,
        grad_w_query,
        grad_w_key,
        grad_w_value,
        grad_w_out,
        grad_w_gate,
        grad_w_up,
        grad_w_down,
    )


def solution(mesh):
    rows = P(everywhere, None)
    placed = (
        rows,
        P(),
        P(),
        P(),
        P(),
        P(),
        P(),
        P(None, "hid"),
        P(None, "hid"),
        P("hid", None),
        P(everywhere),
        P(everywhere, None, None),
        rows,
        rows,
    )
    return jax.shard_map(
        body,
        mesh=mesh,
        in_specs=placed,
        out_specs=(rows, rows, P(), P(), P(), P(), P(), P(), P(None, "hid"), P(None, "hid"), P("hid", None)),
        check_vma=False,
    )
```

```python
import functools

import jax
import jax.numpy as jnp
from jax import lax
from jax.experimental import pallas as pl
from jax.experimental.pallas import tpu as pltpu
from jax.sharding import PartitionSpec as P

HEADS = 4
HEAD_DIM = 128
NEIGH = 16
BLOCK = 1024
ROW_BLOCK = 256
BACK_GRANT = 56
RAISED_PARTS = 1

epsilon = 1e-06
halo_steps = (1, -1, 2, -2)
highest = lax.Precision.HIGHEST
score_scale = HEAD_DIM ** (-0.5)
LOG2_E = 1.4426950408889634
low_type = jnp.bfloat16
everywhere = ("nodes", "hid")
whole = pl.BlockSpec(memory_space=pltpu.VMEM)
scalars = pl.BlockSpec(memory_space=pltpu.SMEM)
anywhere = pl.BlockSpec(memory_space=pl.ANY)


def dot(left, right, left_dim, right_dim):
    return lax.dot_general(
        left, right, (((left_dim,), (right_dim,)), ((), ())), preferred_element_type=jnp.float32
    )


def shaped(shape, dtype=low_type):
    return jax.ShapeDtypeStruct(shape, dtype)


def norm_parts(states):
    centred = states - jnp.mean(states, axis=-1, keepdims=True)
    inverse = lax.rsqrt(jnp.mean(centred * centred, axis=-1, keepdims=True) + epsilon)
    return (centred * inverse, inverse)


def norm_back(grad_plain, plain, inverse):
    first_mean = jnp.mean(grad_plain, axis=-1, keepdims=True)
    second_mean = jnp.mean(grad_plain * plain, axis=-1, keepdims=True)
    return inverse * (grad_plain - first_mean - plain * second_mean)


def call(kernel, out_shape, args, specs=None, out_specs=None, scratch=(), flops=0, moved=0, grant=60):
    single = not isinstance(out_shape, list)
    return pl.pallas_call(
        kernel,
        in_specs=specs or [whole] * len(args),
        out_specs=out_specs or (whole if single else [whole] * len(out_shape)),
        out_shape=out_shape,
        scratch_shapes=list(scratch),
        compiler_params=pltpu.CompilerParams(vmem_limit_bytes=grant * 2**20),
        cost_estimate=pl.CostEstimate(flops=flops, bytes_accessed=moved, transcendentals=0),
    )(*args)


def chosen_rows(send_ref, position, rows, first=0):
    sends = send_ref.shape[1]
    place = lax.broadcasted_iota(jnp.int32, (rows, sends), 0) + first
    return jnp.where(place == send_ref[position : position + 1, :], 1.0, 0.0).astype(low_type)


def prepare_kernel(
    states_ref, condition_ref, mod_w_ref, send_ref, normed_ref, plain_ref, modulation_ref, *refs
):
    *parcel_refs, plain = refs
    step, (block, width) = pl.program_id(0), states_ref.shape

    @pl.when(step == 0)
    def _():
        mixed = sum(
            condition_ref[i] * mod_w_ref[i : i + 1, :].astype(jnp.float32) for i in range(condition_ref.shape[0])
        )
        for piece in range(4):
            modulation_ref[piece : piece + 1, :] = mixed[:, piece * width : (piece + 1) * width]

    values, _ = norm_parts(states_ref[...])
    plain_ref[...] = values.astype(low_type)
    plain[pl.ds(pl.multiple_of(step * block, block), block), :] = plain_ref[...]
    normed_ref[...] = (values * (1.0 + modulation_ref[0:1, :]) + modulation_ref[1:2, :]).astype(low_type)

    @pl.when(step == pl.num_programs(0) - 1)
    def _():
        for position, parcel_ref in enumerate(parcel_refs):
            chosen = chosen_rows(send_ref, position, plain.shape[0])
            parcel_ref[...] = dot(chosen, plain[...], 0, 0).astype(low_type)


def prepare(states, condition, mod_w, send_list):
    rows, width = states.shape
    by_block = pl.BlockSpec((2 * ROW_BLOCK, width), lambda i: (i, 0))

    def once(*shape):
        return pl.BlockSpec(shape, lambda i: (0,) * len(shape))

    count, sends = send_list.shape
    return pl.pallas_call(
        prepare_kernel,
        grid=(rows // ROW_BLOCK // 2,),
        in_specs=[by_block, scalars, once(*mod_w.shape), once(*send_list.shape)],
        out_specs=[by_block, by_block, once(4, width)] + [once(sends, width)] * count,
        out_shape=[shaped((rows, width)), shaped((rows, width)), shaped((4, width), jnp.float32)]
        + [shaped((sends, width))] * count,
        scratch_shapes=[pltpu.VMEM((rows, width), low_type)],
        compiler_params=pltpu.CompilerParams(vmem_limit_bytes=60 * 2**20),
        cost_estimate=pl.CostEstimate(flops=2**30, bytes_accessed=2**22, transcendentals=0),
    )(states, condition, mod_w, send_list)


def count_near(near_ref, cols, groups):
    half = groups // 2
    near = near_ref[:, cols]
    group = near >> 7
    upper = group >= half
    unit = jnp.left_shift(1, 5 * jnp.where(upper, group - half, group))
    low = near & 127
    low_unit = jnp.where(upper, 0, unit)
    high_unit = jnp.where(upper, unit, 0)
    place = lax.broadcasted_iota(jnp.int32, (128, 128), 0)
    low_count = jnp.zeros((128, 128), jnp.int32)
    high_count = low_count
    for n in range(NEIGH):
        same = low[n : n + 1] == place
        low_count = low_count + jnp.where(same, low_unit[n : n + 1], 0)
        high_count = high_count + jnp.where(same, high_unit[n : n + 1], 0)
    return low_count, high_count


def count_bias(packed, position):
    count = (packed >> (5 * position)) & 31
    return jnp.where(count > 0, jnp.log2(count.astype(jnp.float32)), -1e30)


def score_pass(key_ref, query, bias, scores, cols, top):
    width = scores.shape[1]
    for g in range(scores.shape[0] // 128):
        part = slice(g * 128, (g + 1) * 128)
        score = dot(key_ref[part, :], query, 1, 1) * (score_scale * LOG2_E) + bias[part, cols]
        scores[part, :] = score
        top = jnp.maximum(top, jnp.max(score.reshape(16, 8, width), axis=0))
    return jnp.max(top, axis=0, keepdims=True)


def raise_pass(scores, top, raised_refs, cols):
    width = scores.shape[1]
    size = raised_refs[0].shape[1]
    total = jnp.zeros((8, width), jnp.float32)
    for g in range(scores.shape[0] // 128):
        part = slice(g * 128, (g + 1) * 128)
        raised = jnp.exp2(scores[part, :] - top)
        total = total + jnp.sum(raised.reshape(16, 8, width), axis=0)
        lower = g * 128 % size
        raised_refs[g * 128 // size][0, lower : lower + 128, cols] = raised.astype(low_type)
    return jnp.sum(total, axis=0, keepdims=True)


def mix(value_t, raised_refs, cols):
    size = raised_refs[0].shape[1]
    return sum(
        dot(value_t[:, i * size : (i + 1) * size], raised_ref[0, :, cols], 1, 0)
        for i, raised_ref in enumerate(raised_refs)
    )


def raised_parts(count, rows):
    size = count // RAISED_PARTS
    return (
        [pl.BlockSpec((1, size, rows), lambda h: (h, 0, 0))] * RAISED_PARTS,
        [shaped((HEADS, size, rows))] * RAISED_PARTS,
    )


def attend_own_kernel(
    groups, normed_ref, near_ref, w_query_ref, w_key_ref, w_value_ref,
    query_ref, key_ref, value_ref, *refs,
):
    raised_refs, refs = refs[:RAISED_PARTS], refs[RAISED_PARTS:]
    top_ref, total_ref, mixed_ref, packed_ref, bias, scores, value_t = refs
    rows = normed_ref.shape[0]
    half = groups // 2

    @pl.when(pl.program_id(0) == 0)
    def _():
        @pl.loop(0, rows // 128)
        def _(step):
            cols = pl.ds(pl.multiple_of(step * 128, 128), 128)
            packed = count_near(near_ref, cols, groups)
            packed_ref[:, cols] = packed[1]
            for g in range(rows // 128):
                bias[g * 128 : (g + 1) * 128, cols] = count_bias(packed[g // half], g % half)

    for weight_ref, out_ref in ((w_query_ref, query_ref), (w_key_ref, key_ref), (w_value_ref, value_ref)):
        out_ref[...] = dot(normed_ref[...], weight_ref[...], 1, 0).astype(low_type)
    value_t[...] = value_ref[...].T
    width = scores.shape[1]

    @pl.loop(0, rows // width)
    def _(step):
        cols = pl.ds(pl.multiple_of(step * width, width), width)
        least = jnp.full((8, width), -jnp.inf, jnp.float32)
        top = score_pass(key_ref, query_ref[cols, :], bias, scores, cols, least)
        top_ref[0, :, cols] = top
        total_ref[0, :, cols] = raise_pass(scores, top, raised_refs, cols)
        mixed_ref[0, :, cols] = mix(value_t, raised_refs, cols)


def attend_own(normed, near, w_query, w_key, w_value, far_rows):
    rows, width = normed.shape
    groups = (rows + far_rows) // 128
    by_row = pl.BlockSpec((rows, HEAD_DIM), lambda h: (0, h))
    by_weight = pl.BlockSpec((width, HEAD_DIM), lambda h: (0, h))
    by_head = pl.BlockSpec((1, 1, rows), lambda h: (h, 0, 0))
    return pl.pallas_call(
        functools.partial(attend_own_kernel, groups),
        grid=(HEADS,),
        in_specs=[pl.BlockSpec((rows, width), lambda h: (0, 0)), pl.BlockSpec((NEIGH, rows), lambda h: (0, 0))]
        + [by_weight] * 3,
        out_specs=[
            by_row,
            by_row,
            by_row,
            *raised_parts(rows, rows)[0],
            by_head,
            by_head,
            pl.BlockSpec((1, HEAD_DIM, rows), lambda h: (h, 0, 0)),
            pl.BlockSpec((128, rows), lambda h: (0, 0)),
        ],
        out_shape=[shaped((rows, width))] * 3
        + [
            *raised_parts(rows, rows)[1],
            shaped((HEADS, 1, rows), jnp.float32),
            shaped((HEADS, 1, rows), jnp.float32),
            shaped((HEADS, HEAD_DIM, rows), jnp.float32),
            shaped((128, rows), jnp.int32),
        ],
        scratch_shapes=[
            pltpu.VMEM((rows, rows), jnp.float32),
            pltpu.VMEM((rows, BLOCK), jnp.float32),
            pltpu.VMEM((HEAD_DIM, rows), low_type),
        ],
        compiler_params=pltpu.CompilerParams(vmem_limit_bytes=56 * 2**20),
        cost_estimate=pl.CostEstimate(flops=2**34, bytes_accessed=2**24, transcendentals=0),
    )(normed, near, w_query, w_key, w_value)


def fetch(parts, to_ref, sems):
    copies, lower = [], 0
    for position, part in enumerate(parts):
        upper = lower + part.shape[0]
        copies.append(pltpu.make_async_copy(part, to_ref.at[lower:upper, :], sems.at[position]))
        copies[-1].start()
        lower = upper
    return copies


def attend_far_kernel(
    skip, modulation_ref, query_ref, w_key_ref, w_value_ref, packed_ref, top_ref, total_ref, mixed_ref, *refs
):
    landed_refs, refs = refs[:4], refs[4:]
    raised_refs, refs = refs[:RAISED_PARTS], refs[RAISED_PARTS:]
    attended_ref, spread_own_ref, spread_far_ref, key_ref, value_ref, plain_ref, *refs = refs
    bias, scores, value_t, normed_ref, sems = refs
    far, rows = bias.shape

    @pl.when(pl.program_id(0) == 0)
    def _():
        copies = fetch(landed_refs, plain_ref, sems)

        @pl.loop(0, rows // 128)
        def _(step):
            cols = pl.ds(pl.multiple_of(step * 128, 128), 128)
            for g in range(far // 128):
                bias[g * 128 : (g + 1) * 128, cols] = count_bias(packed_ref[:, cols], g + skip)

        for copy in copies:
            copy.wait()
        plain = plain_ref[...].astype(jnp.float32)
        normed_ref[...] = (plain * (1.0 + modulation_ref[0:1, :]) + modulation_ref[1:2, :]).astype(low_type)

    key_ref[...] = dot(normed_ref[...], w_key_ref[...], 1, 0).astype(low_type)
    value_ref[...] = dot(normed_ref[...], w_value_ref[...], 1, 0).astype(low_type)
    value_t[...] = value_ref[...].T
    width = scores.shape[1]

    @pl.loop(0, rows // width)
    def _(step):
        cols = pl.ds(pl.multiple_of(step * width, width), width)
        own_top = top_ref[0, :, cols]
        least = jnp.broadcast_to(own_top, (8, width))
        top = score_pass(key_ref, query_ref[cols, :], bias, scores, cols, least)
        factor = jnp.exp2(own_top - top)
        total = raise_pass(scores, top, raised_refs, cols) + total_ref[0, :, cols] * factor
        inverse = 1.0 / total
        own_inverse = inverse * factor
        spread_far_ref[cols, :] = jnp.broadcast_to(inverse, (HEAD_DIM, width)).T
        spread_own_ref[cols, :] = jnp.broadcast_to(own_inverse, (HEAD_DIM, width)).T
        mixed = mix(value_t, raised_refs, cols) * inverse + mixed_ref[0, :, cols] * own_inverse
        attended_ref[cols, :] = mixed.T.astype(low_type)


def attend_far(modulation, queries, w_key, w_value, packed, top, total, mixed, landed):
    rows, width = queries.shape
    far = sum(part.shape[0] for part in landed)
    by_row = pl.BlockSpec((rows, HEAD_DIM), lambda h: (0, h))
    by_far = pl.BlockSpec((far, HEAD_DIM), lambda h: (0, h))
    by_weight = pl.BlockSpec((width, HEAD_DIM), lambda h: (0, h))
    by_head = pl.BlockSpec((1, 1, rows), lambda h: (h, 0, 0))
    groups = (rows + far) // 128
    return pl.pallas_call(
        functools.partial(attend_far_kernel, rows // 128 - groups // 2),
        grid=(HEADS,),
        in_specs=[
            pl.BlockSpec(modulation.shape, lambda h: (0, 0)),
            by_row,
            by_weight,
            by_weight,
            pl.BlockSpec(packed.shape, lambda h: (0, 0)),
            by_head,
            by_head,
            pl.BlockSpec((1, HEAD_DIM, rows), lambda h: (h, 0, 0)),
        ]
        + [anywhere] * len(landed),
        out_specs=[*raised_parts(far, rows)[0], by_row, by_row, by_row, by_far, by_far]
        + [pl.BlockSpec((far, width), lambda h: (0, 0))],
        out_shape=[
            *raised_parts(far, rows)[1],
            shaped((rows, width)),
            shaped((rows, width), jnp.float32),
            shaped((rows, width), jnp.float32),
            shaped((far, width)),
            shaped((far, width)),
            shaped((far, width)),
        ],
        scratch_shapes=[
            pltpu.VMEM((far, rows), jnp.float32),
            pltpu.VMEM((far, BLOCK), jnp.float32),
            pltpu.VMEM((HEAD_DIM, far), low_type),
            pltpu.VMEM((far, width), low_type),
            pltpu.SemaphoreType.DMA((len(landed),)),
        ],
        compiler_params=pltpu.CompilerParams(vmem_limit_bytes=56 * 2**20),
        cost_estimate=pl.CostEstimate(flops=2**33, bytes_accessed=2**23, transcendentals=0),
    )(modulation, queries, w_key, w_value, packed, top, total, mixed, *landed)


def attend_back_kernel(has_partial, query_ref, attended_ref, key_ref, value_ref, grad_ref, *refs):
    raised_refs, refs = refs[:RAISED_PARTS], refs[RAISED_PARTS:]
    size = raised_refs[0].shape[1]
    if has_partial:
        partial_ref, *refs = refs
    else:
        w_key_ref, w_value_ref, *refs = refs
    grad_query_ref, grad_key_ref, grad_value_ref, *refs = refs
    if not has_partial:
        *parcel_refs, low, key_t, grad_normed = refs
    else:
        low, key_t = refs
    rows = query_ref.shape[0]
    key_t[...] = key_ref[...].T

    @pl.loop(0, rows // BLOCK)
    def _(step):
        cols = pl.ds(pl.multiple_of(step * BLOCK, BLOCK), BLOCK)
        attended = attended_ref[cols, :].astype(jnp.float32)
        grad = grad_ref[cols, :]
        mean = jnp.sum((grad.astype(jnp.float32) * attended).T, axis=0, keepdims=True)
        for g in range(value_ref.shape[0] // 128):
            part = slice(g * 128, (g + 1) * 128)
            term = dot(value_ref[part, :], grad, 1, 1) - mean
            lower = g * 128 % size
            raised = raised_refs[g * 128 // size][0, lower : lower + 128, cols]
            low[part, cols] = (term * raised.astype(jnp.float32)).astype(low_type)
        total = dot(key_t[...], low[:, cols], 1, 0)
        if has_partial:
            total = (total + partial_ref[0, :, cols]) * score_scale
            grad_query_ref[cols, :] = total.T.astype(low_type)
        else:
            grad_query_ref[0, :, cols] = total

    for i, raised_ref in enumerate(raised_refs):
        grad_value_ref[i * size : (i + 1) * size, :] = dot(raised_ref[0], grad_ref[...], 1, 0).astype(low_type)
    grad_key_ref[...] = (dot(low[...], query_ref[...], 1, 0) * score_scale).astype(low_type)
    if has_partial:
        return

    back = dot(grad_key_ref[...], w_key_ref[...], 1, 1) + dot(grad_value_ref[...], w_value_ref[...], 1, 1)

    @pl.when(pl.program_id(0) == 0)
    def _():
        grad_normed[...] = back

    @pl.when(pl.program_id(0) > 0)
    def _():
        grad_normed[...] += back

    @pl.when(pl.program_id(0) == HEADS - 1)
    def _():
        grad = grad_normed[...]
        for position, parcel_ref in enumerate(parcel_refs):
            sends = parcel_ref.shape[0]
            parcel_ref[...] = grad[position * sends : (position + 1) * sends, :].astype(low_type)


def attend_back(queries, attended, keys, values, grads, raised, partial=None, returns=None):
    rows, width = queries.shape
    count = keys.shape[0]
    by_row = pl.BlockSpec((rows, HEAD_DIM), lambda h: (0, h))
    by_count = pl.BlockSpec((count, HEAD_DIM), lambda h: (0, h))
    by_head = pl.BlockSpec((1, HEAD_DIM, rows), lambda h: (h, 0, 0))
    in_specs = [by_row, by_row, by_count, by_count, by_row, *raised_parts(count, rows)[0]]
    out_specs = [by_row if returns is None else by_head, by_count, by_count]
    out_shape = [
        shaped((rows, width)) if returns is None else shaped((HEADS, HEAD_DIM, rows), jnp.float32),
        shaped((count, width)),
        shaped((count, width)),
    ]
    scratch = [pltpu.VMEM((count, rows), low_type), pltpu.VMEM((HEAD_DIM, count), low_type)]
    if returns is None:
        in_specs.append(by_head)
    else:
        by_weight = pl.BlockSpec((width, HEAD_DIM), lambda h: (0, h))
        in_specs += [by_weight, by_weight]
        sends = count // len(halo_steps)
        out_specs += [pl.BlockSpec((sends, width), lambda h: (0, 0))] * len(halo_steps)
        out_shape += [shaped((sends, width))] * len(halo_steps)
        scratch.append(pltpu.VMEM((count, width), jnp.float32))
    return pl.pallas_call(
        functools.partial(attend_back_kernel, returns is None),
        grid=(HEADS,),
        in_specs=in_specs,
        out_specs=out_specs,
        out_shape=out_shape,
        scratch_shapes=scratch,
        compiler_params=pltpu.CompilerParams(vmem_limit_bytes=BACK_GRANT * 2**20),
        cost_estimate=pl.CostEstimate(flops=count * 2**22, bytes_accessed=2**22, transcendentals=0),
    )(queries, attended, keys, values, grads, *raised, *([partial] if returns is None else returns))


def live_rows(count_ref, start, rows):
    place = lax.broadcasted_iota(jnp.int32, (rows, 1), 0) + start
    return (place < count_ref[0]).astype(jnp.float32)


class Mover:
    def __init__(self, sems):
        self.sems, self.used, self.open = sems, 0, []

    def start(self, source, target):
        copy = pltpu.make_async_copy(source, target, self.sems.at[self.used])
        self.used += 1
        copy.start()
        return copy

    def send(self, source, target):
        self.open.append(self.start(source, target))

    def finish(self):
        for copy in self.open:
            copy.wait()


def feed_chunk(weight_ref, second_ref, branch_ref, out_ref, grad_ref, hidden, grad_gate, grad_up, store, fresh, done, ready=None):
    units = weight_ref.shape[0] // 3
    gate_rows, up_rows, down_rows = (slice(i * units, (i + 1) * units) for i in range(3))
    for step in range(second_ref.shape[0] // ROW_BLOCK):
        rows = slice(step * ROW_BLOCK, (step + 1) * ROW_BLOCK)
        second = second_ref[rows, :]
        gate = dot(second, weight_ref[gate_rows, :], 1, 0)
        up = dot(second, weight_ref[up_rows, :], 1, 0)
        sigmoid = 1.0 / (1.0 + jnp.exp(-gate))
        activated = gate * sigmoid
        hidden[rows, :] = (activated * up).astype(low_type)
        back = dot(branch_ref[rows, :], weight_ref[down_rows, :], 1, 1)
        grad_gate[rows, :] = (back * up * (sigmoid + activated * (1.0 - sigmoid))).astype(low_type)
        grad_up[rows, :] = (back * activated).astype(low_type)
        out = dot(hidden[rows, :], weight_ref[down_rows, :], 1, 0)
        grad = dot(grad_gate[rows, :], weight_ref[gate_rows, :], 1, 1) + dot(
            grad_up[rows, :], weight_ref[up_rows, :], 1, 1
        )
        if step == 0 and ready is not None:
            ready()
        if fresh:
            out_ref[rows, :] = out
            grad_ref[rows, :] = grad
        else:
            out_ref[rows, :] += out
            grad_ref[rows, :] += grad
        if done is not None:
            done(rows)

    one, two = store
    half = units // 2
    one[:units, :] = dot(second_ref[...], grad_gate[...], 0, 0).astype(low_type)
    grad_up_weight = dot(second_ref[...], grad_up[...], 0, 0).astype(low_type)
    one[units:, :] = grad_up_weight[:half, :]
    two[:half, :] = grad_up_weight[half:, :]
    two[half : half + units, :] = dot(hidden[...], branch_ref[...], 0, 0).astype(low_type)


def feed_first_kernel(
    count_ref, modulation_ref, states_in, cotangent_in, attended_in, w_out_in,
    core_gate_in, core_up_in, core_down_in, own_gate_in, own_up_in, own_down_in,
    middle_out, second_out, branch_out, out_out, grad_out, core_one_out, core_two_out, own_one_out, own_two_out,
    states, cotangent, attended, w_out, core, own, second, branch, out, grad,
    core_one, core_two, own_one, own_two, hidden, grad_gate, grad_up, in_sems, out_sems,
):
    come, go = Mover(in_sems), Mover(out_sems)
    w_out_copy = come.start(w_out_in, w_out)
    blocks = [slice(lower, lower + ROW_BLOCK) for lower in range(0, states.shape[0], ROW_BLOCK)]
    pairs = [slice(lower, lower + 2 * ROW_BLOCK) for lower in range(0, states.shape[0], 2 * ROW_BLOCK)]
    units = own_gate_in.shape[0]

    def start_rows(rows):
        pairs = ((attended_in, attended), (states_in, states), (cotangent_in, cotangent))
        return [come.start(source.at[rows, :], target.at[rows, :]) for source, target in pairs]

    def start_units(sources, target):
        return [come.start(source, target.at[i * units : (i + 1) * units, :]) for i, source in enumerate(sources)]

    row_copies = [start_rows(rows) for rows in pairs]
    weight_copies = [start_units((core_gate_in, core_up_in, core_down_in), core)]
    weight_copies.append(start_units((own_gate_in, own_up_in, own_down_in), own))
    w_out_copy.wait()
    for index, rows in enumerate(blocks):
        if index % 2 == 0:
            for copy in row_copies[index // 2]:
                copy.wait()
        live = live_rows(count_ref, rows.start, ROW_BLOCK)
        middle = states[rows, :] + live * dot(attended[rows, :], w_out[...], 1, 0)
        states[rows, :] = middle
        plain, _ = norm_parts(middle)
        second[rows, :] = (plain * (1.0 + modulation_ref[2:3, :]) + modulation_ref[3:4, :]).astype(low_type)
        branch[rows, :] = (live * cotangent[rows, :]).astype(low_type)

    for source, target in ((states, middle_out), (second, second_out), (branch, branch_out)):
        go.send(source, target)

    def done(rows):
        if rows.stop == out.shape[0]:
            go.send(out, out_out)
            go.send(grad, grad_out)

    scratch = (hidden, grad_gate, grad_up)
    for copy in weight_copies[0]:
        copy.wait()
    feed_chunk(core, second, branch, out, grad, *scratch, (core_one, core_two), True, None)
    go.send(core_one, core_one_out)
    go.send(core_two, core_two_out)
    for copy in weight_copies[1]:
        copy.wait()
    feed_chunk(own, second, branch, out, grad, *scratch, (own_one, own_two), False, done)
    go.send(own_one, own_one_out)
    go.send(own_two, own_two_out)
    go.finish()


def feed_last_kernel(
    count_ref, core_ref, modulation_ref, cotangent_in, attended_in, w_out_in, spread_own_in, spread_far_in,
    middle_in, second_in, branch_in, out_in, grad_in, cross_half_in, cross_rest_in, far_half_in, far_rest_in,
    output_out, grad_middle_out, grad_own_out, grad_far_out, mod_grad_ref,
    cross_one_out, cross_two_out, far_one_out, far_two_out,
    cotangent, attended, w_out, spread_own, spread_far, middle, second, branch, out, grad, cross, far,
    grad_own, grad_far, cross_one, cross_two, far_one, far_two, w_out_grad,
    hidden, grad_gate, grad_up, in_sems, out_sems,
):
    come, go = Mover(in_sems), Mover(out_sems)
    half_rows = far_half_in.shape[0]

    def halves(half_in, rest_in, target):
        return [
            (source, target.at[pl.ds(pl.multiple_of(which * half_rows, half_rows), half_rows), :])
            for source, which in ((half_in, core_ref[1]), (rest_in, 1 - core_ref[1]))
        ]

    def start_all(pairs):
        return [come.start(source, target) for source, target in pairs]

    first_copies = start_all([(second_in, second), *halves(far_half_in, far_rest_in, far), (branch_in, branch)])
    scratch = (hidden, grad_gate, grad_up)
    for copy in first_copies:
        copy.wait()
    sum_copies = start_all([(out_in, out), (grad_in, grad)])
    late_copies = []

    def ready():
        for copy in sum_copies:
            copy.wait()
        late_copies.extend(
            start_all(
                [
                    *halves(cross_half_in, cross_rest_in, cross), (w_out_in, w_out), (middle_in, middle),
                    (cotangent_in, cotangent), (spread_own_in, spread_own), (spread_far_in, spread_far),
                    (attended_in, attended),
                ]
            )
        )

    feed_chunk(far, second, branch, out, grad, *scratch, (far_one, far_two), False, None, ready)
    go.send(far_one, far_one_out)
    for copy in late_copies:
        copy.wait()
    feed_chunk(cross, second, branch, out, grad, *scratch, (cross_one, cross_two), False, None)
    go.send(cross_one, cross_one_out)
    low_grad = hidden
    scale, bias = 0.0, 0.0
    for lower in range(0, middle.shape[0], ROW_BLOCK):
        rows = slice(lower, lower + ROW_BLOCK)
        live = live_rows(count_ref, lower, ROW_BLOCK)
        block = middle[rows, :]
        plain, inverse = norm_parts(block)
        middle[rows, :] = block + live * out[rows, :]
        grad_second = grad[rows, :]
        scale += jnp.sum(grad_second * plain, axis=0, keepdims=True)
        bias += jnp.sum(grad_second, axis=0, keepdims=True)
        grad_middle = cotangent[rows, :] + norm_back(grad_second * (1.0 + modulation_ref[2:3, :]), plain, inverse)
        cotangent[rows, :] = grad_middle
        low_grad[rows, :] = (live * grad_middle).astype(low_type)
        grad_attended = dot(low_grad[rows, :], w_out[...], 1, 1)
        grad_own[rows, :] = (grad_attended * spread_own[rows, :]).astype(low_type)
        grad_far[rows, :] = (grad_attended * spread_far[rows, :]).astype(low_type)
        if lower // ROW_BLOCK % 2:
            pair = slice(lower - ROW_BLOCK, lower + ROW_BLOCK)
            for source, target in (
                (middle, output_out), (cotangent, grad_middle_out), (grad_own, grad_own_out), (grad_far, grad_far_out),
            ):
                go.send(source.at[pair, :], target.at[pair, :])
    mod_grad_ref[0:1, :] = scale
    mod_grad_ref[1:2, :] = bias

    half = w_out_grad.shape[0] // 2
    w_out_grad[...] = dot(attended[...], low_grad[...], 0, 0).astype(low_type)
    for two, two_out, side_of in ((far_two, far_two_out, core_ref[0]), (cross_two, cross_two_out, 1 - core_ref[0])):
        start = pl.multiple_of(side_of * half, half)
        two[two.shape[0] - half :, :] = w_out_grad[pl.ds(start, half), :]
        go.send(two, two_out)
    go.finish()


def project_back_kernel(
    core_ref, modulation_ref, mod_two_ref, plain_in, query_in, plain_far_in, key_in, far_key_in, value_in, far_value_in,
    w_query_in, w_key_in, w_value_in,
    kept_out, sent_out, mod_grad_ref,
    plain, query, plain_far, key, far_key, value, far_value, w_query, w_key, w_value,
    weight_grad, packed, in_sems, out_sems,
):
    come, go = Mover(in_sems), Mover(out_sems)
    width = weight_grad.shape[2]
    half = width // 2
    own_half = pl.ds(pl.multiple_of(core_ref[0] * half, half), half)
    other_half = pl.ds(pl.multiple_of((1 - core_ref[0]) * half, half), half)
    groups = (
        ((plain_in, plain), (query_in, query), (w_query_in, w_query)),
        ((key_in, key), (plain_far_in, plain_far), (far_key_in, far_key), (w_key_in, w_key)),
        ((value_in, value), (far_value_in, far_value), (w_value_in, w_value)),
    )
    copies = [[come.start(source, target) for source, target in group] for group in groups]
    gain = (1.0 + modulation_ref[0:1, :]).T
    shift = modulation_ref[1:2, :].T
    scale, bias = 0.0, 0.0
    for kind, (own, far, weight) in enumerate(
        ((query, None, w_query), (key, far_key, w_key), (value, far_value, w_value))
    ):
        for copy in copies[kind]:
            copy.wait()
        grad = dot(plain[...], own[...], 0, 0)
        total = jnp.sum(own[...].astype(jnp.float32), axis=0, keepdims=True)
        if far is not None:
            grad += dot(plain_far[...], far[...], 0, 0)
            total += jnp.sum(far[...].astype(jnp.float32), axis=0, keepdims=True)
        matrix = weight[...].astype(jnp.float32)
        scale += jnp.sum(grad * matrix, axis=1, keepdims=True)
        bias += jnp.sum(matrix * total, axis=1, keepdims=True)
        weight_grad[kind] = (grad * gain + shift * total).astype(low_type)
        go.send(weight_grad.at[kind, own_half, :], kept_out.at[kind])
        go.send(weight_grad.at[kind, other_half, :], sent_out.at[kind * half : (kind + 1) * half, :])
    mod_grad_ref[0:1, :] = scale.T
    mod_grad_ref[1:2, :] = bias.T
    mod_grad_ref[2:4, :] = mod_two_ref[...]
    mod_grad = mod_grad_ref[...]
    high = mod_grad.astype(low_type).astype(jnp.float32)
    packed[...] = jnp.concatenate([high, mod_grad - high, jnp.zeros((8, high.shape[1]), jnp.float32)]).astype(low_type)
    go.send(packed, sent_out.at[3 * half : 3 * half + 16, :])
    go.finish()


def small(work, out_shapes, scalar_args, args, grant=16):
    def kernel(scalar_ref, *refs):
        for out_ref, value in zip(refs[len(args) :], work(scalar_ref, *refs[: len(args)])):
            out_ref[...] = value.astype(out_ref.dtype)

    return call(
        kernel, list(out_shapes), (scalar_args, *args), specs=[scalars] + [whole] * len(args), grant=grant, flops=2**29
    )


def half_of(ref, which):
    half = ref.shape[1] // 2
    return ref[:, pl.ds(pl.multiple_of(which * half, half), half), :].astype(jnp.float32)


def halves_of(side_of, *refs):
    return sum(half_of(ref, 1 - side_of) for ref in refs), sum(half_of(ref, side_of) for ref in refs)


def finish_kernel(
    states_ref, grad_middle_ref, query_ref, key_ref, value_ref, modulation_ref, send_ref, w_query_ref, w_key_ref, w_value_ref, *refs
):
    returned_refs, (grad_states_ref, returned, sems) = refs[:4], refs[4:]

    @pl.when(pl.program_id(0) == 0)
    def _():
        for copy in fetch(returned_refs, returned, sems):
            copy.wait()

    rows = states_ref.shape[0]
    sends = send_ref.shape[1]
    grad = sum(
        dot(own_ref[...], weight_ref[...], 1, 1)
        for own_ref, weight_ref in ((query_ref, w_query_ref), (key_ref, w_key_ref), (value_ref, w_value_ref))
    )
    for position in range(len(returned_refs)):
        chosen = chosen_rows(send_ref, position, rows, pl.program_id(0) * rows)
        grad += dot(chosen, returned[position * sends : (position + 1) * sends, :], 1, 0)
    plain, inverse = norm_parts(states_ref[...])
    grad_states_ref[...] = grad_middle_ref[...] + norm_back(grad * (1.0 + modulation_ref[0:1, :]), plain, inverse)


def finish(states, grad_middle, grads, modulation, send_list, weights, returned):
    rows, width = states.shape
    by_block = pl.BlockSpec((ROW_BLOCK, width), lambda i: (i, 0))
    once = [pl.BlockSpec(part.shape, lambda i: (0, 0)) for part in (modulation, send_list, *weights)]
    return pl.pallas_call(
        finish_kernel,
        grid=(rows // ROW_BLOCK,),
        in_specs=[by_block] * 5 + once + [anywhere] * len(returned),
        out_specs=by_block,
        out_shape=shaped((rows, width), jnp.float32),
        scratch_shapes=[
            pltpu.VMEM((sum(part.shape[0] for part in returned), width), low_type),
            pltpu.SemaphoreType.DMA((len(returned),)),
        ],
        compiler_params=pltpu.CompilerParams(vmem_limit_bytes=24 * 2**20),
        cost_estimate=pl.CostEstimate(flops=2**31, bytes_accessed=2**23, transcendentals=0),
    )(states, grad_middle, *grads, modulation, send_list, *weights, *returned)


def from_behind(block, axis, distance):
    devices = range(lax.axis_size(axis))
    route = [((i - distance) % len(devices), i) for i in devices]
    return lax.ppermute(block, axis, route)


def swap(block, mask):
    count = lax.axis_size("nodes") * lax.axis_size("hid")
    return lax.ppermute(block, everywhere, [(i, i ^ mask) for i in range(count)])


def place():
    return lax.axis_index("nodes") * lax.axis_size("hid") + lax.axis_index("hid")


def side(link):
    return (place() >> link) & 1


def added(parts):
    return sum(part.astype(jnp.float32) for part in parts).astype(low_type)


def pieces_of(block, count, index):
    size = block.shape[1] // count
    return lax.dynamic_slice_in_dim(block, index * size, size, 1)


def half_sum(block, link):
    return pieces_of(block, 2, side(link)) + swap(pieces_of(block, 2, 1 - side(link)), 1 << link)


def half_join(block, link):
    other = swap(block, 1 << link)
    return jnp.where(
        side(link) == 0, jnp.concatenate([block, other], axis=1), jnp.concatenate([other, block], axis=1)
    )


def whole_sum(block, link):
    return block + swap(block, 1 << link)


def pack_wide(values):
    high = lax.reduce_precision(values, 8, 7)
    both = jnp.concatenate([high, values - high]).astype(low_type)
    return jnp.concatenate([both, jnp.zeros((16 - both.shape[0], both.shape[1]), low_type)])


def unpack_wide(packed, count):
    packed = packed.astype(jnp.float32)
    return packed[:count] + packed[count : 2 * count]


def group_sum(block, wide, links):
    count = 1 << len(links)
    here = sum(side(link) << i for i, link in enumerate(links))
    total = pieces_of(block, count, here).astype(jnp.float32)
    shape = total.shape
    packed = pack_wide(wide)
    for mask in range(1, count):
        sent = pieces_of(block, count, here ^ mask).reshape(-1, shape[-1])
        come = swap(jnp.concatenate([sent, packed]), sum(((mask >> i) & 1) << link for i, link in enumerate(links)))
        total = total + come[: -packed.shape[0]].reshape(shape).astype(jnp.float32)
        wide = wide + unpack_wide(come[-packed.shape[0] :], wide.shape[0])
    return total.astype(low_type), wide


def group_join(block, links):
    found = [block]
    for mask in range(1, 1 << len(links)):
        found.append(swap(block, sum(((mask >> i) & 1) << link for i, link in enumerate(links))))
    for i, link in enumerate(links):
        turned = [found[k ^ (1 << i)] for k in range(len(found))]
        found = [jnp.where(side(link) == 0, kept, other) for kept, other in zip(found, turned)]
    return jnp.concatenate(found, axis=1)


def after(values, previous):
    return lax.optimization_barrier((values, previous))


def body(
    states,
    condition,
    mod_w,
    w_query,
    w_key,
    w_value,
    w_out,
    w_gate,
    w_up,
    w_down,
    counts,
    send_rows,
    neighbours,
    cotangent,
):
    rows, width = states.shape
    sends = send_rows.shape[2]
    ext = rows + len(halo_steps) * sends
    f32 = jnp.float32
    parcel = shaped((sends, width))
    send_list = send_rows[0]

    links = (lax.axis_size("nodes") * lax.axis_size("hid")).bit_length() - 1
    core, across, *around = range(links)

    normed, plain, modulation, *parcels = prepare(states, condition, mod_w, send_list)
    landed = [from_behind(part, everywhere, hop) for part, hop in zip(parcels, halo_steps)]
    shard, normed = after((w_gate, w_up, w_down), normed)
    near_half = side(around[0])
    middle_row = shard[1].shape[0] // 2
    far_half = jnp.where(
        near_half == 0,
        jnp.concatenate([shard[0], shard[1][:middle_row]]),
        jnp.concatenate([shard[1][middle_row:], shard[2]]),
    )
    far_half = swap(far_half, 1 << across)

    queries, own_keys, own_values, *own_raised, top, total, mixed, packed = attend_own(
        normed, neighbours.T, w_query, w_key, w_value, ext - rows
    )
    queries, far_half, landed, shard = lax.optimization_barrier((queries, far_half, landed, shard))
    core_shard = [swap(weight, 1 << core) for weight in shard]
    far_rest = swap(far_half, 1 << around[0])
    cross_half = swap(far_half, 1 << core)
    *far_raised, attended, spread_own, spread_far, far_keys, far_values, plain_far = attend_far(
        modulation, queries, w_key, w_value, packed, top, total, mixed, landed
    )

    low_rows = shaped((rows, width))
    wide_rows = shaped((rows, width), f32)
    shard_rows = sum(weight.size for weight in shard) // width
    all_units = shaped((shard_rows, width))
    half_grad = shaped((shard_rows // 2, width))
    joint_grad = shaped((shard_rows // 2 + width // 2, width))

    def room(*shapes):
        return [pltpu.VMEM(one.shape, one.dtype) for one in shapes]

    middle, second, branch, out, grad, core_one, core_two, own_one, own_two = call(
        feed_first_kernel,
        [wide_rows, low_rows, low_rows, wide_rows, wide_rows] + [half_grad] * 4,
        (counts, modulation, states, cotangent, attended, w_out, *core_shard, *shard),
        grant=56,
        specs=[scalars, whole] + [anywhere] * 10,
        out_specs=[anywhere] * 9,
        scratch=room(wide_rows, wide_rows, low_rows, w_out, all_units, all_units, low_rows, low_rows)
        + room(wide_rows, wide_rows)
        + room(*[half_grad] * 4, *[low_rows] * 3)
        + [pltpu.SemaphoreType.DMA((13,)), pltpu.SemaphoreType.DMA((9,))],
        flops=2**34,
        moved=2**24,
    )
    core_index = jnp.stack([lax.axis_index("hid") & 1, near_half])
    (cross_half, far_rest), grad = after((cross_half, far_rest), grad)
    cross_rest = swap(far_rest, 1 << core)
    fold = (-1, width // 2, width)

    def over_cores(*grads):
        return [[kept.reshape(fold), swap(sent, 1 << core).reshape(fold)] for kept, sent in grads]

    first, second_link, *rest = around
    sides = jnp.stack([side(first), side(second_link)])

    def lines(blocks, count):
        return shaped((blocks, count, width))

    def first_halves(side_ref, one, one_come, two, two_come):
        return *halves_of(side_ref[0], one, one_come), *halves_of(side_ref[1], two, two_come)

    own_sums = over_cores((own_one, core_one), (own_two, core_two))
    kept = own_sums[0][0].shape[0]
    eighth = fold[1] // 2
    quarter = eighth // 2
    one_sent, one_own, two_sent, two_own = small(
        first_halves, [lines(kept, eighth)] * 4, sides, (*own_sums[0], *own_sums[1])
    )
    (one_sent, two_sent), cross_rest = after((one_sent, two_sent), cross_rest)
    own_come = swap(one_sent, 1 << first), swap(two_sent, 1 << second_link)
    output, grad_middle, grad_own, grad_far, mod_two, cross_one, cross_two, far_one, far_two = call(
        feed_last_kernel,
        [wide_rows, wide_rows, low_rows, low_rows, shaped((2, width), f32)] + [half_grad, joint_grad] * 2,
        (counts, core_index, modulation, cotangent, attended, w_out, spread_own, spread_far)
        + (middle, second, branch, out, grad, cross_half, cross_rest, far_half, far_rest),
        grant=56,
        specs=[scalars, scalars, whole] + [anywhere] * 14,
        out_specs=[anywhere] * 4 + [whole] + [anywhere] * 4,
        scratch=room(wide_rows, low_rows, w_out, wide_rows, wide_rows, wide_rows, low_rows, low_rows)
        + room(wide_rows, wide_rows, all_units, all_units, low_rows, low_rows)
        + room(half_grad, joint_grad, half_grad, joint_grad)
        + room(w_out, *[low_rows] * 3)
        + [pltpu.SemaphoreType.DMA((14,)), pltpu.SemaphoreType.DMA((12,))],
        flops=2**34,
        moved=2**24,
    )

    (cross_one, cross_two), own_come = after((cross_one, cross_two), own_come)
    far_sums = over_cores((far_one, cross_one), (far_two, cross_two))
    one_sent, one_far, two_sent, two_far = small(
        first_halves,
        [lines(kept, eighth)] * 2 + [lines(kept + 1, eighth)] * 2,
        sides,
        (*far_sums[0], *far_sums[1]),
    )
    grad_far, (one_sent, two_sent) = after(grad_far, (one_sent, two_sent))
    far_come = swap(one_sent, 1 << first), swap(two_sent, 1 << second_link)
    partial, *far_pieces = attend_back(
        queries, attended, far_keys, far_values, grad_far, far_raised, returns=(w_key, w_value)
    )
    far_pieces, parcels = far_pieces[:2], far_pieces[2:]
    far_come, (grad_own, partial) = after(far_come, (grad_own, partial))

    def second_halves(side_ref, one_own, one_own_come, one_far, one_far_come, two_own, two_own_come, two_far, two_far_come):
        own_sent, own_kept = halves_of(side_ref[1], one_own, one_own_come)
        far_sent, far_kept = halves_of(side_ref[1], one_far, one_far_come)
        two_kept = two_own[...].astype(f32) + two_own_come[...].astype(f32)
        two_sent = two_far[...].astype(f32) + two_far_come[...].astype(f32)
        return jnp.concatenate([own_sent, far_sent]), own_kept, far_kept, two_kept, two_sent

    one_sent, one_own, one_far, two_own, two_sent = small(
        second_halves,
        [lines(2 * kept, quarter), lines(kept, quarter), lines(kept, quarter), lines(kept, eighth), lines(kept + 1, eighth)],
        sides,
        (one_own, own_come[0], one_far, far_come[0], two_own, own_come[1], two_far, far_come[1]),
    )
    (one_sent, two_sent), grad_own = after((one_sent, two_sent), grad_own)
    one_come, two_come = swap(one_sent, 1 << second_link), swap(two_sent, 1 << across)
    pieces = attend_back(queries, attended, own_keys, own_values, grad_own, own_raised, partial)
    (one_come, two_come), pieces = after((one_come, two_come), pieces)

    def third_halves(side_ref, one_own, one_far, one_come, two_own, two_last, two_come):
        one_kept = one_own[...].astype(f32) + one_come[:kept].astype(f32)
        one_sent = one_far[...].astype(f32) + one_come[kept:].astype(f32)
        here = side_ref[0]
        own_sent, own_kept = halves_of(here, two_own, two_come.at[:kept])
        last_sent, last_kept = halves_of(here, two_last.at[kept:], two_come.at[kept:])
        return one_sent, one_kept, jnp.concatenate([own_sent, last_sent]), jnp.concatenate([own_kept, last_kept])

    one_sent, one_kept, two_sent, two_kept = small(
        third_halves,
        [lines(kept, quarter)] * 2 + [lines(kept + 1, quarter)] * 2,
        sides,
        (one_own, one_far, one_come, two_own, two_sent, two_come),
    )
    (one_sent, two_sent), pieces = after((one_sent, two_sent), pieces)
    one_come, two_come = swap(one_sent, 1 << across), swap(two_sent, 1 << first)
    returned = [from_behind(part, everywhere, -hop) for part, hop in zip(parcels[:3], halo_steps)]
    far_low = shaped((ext - rows, width))
    attn_kept, attn_sent, mod_grad = call(
        project_back_kernel,
        [shaped((3, width // 2, width)), shaped((3 * width // 2 + 16, width)), shaped((4, width), f32)],
        (core_index, modulation, mod_two, plain, pieces[0], plain_far, pieces[1], far_pieces[0], pieces[2], far_pieces[1])
        + (w_query, w_key, w_value),
        specs=[scalars, whole, whole] + [anywhere] * 10,
        out_specs=[anywhere, anywhere, whole],
        scratch=room(low_rows, low_rows, far_low, low_rows, far_low, low_rows, far_low, w_query, w_key, w_value)
        + room(shaped((3, width, width)), shaped((16, width)))
        + [pltpu.SemaphoreType.DMA((10,)), pltpu.SemaphoreType.DMA((7,))],
        flops=2**32,
        moved=2**23,
    )

    def on_both(step, link):
        def run(one, two):
            both = step(jnp.concatenate([one, two]), link)
            return both[:kept], both[kept:]

        return run

    shard_steps = [on_both(whole_sum, link) for link in rest]
    shard_steps.append(lambda one, two: (half_join(one, second_link), half_join(two, first)))
    shard_steps.append(lambda one, two: (half_join(one, first), half_join(two, second_link)))

    groups = [[across, first]] + [around[i : i + 2] for i in range(1, len(around), 2)]
    def over_attn_cores(kept, wide):
        come = swap(attn_sent, 1 << core)
        total = kept.astype(f32) + come[:-16].reshape(kept.shape).astype(f32)
        return total.astype(low_type), wide + unpack_wide(come[-16:], wide.shape[0])

    attn_steps = [over_attn_cores] + [functools.partial(group_sum, links=group) for group in groups]
    attn_steps += [lambda grad, wide, group=group: (group_join(grad, group), wide) for group in reversed(groups)]

    returned, (one_come, two_come), parcels, attn_sent = lax.optimization_barrier(
        (returned, (one_come, two_come), parcels, attn_sent)
    )
    returned.append(from_behind(parcels[3], everywhere, -halo_steps[3]))
    shard_state = added([one_kept, one_come]), added([two_kept, two_come])
    attn_state = attn_kept, mod_grad
    shard_turns = [[]] + [[step] for step in shard_steps]
    for index in range(max(len(shard_turns), len(attn_steps))):
        for step in shard_turns[index] if index < len(shard_turns) else []:
            shard_state = step(*shard_state)
        if index < len(attn_steps):
            attn_state = attn_steps[index](*attn_state)
        if index == 1:
            returned, attn_state = after(returned, attn_state)
        if index == 4:
            grad_states = finish(
                states, grad_middle, pieces, modulation, send_list, (w_query, w_key, w_value), returned
            )
            grad_states, attn_state = after(grad_states, attn_state)
        if index in (1, 2):
            shard_state, attn_state = after(shard_state, attn_state)
    (one, two), (attn_grad, mod_grad) = shard_state, attn_state
    shard_grad = jnp.concatenate([one, two[:kept]]).reshape(-1, width).astype(f32)
    grad_w_gate, grad_w_up, grad_w_down = jnp.split(shard_grad, 3)
    grad_w_query, grad_w_key, grad_w_value = half_join(attn_grad, core).astype(f32)
    grad_w_out = half_join(two[kept:], core)[0].astype(f32)
    mod_grad = mod_grad.reshape(-1)
    grad_mod_w = condition[:, None] * mod_grad[None, :]
    grad_condition = jnp.sum(mod_w.astype(f32) * mod_grad[None, :], axis=1)
    return (
        output,
        grad_states,
        grad_condition,
        grad_mod_w,
        grad_w_query,
        grad_w_key,
        grad_w_value,
        grad_w_out,
        grad_w_gate,
        grad_w_up,
        grad_w_down,
    )


def solution(mesh):
    rows = P(everywhere, None)
    placed = (
        rows,
        P(),
        P(),
        P(),
        P(),
        P(),
        P(),
        P(None, "hid"),
        P(None, "hid"),
        P("hid", None),
        P(everywhere),
        P(everywhere, None, None),
        rows,
        rows,
    )
    return jax.shard_map(
        body,
        mesh=mesh,
        in_specs=placed,
        out_specs=(rows, rows, P(), P(), P(), P(), P(), P(), P(None, "hid"), P(None, "hid"), P("hid", None)),
        check_vma=False,
    )
```

```python
import functools

import jax
import jax.numpy as jnp
from jax import lax
from jax.experimental import pallas as pl
from jax.experimental.pallas import tpu as pltpu
from jax.sharding import PartitionSpec as P

HEADS = 4
HEAD_DIM = 128
NEIGH = 16
BLOCK = 1024
ROW_BLOCK = 256
BACK_GRANT = 56
RAISED_PARTS = 1

epsilon = 1e-06
halo_steps = (1, -1, 2, -2)
highest = lax.Precision.HIGHEST
score_scale = HEAD_DIM ** (-0.5)
LOG2_E = 1.4426950408889634
low_type = jnp.bfloat16
everywhere = ("nodes", "hid")
whole = pl.BlockSpec(memory_space=pltpu.VMEM)
scalars = pl.BlockSpec(memory_space=pltpu.SMEM)
anywhere = pl.BlockSpec(memory_space=pl.ANY)


def dot(left, right, left_dim, right_dim):
    return lax.dot_general(
        left, right, (((left_dim,), (right_dim,)), ((), ())), preferred_element_type=jnp.float32
    )


def shaped(shape, dtype=low_type):
    return jax.ShapeDtypeStruct(shape, dtype)


def norm_parts(states):
    centred = states - jnp.mean(states, axis=-1, keepdims=True)
    inverse = lax.rsqrt(jnp.mean(centred * centred, axis=-1, keepdims=True) + epsilon)
    return (centred * inverse, inverse)


def norm_back(grad_plain, plain, inverse):
    first_mean = jnp.mean(grad_plain, axis=-1, keepdims=True)
    second_mean = jnp.mean(grad_plain * plain, axis=-1, keepdims=True)
    return inverse * (grad_plain - first_mean - plain * second_mean)


def call(kernel, out_shape, args, specs=None, out_specs=None, scratch=(), flops=0, moved=0, grant=60):
    single = not isinstance(out_shape, list)
    return pl.pallas_call(
        kernel,
        in_specs=specs or [whole] * len(args),
        out_specs=out_specs or (whole if single else [whole] * len(out_shape)),
        out_shape=out_shape,
        scratch_shapes=list(scratch),
        compiler_params=pltpu.CompilerParams(vmem_limit_bytes=grant * 2**20),
        cost_estimate=pl.CostEstimate(flops=flops, bytes_accessed=moved, transcendentals=0),
    )(*args)


def chosen_rows(send_ref, position, rows, first=0):
    sends = send_ref.shape[1]
    place = lax.broadcasted_iota(jnp.int32, (rows, sends), 0) + first
    return jnp.where(place == send_ref[position : position + 1, :], 1.0, 0.0).astype(low_type)


def prepare_kernel(
    states_ref, condition_ref, mod_w_ref, send_ref, normed_ref, plain_ref, modulation_ref, *refs
):
    *parcel_refs, plain = refs
    step, (block, width) = pl.program_id(0), states_ref.shape

    @pl.when(step == 0)
    def _():
        mixed = sum(
            condition_ref[i] * mod_w_ref[i : i + 1, :].astype(jnp.float32) for i in range(condition_ref.shape[0])
        )
        for piece in range(4):
            modulation_ref[piece : piece + 1, :] = mixed[:, piece * width : (piece + 1) * width]

    values, _ = norm_parts(states_ref[...])
    plain_ref[...] = values.astype(low_type)
    plain[pl.ds(pl.multiple_of(step * block, block), block), :] = plain_ref[...]
    normed_ref[...] = (values * (1.0 + modulation_ref[0:1, :]) + modulation_ref[1:2, :]).astype(low_type)

    @pl.when(step == pl.num_programs(0) - 1)
    def _():
        for position, parcel_ref in enumerate(parcel_refs):
            chosen = chosen_rows(send_ref, position, plain.shape[0])
            parcel_ref[...] = dot(chosen, plain[...], 0, 0).astype(low_type)


def prepare(states, condition, mod_w, send_list):
    rows, width = states.shape
    by_block = pl.BlockSpec((2 * ROW_BLOCK, width), lambda i: (i, 0))

    def once(*shape):
        return pl.BlockSpec(shape, lambda i: (0,) * len(shape))

    count, sends = send_list.shape
    return pl.pallas_call(
        prepare_kernel,
        grid=(rows // ROW_BLOCK // 2,),
        in_specs=[by_block, scalars, once(*mod_w.shape), once(*send_list.shape)],
        out_specs=[by_block, by_block, once(4, width)] + [once(sends, width)] * count,
        out_shape=[shaped((rows, width)), shaped((rows, width)), shaped((4, width), jnp.float32)]
        + [shaped((sends, width))] * count,
        scratch_shapes=[pltpu.VMEM((rows, width), low_type)],
        compiler_params=pltpu.CompilerParams(vmem_limit_bytes=60 * 2**20),
        cost_estimate=pl.CostEstimate(flops=2**30, bytes_accessed=2**22, transcendentals=0),
    )(states, condition, mod_w, send_list)


def count_near(near_ref, cols, groups):
    half = groups // 2
    near = near_ref[:, cols]
    group = near >> 7
    upper = group >= half
    unit = jnp.left_shift(1, 5 * jnp.where(upper, group - half, group))
    low = near & 127
    low_unit = jnp.where(upper, 0, unit)
    high_unit = jnp.where(upper, unit, 0)
    place = lax.broadcasted_iota(jnp.int32, (128, 128), 0)
    low_count = jnp.zeros((128, 128), jnp.int32)
    high_count = low_count
    for n in range(NEIGH):
        same = low[n : n + 1] == place
        low_count = low_count + jnp.where(same, low_unit[n : n + 1], 0)
        high_count = high_count + jnp.where(same, high_unit[n : n + 1], 0)
    return low_count, high_count


def count_bias(packed, position):
    count = (packed >> (5 * position)) & 31
    return jnp.where(count > 0, jnp.log2(count.astype(jnp.float32)), -1e30)


def score_pass(key_ref, query, bias, scores, cols, top):
    width = scores.shape[1]
    for g in range(scores.shape[0] // 128):
        part = slice(g * 128, (g + 1) * 128)
        score = dot(key_ref[part, :], query, 1, 1) * (score_scale * LOG2_E) + bias[part, cols]
        scores[part, :] = score
        top = jnp.maximum(top, jnp.max(score.reshape(16, 8, width), axis=0))
    return jnp.max(top, axis=0, keepdims=True)


def raise_pass(scores, top, raised_refs, cols):
    width = scores.shape[1]
    size = raised_refs[0].shape[1]
    total = jnp.zeros((8, width), jnp.float32)
    for g in range(scores.shape[0] // 128):
        part = slice(g * 128, (g + 1) * 128)
        raised = jnp.exp2(scores[part, :] - top)
        total = total + jnp.sum(raised.reshape(16, 8, width), axis=0)
        lower = g * 128 % size
        raised_refs[g * 128 // size][0, lower : lower + 128, cols] = raised.astype(low_type)
    return jnp.sum(total, axis=0, keepdims=True)


def mix(value_t, raised_refs, cols):
    size = raised_refs[0].shape[1]
    return sum(
        dot(value_t[:, i * size : (i + 1) * size], raised_ref[0, :, cols], 1, 0)
        for i, raised_ref in enumerate(raised_refs)
    )


def raised_parts(count, rows):
    size = count // RAISED_PARTS
    return (
        [pl.BlockSpec((1, size, rows), lambda h: (h, 0, 0))] * RAISED_PARTS,
        [shaped((HEADS, size, rows))] * RAISED_PARTS,
    )


def attend_own_kernel(
    groups, normed_ref, near_ref, w_query_ref, w_key_ref, w_value_ref,
    query_ref, key_ref, value_ref, *refs,
):
    raised_refs, refs = refs[:RAISED_PARTS], refs[RAISED_PARTS:]
    top_ref, total_ref, mixed_ref, packed_ref, bias, scores, value_t = refs
    rows = normed_ref.shape[0]
    half = groups // 2

    @pl.when(pl.program_id(0) == 0)
    def _():
        @pl.loop(0, rows // 128)
        def _(step):
            cols = pl.ds(pl.multiple_of(step * 128, 128), 128)
            packed = count_near(near_ref, cols, groups)
            packed_ref[:, cols] = packed[1]
            for g in range(rows // 128):
                bias[g * 128 : (g + 1) * 128, cols] = count_bias(packed[g // half], g % half)

    for weight_ref, out_ref in ((w_query_ref, query_ref), (w_key_ref, key_ref), (w_value_ref, value_ref)):
        out_ref[...] = dot(normed_ref[...], weight_ref[...], 1, 0).astype(low_type)
    value_t[...] = value_ref[...].T
    width = scores.shape[1]

    @pl.loop(0, rows // width)
    def _(step):
        cols = pl.ds(pl.multiple_of(step * width, width), width)
        least = jnp.full((8, width), -jnp.inf, jnp.float32)
        top = score_pass(key_ref, query_ref[cols, :], bias, scores, cols, least)
        top_ref[0, :, cols] = top
        total_ref[0, :, cols] = raise_pass(scores, top, raised_refs, cols)
        mixed_ref[0, :, cols] = mix(value_t, raised_refs, cols)


def attend_own(normed, near, w_query, w_key, w_value, far_rows):
    rows, width = normed.shape
    groups = (rows + far_rows) // 128
    by_row = pl.BlockSpec((rows, HEAD_DIM), lambda h: (0, h))
    by_weight = pl.BlockSpec((width, HEAD_DIM), lambda h: (0, h))
    by_head = pl.BlockSpec((1, 1, rows), lambda h: (h, 0, 0))
    return pl.pallas_call(
        functools.partial(attend_own_kernel, groups),
        grid=(HEADS,),
        in_specs=[pl.BlockSpec((rows, width), lambda h: (0, 0)), pl.BlockSpec((NEIGH, rows), lambda h: (0, 0))]
        + [by_weight] * 3,
        out_specs=[
            by_row,
            by_row,
            by_row,
            *raised_parts(rows, rows)[0],
            by_head,
            by_head,
            pl.BlockSpec((1, HEAD_DIM, rows), lambda h: (h, 0, 0)),
            pl.BlockSpec((128, rows), lambda h: (0, 0)),
        ],
        out_shape=[shaped((rows, width))] * 3
        + [
            *raised_parts(rows, rows)[1],
            shaped((HEADS, 1, rows), jnp.float32),
            shaped((HEADS, 1, rows), jnp.float32),
            shaped((HEADS, HEAD_DIM, rows), jnp.float32),
            shaped((128, rows), jnp.int32),
        ],
        scratch_shapes=[
            pltpu.VMEM((rows, rows), jnp.float32),
            pltpu.VMEM((rows, BLOCK), jnp.float32),
            pltpu.VMEM((HEAD_DIM, rows), low_type),
        ],
        compiler_params=pltpu.CompilerParams(vmem_limit_bytes=56 * 2**20),
        cost_estimate=pl.CostEstimate(flops=2**34, bytes_accessed=2**24, transcendentals=0),
    )(normed, near, w_query, w_key, w_value)


def fetch(parts, to_ref, sems):
    copies, lower = [], 0
    for position, part in enumerate(parts):
        upper = lower + part.shape[0]
        copies.append(pltpu.make_async_copy(part, to_ref.at[lower:upper, :], sems.at[position]))
        copies[-1].start()
        lower = upper
    return copies


def attend_far_kernel(
    skip, modulation_ref, query_ref, w_key_ref, w_value_ref, packed_ref, top_ref, total_ref, mixed_ref, *refs
):
    landed_refs, refs = refs[:4], refs[4:]
    raised_refs, refs = refs[:RAISED_PARTS], refs[RAISED_PARTS:]
    attended_ref, spread_own_ref, spread_far_ref, key_ref, value_ref, plain_ref, *refs = refs
    bias, scores, value_t, normed_ref, sems = refs
    far, rows = bias.shape

    @pl.when(pl.program_id(0) == 0)
    def _():
        copies = fetch(landed_refs, plain_ref, sems)

        @pl.loop(0, rows // 128)
        def _(step):
            cols = pl.ds(pl.multiple_of(step * 128, 128), 128)
            for g in range(far // 128):
                bias[g * 128 : (g + 1) * 128, cols] = count_bias(packed_ref[:, cols], g + skip)

        for copy in copies:
            copy.wait()
        plain = plain_ref[...].astype(jnp.float32)
        normed_ref[...] = (plain * (1.0 + modulation_ref[0:1, :]) + modulation_ref[1:2, :]).astype(low_type)

    key_ref[...] = dot(normed_ref[...], w_key_ref[...], 1, 0).astype(low_type)
    value_ref[...] = dot(normed_ref[...], w_value_ref[...], 1, 0).astype(low_type)
    value_t[...] = value_ref[...].T
    width = scores.shape[1]

    @pl.loop(0, rows // width)
    def _(step):
        cols = pl.ds(pl.multiple_of(step * width, width), width)
        own_top = top_ref[0, :, cols]
        least = jnp.broadcast_to(own_top, (8, width))
        top = score_pass(key_ref, query_ref[cols, :], bias, scores, cols, least)
        factor = jnp.exp2(own_top - top)
        total = raise_pass(scores, top, raised_refs, cols) + total_ref[0, :, cols] * factor
        inverse = 1.0 / total
        own_inverse = inverse * factor
        spread_far_ref[cols, :] = jnp.broadcast_to(inverse, (HEAD_DIM, width)).T
        spread_own_ref[cols, :] = jnp.broadcast_to(own_inverse, (HEAD_DIM, width)).T
        mixed = mix(value_t, raised_refs, cols) * inverse + mixed_ref[0, :, cols] * own_inverse
        attended_ref[cols, :] = mixed.T.astype(low_type)


def attend_far(modulation, queries, w_key, w_value, packed, top, total, mixed, landed):
    rows, width = queries.shape
    far = sum(part.shape[0] for part in landed)
    by_row = pl.BlockSpec((rows, HEAD_DIM), lambda h: (0, h))
    by_far = pl.BlockSpec((far, HEAD_DIM), lambda h: (0, h))
    by_weight = pl.BlockSpec((width, HEAD_DIM), lambda h: (0, h))
    by_head = pl.BlockSpec((1, 1, rows), lambda h: (h, 0, 0))
    groups = (rows + far) // 128
    return pl.pallas_call(
        functools.partial(attend_far_kernel, rows // 128 - groups // 2),
        grid=(HEADS,),
        in_specs=[
            pl.BlockSpec(modulation.shape, lambda h: (0, 0)),
            by_row,
            by_weight,
            by_weight,
            pl.BlockSpec(packed.shape, lambda h: (0, 0)),
            by_head,
            by_head,
            pl.BlockSpec((1, HEAD_DIM, rows), lambda h: (h, 0, 0)),
        ]
        + [anywhere] * len(landed),
        out_specs=[*raised_parts(far, rows)[0], by_row, by_row, by_row, by_far, by_far]
        + [pl.BlockSpec((far, width), lambda h: (0, 0))],
        out_shape=[
            *raised_parts(far, rows)[1],
            shaped((rows, width)),
            shaped((rows, width), jnp.float32),
            shaped((rows, width), jnp.float32),
            shaped((far, width)),
            shaped((far, width)),
            shaped((far, width)),
        ],
        scratch_shapes=[
            pltpu.VMEM((far, rows), jnp.float32),
            pltpu.VMEM((far, BLOCK), jnp.float32),
            pltpu.VMEM((HEAD_DIM, far), low_type),
            pltpu.VMEM((far, width), low_type),
            pltpu.SemaphoreType.DMA((len(landed),)),
        ],
        compiler_params=pltpu.CompilerParams(vmem_limit_bytes=56 * 2**20),
        cost_estimate=pl.CostEstimate(flops=2**33, bytes_accessed=2**23, transcendentals=0),
    )(modulation, queries, w_key, w_value, packed, top, total, mixed, *landed)


def attend_back_kernel(has_partial, query_ref, attended_ref, key_ref, value_ref, grad_ref, *refs):
    raised_refs, refs = refs[:RAISED_PARTS], refs[RAISED_PARTS:]
    size = raised_refs[0].shape[1]
    if has_partial:
        partial_ref, *refs = refs
    else:
        w_key_ref, w_value_ref, *refs = refs
    grad_query_ref, grad_key_ref, grad_value_ref, *refs = refs
    if not has_partial:
        *parcel_refs, low, key_t, grad_normed = refs
    else:
        low, key_t = refs
    rows = query_ref.shape[0]
    key_t[...] = key_ref[...].T

    @pl.loop(0, rows // BLOCK)
    def _(step):
        cols = pl.ds(pl.multiple_of(step * BLOCK, BLOCK), BLOCK)
        attended = attended_ref[cols, :].astype(jnp.float32)
        grad = grad_ref[cols, :]
        mean = jnp.sum((grad.astype(jnp.float32) * attended).T, axis=0, keepdims=True)
        for g in range(value_ref.shape[0] // 128):
            part = slice(g * 128, (g + 1) * 128)
            term = dot(value_ref[part, :], grad, 1, 1) - mean
            lower = g * 128 % size
            raised = raised_refs[g * 128 // size][0, lower : lower + 128, cols]
            low[part, cols] = (term * raised.astype(jnp.float32)).astype(low_type)
        total = dot(key_t[...], low[:, cols], 1, 0)
        if has_partial:
            total = (total + partial_ref[0, :, cols]) * score_scale
            grad_query_ref[cols, :] = total.T.astype(low_type)
        else:
            grad_query_ref[0, :, cols] = total

    for i, raised_ref in enumerate(raised_refs):
        grad_value_ref[i * size : (i + 1) * size, :] = dot(raised_ref[0], grad_ref[...], 1, 0).astype(low_type)
    grad_key_ref[...] = (dot(low[...], query_ref[...], 1, 0) * score_scale).astype(low_type)
    if has_partial:
        return

    back = dot(grad_key_ref[...], w_key_ref[...], 1, 1) + dot(grad_value_ref[...], w_value_ref[...], 1, 1)

    @pl.when(pl.program_id(0) == 0)
    def _():
        grad_normed[...] = back

    @pl.when(pl.program_id(0) > 0)
    def _():
        grad_normed[...] += back

    @pl.when(pl.program_id(0) == HEADS - 1)
    def _():
        grad = grad_normed[...]
        for position, parcel_ref in enumerate(parcel_refs):
            sends = parcel_ref.shape[0]
            parcel_ref[...] = grad[position * sends : (position + 1) * sends, :].astype(low_type)


def attend_back(queries, attended, keys, values, grads, raised, partial=None, returns=None):
    rows, width = queries.shape
    count = keys.shape[0]
    by_row = pl.BlockSpec((rows, HEAD_DIM), lambda h: (0, h))
    by_count = pl.BlockSpec((count, HEAD_DIM), lambda h: (0, h))
    by_head = pl.BlockSpec((1, HEAD_DIM, rows), lambda h: (h, 0, 0))
    in_specs = [by_row, by_row, by_count, by_count, by_row, *raised_parts(count, rows)[0]]
    out_specs = [by_row if returns is None else by_head, by_count, by_count]
    out_shape = [
        shaped((rows, width)) if returns is None else shaped((HEADS, HEAD_DIM, rows), jnp.float32),
        shaped((count, width)),
        shaped((count, width)),
    ]
    scratch = [pltpu.VMEM((count, rows), low_type), pltpu.VMEM((HEAD_DIM, count), low_type)]
    if returns is None:
        in_specs.append(by_head)
    else:
        by_weight = pl.BlockSpec((width, HEAD_DIM), lambda h: (0, h))
        in_specs += [by_weight, by_weight]
        sends = count // len(halo_steps)
        out_specs += [pl.BlockSpec((sends, width), lambda h: (0, 0))] * len(halo_steps)
        out_shape += [shaped((sends, width))] * len(halo_steps)
        scratch.append(pltpu.VMEM((count, width), jnp.float32))
    return pl.pallas_call(
        functools.partial(attend_back_kernel, returns is None),
        grid=(HEADS,),
        in_specs=in_specs,
        out_specs=out_specs,
        out_shape=out_shape,
        scratch_shapes=scratch,
        compiler_params=pltpu.CompilerParams(vmem_limit_bytes=BACK_GRANT * 2**20),
        cost_estimate=pl.CostEstimate(flops=count * 2**22, bytes_accessed=2**22, transcendentals=0),
    )(queries, attended, keys, values, grads, *raised, *([partial] if returns is None else returns))


def live_rows(count_ref, start, rows):
    place = lax.broadcasted_iota(jnp.int32, (rows, 1), 0) + start
    return (place < count_ref[0]).astype(jnp.float32)


class Mover:
    def __init__(self, sems):
        self.sems, self.used, self.open = sems, 0, []

    def start(self, source, target):
        copy = pltpu.make_async_copy(source, target, self.sems.at[self.used])
        self.used += 1
        copy.start()
        return copy

    def send(self, source, target):
        self.open.append(self.start(source, target))

    def finish(self):
        for copy in self.open:
            copy.wait()


def feed_chunk(weight_ref, second_ref, branch_ref, out_ref, grad_ref, hidden, grad_gate, grad_up, store, fresh, done, ready=None):
    units = weight_ref.shape[0] // 3
    gate_rows, up_rows, down_rows = (slice(i * units, (i + 1) * units) for i in range(3))
    for step in range(second_ref.shape[0] // ROW_BLOCK):
        rows = slice(step * ROW_BLOCK, (step + 1) * ROW_BLOCK)
        second = second_ref[rows, :]
        gate = dot(second, weight_ref[gate_rows, :], 1, 0)
        up = dot(second, weight_ref[up_rows, :], 1, 0)
        sigmoid = 1.0 / (1.0 + jnp.exp(-gate))
        activated = gate * sigmoid
        hidden[rows, :] = (activated * up).astype(low_type)
        back = dot(branch_ref[rows, :], weight_ref[down_rows, :], 1, 1)
        grad_gate[rows, :] = (back * up * (sigmoid + activated * (1.0 - sigmoid))).astype(low_type)
        grad_up[rows, :] = (back * activated).astype(low_type)
        out = dot(hidden[rows, :], weight_ref[down_rows, :], 1, 0)
        grad = dot(grad_gate[rows, :], weight_ref[gate_rows, :], 1, 1) + dot(
            grad_up[rows, :], weight_ref[up_rows, :], 1, 1
        )
        if step == 0 and ready is not None:
            ready()
        if fresh:
            out_ref[rows, :] = out
            grad_ref[rows, :] = grad
        else:
            out_ref[rows, :] += out
            grad_ref[rows, :] += grad
        if done is not None:
            done(rows)

    one, two = store
    half = units // 2
    one[:units, :] = dot(second_ref[...], grad_gate[...], 0, 0).astype(low_type)
    grad_up_weight = dot(second_ref[...], grad_up[...], 0, 0).astype(low_type)
    one[units:, :] = grad_up_weight[:half, :]
    two[:half, :] = grad_up_weight[half:, :]
    two[half : half + units, :] = dot(hidden[...], branch_ref[...], 0, 0).astype(low_type)


def feed_first_kernel(
    count_ref, modulation_ref, states_in, cotangent_in, attended_in, w_out_in,
    core_gate_in, core_up_in, core_down_in, own_gate_in, own_up_in, own_down_in,
    middle_out, second_out, branch_out, out_out, grad_out, core_one_out, core_two_out, own_one_out, own_two_out,
    states, cotangent, attended, w_out, core, own, second, branch, out, grad,
    core_one, core_two, own_one, own_two, hidden, grad_gate, grad_up, in_sems, out_sems,
):
    come, go = Mover(in_sems), Mover(out_sems)
    w_out_copy = come.start(w_out_in, w_out)
    blocks = [slice(lower, lower + ROW_BLOCK) for lower in range(0, states.shape[0], ROW_BLOCK)]
    pairs = [slice(lower, lower + 2 * ROW_BLOCK) for lower in range(0, states.shape[0], 2 * ROW_BLOCK)]
    units = own_gate_in.shape[0]

    def start_rows(rows):
        pairs = ((attended_in, attended), (states_in, states), (cotangent_in, cotangent))
        return [come.start(source.at[rows, :], target.at[rows, :]) for source, target in pairs]

    def start_units(sources, target):
        return [come.start(source, target.at[i * units : (i + 1) * units, :]) for i, source in enumerate(sources)]

    row_copies = [start_rows(rows) for rows in pairs]
    weight_copies = [start_units((core_gate_in, core_up_in, core_down_in), core)]
    weight_copies.append(start_units((own_gate_in, own_up_in, own_down_in), own))
    w_out_copy.wait()
    for index, rows in enumerate(blocks):
        if index % 2 == 0:
            for copy in row_copies[index // 2]:
                copy.wait()
        live = live_rows(count_ref, rows.start, ROW_BLOCK)
        middle = states[rows, :] + live * dot(attended[rows, :], w_out[...], 1, 0)
        states[rows, :] = middle
        plain, _ = norm_parts(middle)
        second[rows, :] = (plain * (1.0 + modulation_ref[2:3, :]) + modulation_ref[3:4, :]).astype(low_type)
        branch[rows, :] = (live * cotangent[rows, :]).astype(low_type)

    for source, target in ((states, middle_out), (second, second_out), (branch, branch_out)):
        go.send(source, target)

    def done(rows):
        if rows.stop == out.shape[0]:
            go.send(out, out_out)
            go.send(grad, grad_out)

    scratch = (hidden, grad_gate, grad_up)
    for copy in weight_copies[0]:
        copy.wait()
    feed_chunk(core, second, branch, out, grad, *scratch, (core_one, core_two), True, None)
    go.send(core_one, core_one_out)
    go.send(core_two, core_two_out)
    for copy in weight_copies[1]:
        copy.wait()
    feed_chunk(own, second, branch, out, grad, *scratch, (own_one, own_two), False, done)
    go.send(own_one, own_one_out)
    go.send(own_two, own_two_out)
    go.finish()


def feed_last_kernel(
    count_ref, core_ref, modulation_ref, cotangent_in, attended_in, w_out_in, spread_own_in, spread_far_in,
    middle_in, second_in, branch_in, out_in, grad_in, cross_half_in, cross_rest_in, far_half_in, far_rest_in,
    output_out, grad_middle_out, grad_own_out, grad_far_out, mod_grad_ref,
    cross_one_out, cross_two_out, far_one_out, far_two_out,
    cotangent, attended, w_out, spread_own, spread_far, middle, second, branch, out, grad, cross, far,
    grad_own, grad_far, cross_one, cross_two, far_one, far_two, w_out_grad,
    hidden, grad_gate, grad_up, in_sems, out_sems,
):
    come, go = Mover(in_sems), Mover(out_sems)
    half_rows = far_half_in.shape[0]

    def halves(half_in, rest_in, target):
        return [
            (source, target.at[pl.ds(pl.multiple_of(which * half_rows, half_rows), half_rows), :])
            for source, which in ((half_in, core_ref[1]), (rest_in, 1 - core_ref[1]))
        ]

    def start_all(pairs):
        return [come.start(source, target) for source, target in pairs]

    first_copies = start_all([(second_in, second), *halves(far_half_in, far_rest_in, far), (branch_in, branch)])
    scratch = (hidden, grad_gate, grad_up)
    for copy in first_copies:
        copy.wait()
    sum_copies = start_all([(out_in, out), (grad_in, grad)])
    late_copies = []

    def ready():
        for copy in sum_copies:
            copy.wait()
        late_copies.extend(
            start_all(
                [
                    *halves(cross_half_in, cross_rest_in, cross), (w_out_in, w_out), (middle_in, middle),
                    (cotangent_in, cotangent), (spread_own_in, spread_own), (spread_far_in, spread_far),
                    (attended_in, attended),
                ]
            )
        )

    feed_chunk(far, second, branch, out, grad, *scratch, (far_one, far_two), False, None, ready)
    go.send(far_one, far_one_out)
    for copy in late_copies:
        copy.wait()
    feed_chunk(cross, second, branch, out, grad, *scratch, (cross_one, cross_two), False, None)
    go.send(cross_one, cross_one_out)
    low_grad = hidden
    scale, bias = 0.0, 0.0
    for lower in range(0, middle.shape[0], ROW_BLOCK):
        rows = slice(lower, lower + ROW_BLOCK)
        live = live_rows(count_ref, lower, ROW_BLOCK)
        block = middle[rows, :]
        plain, inverse = norm_parts(block)
        middle[rows, :] = block + live * out[rows, :]
        grad_second = grad[rows, :]
        scale += jnp.sum(grad_second * plain, axis=0, keepdims=True)
        bias += jnp.sum(grad_second, axis=0, keepdims=True)
        grad_middle = cotangent[rows, :] + norm_back(grad_second * (1.0 + modulation_ref[2:3, :]), plain, inverse)
        cotangent[rows, :] = grad_middle
        low_grad[rows, :] = (live * grad_middle).astype(low_type)
        grad_attended = dot(low_grad[rows, :], w_out[...], 1, 1)
        grad_own[rows, :] = (grad_attended * spread_own[rows, :]).astype(low_type)
        grad_far[rows, :] = (grad_attended * spread_far[rows, :]).astype(low_type)
        if lower // ROW_BLOCK % 2:
            pair = slice(lower - ROW_BLOCK, lower + ROW_BLOCK)
            for source, target in (
                (middle, output_out), (cotangent, grad_middle_out), (grad_own, grad_own_out), (grad_far, grad_far_out),
            ):
                go.send(source.at[pair, :], target.at[pair, :])
    mod_grad_ref[0:1, :] = scale
    mod_grad_ref[1:2, :] = bias

    half = w_out_grad.shape[0] // 2
    w_out_grad[...] = dot(attended[...], low_grad[...], 0, 0).astype(low_type)
    for two, two_out, side_of in ((far_two, far_two_out, core_ref[0]), (cross_two, cross_two_out, 1 - core_ref[0])):
        start = pl.multiple_of(side_of * half, half)
        two[two.shape[0] - half :, :] = w_out_grad[pl.ds(start, half), :]
        go.send(two, two_out)
    go.finish()


def project_back_kernel(
    core_ref, modulation_ref, mod_two_ref, plain_in, query_in, plain_far_in, key_in, far_key_in, value_in, far_value_in,
    w_query_in, w_key_in, w_value_in,
    kept_out, sent_out, mod_grad_ref,
    plain, query, plain_far, key, far_key, value, far_value, w_query, w_key, w_value,
    weight_grad, packed, in_sems, out_sems,
):
    come, go = Mover(in_sems), Mover(out_sems)
    width = weight_grad.shape[2]
    half = width // 2
    own_half = pl.ds(pl.multiple_of(core_ref[0] * half, half), half)
    other_half = pl.ds(pl.multiple_of((1 - core_ref[0]) * half, half), half)
    groups = (
        ((plain_in, plain), (query_in, query), (w_query_in, w_query)),
        ((key_in, key), (plain_far_in, plain_far), (far_key_in, far_key), (w_key_in, w_key)),
        ((value_in, value), (far_value_in, far_value), (w_value_in, w_value)),
    )
    copies = [[come.start(source, target) for source, target in group] for group in groups]
    gain = (1.0 + modulation_ref[0:1, :]).T
    shift = modulation_ref[1:2, :].T
    scale, bias = 0.0, 0.0
    for kind, (own, far, weight) in enumerate(
        ((query, None, w_query), (key, far_key, w_key), (value, far_value, w_value))
    ):
        for copy in copies[kind]:
            copy.wait()
        grad = dot(plain[...], own[...], 0, 0)
        total = jnp.sum(own[...].astype(jnp.float32), axis=0, keepdims=True)
        if far is not None:
            grad += dot(plain_far[...], far[...], 0, 0)
            total += jnp.sum(far[...].astype(jnp.float32), axis=0, keepdims=True)
        matrix = weight[...].astype(jnp.float32)
        scale += jnp.sum(grad * matrix, axis=1, keepdims=True)
        bias += jnp.sum(matrix * total, axis=1, keepdims=True)
        weight_grad[kind] = (grad * gain + shift * total).astype(low_type)
        go.send(weight_grad.at[kind, own_half, :], kept_out.at[kind])
        go.send(weight_grad.at[kind, other_half, :], sent_out.at[kind * half : (kind + 1) * half, :])
    mod_grad_ref[0:1, :] = scale.T
    mod_grad_ref[1:2, :] = bias.T
    mod_grad_ref[2:4, :] = mod_two_ref[...]
    mod_grad = mod_grad_ref[...]
    high = mod_grad.astype(low_type).astype(jnp.float32)
    packed[...] = jnp.concatenate([high, mod_grad - high, jnp.zeros((8, high.shape[1]), jnp.float32)]).astype(low_type)
    go.send(packed, sent_out.at[3 * half : 3 * half + 16, :])
    go.finish()


def small(work, out_shapes, scalar_args, args, grant=16):
    def kernel(scalar_ref, *refs):
        for out_ref, value in zip(refs[len(args) :], work(scalar_ref, *refs[: len(args)])):
            out_ref[...] = value.astype(out_ref.dtype)

    return call(
        kernel, list(out_shapes), (scalar_args, *args), specs=[scalars] + [whole] * len(args), grant=grant, flops=2**29
    )


def half_of(ref, which):
    half = ref.shape[1] // 2
    return ref[:, pl.ds(pl.multiple_of(which * half, half), half), :].astype(jnp.float32)


def halves_of(side_of, *refs):
    return sum(half_of(ref, 1 - side_of) for ref in refs), sum(half_of(ref, side_of) for ref in refs)


def finish_kernel(
    states_ref, grad_middle_ref, query_ref, key_ref, value_ref, modulation_ref, send_ref, w_query_ref, w_key_ref, w_value_ref, *refs
):
    returned_refs, (grad_states_ref, returned, sems) = refs[:4], refs[4:]

    @pl.when(pl.program_id(0) == 0)
    def _():
        for copy in fetch(returned_refs, returned, sems):
            copy.wait()

    rows = states_ref.shape[0]
    sends = send_ref.shape[1]
    grad = sum(
        dot(own_ref[...], weight_ref[...], 1, 1)
        for own_ref, weight_ref in ((query_ref, w_query_ref), (key_ref, w_key_ref), (value_ref, w_value_ref))
    )
    for position in range(len(returned_refs)):
        chosen = chosen_rows(send_ref, position, rows, pl.program_id(0) * rows)
        grad += dot(chosen, returned[position * sends : (position + 1) * sends, :], 1, 0)
    plain, inverse = norm_parts(states_ref[...])
    grad_states_ref[...] = grad_middle_ref[...] + norm_back(grad * (1.0 + modulation_ref[0:1, :]), plain, inverse)


def finish(states, grad_middle, grads, modulation, send_list, weights, returned):
    rows, width = states.shape
    by_block = pl.BlockSpec((ROW_BLOCK, width), lambda i: (i, 0))
    once = [pl.BlockSpec(part.shape, lambda i: (0, 0)) for part in (modulation, send_list, *weights)]
    return pl.pallas_call(
        finish_kernel,
        grid=(rows // ROW_BLOCK,),
        in_specs=[by_block] * 5 + once + [anywhere] * len(returned),
        out_specs=by_block,
        out_shape=shaped((rows, width), jnp.float32),
        scratch_shapes=[
            pltpu.VMEM((sum(part.shape[0] for part in returned), width), low_type),
            pltpu.SemaphoreType.DMA((len(returned),)),
        ],
        compiler_params=pltpu.CompilerParams(vmem_limit_bytes=24 * 2**20),
        cost_estimate=pl.CostEstimate(flops=2**31, bytes_accessed=2**23, transcendentals=0),
    )(states, grad_middle, *grads, modulation, send_list, *weights, *returned)


def from_behind(block, axis, distance):
    devices = range(lax.axis_size(axis))
    route = [((i - distance) % len(devices), i) for i in devices]
    return lax.ppermute(block, axis, route)


def swap(block, mask):
    count = lax.axis_size("nodes") * lax.axis_size("hid")
    return lax.ppermute(block, everywhere, [(i, i ^ mask) for i in range(count)])


def place():
    return lax.axis_index("nodes") * lax.axis_size("hid") + lax.axis_index("hid")


def side(link):
    return (place() >> link) & 1


def added(parts):
    return sum(part.astype(jnp.float32) for part in parts).astype(low_type)


def pieces_of(block, count, index):
    size = block.shape[1] // count
    return lax.dynamic_slice_in_dim(block, index * size, size, 1)


def half_sum(block, link):
    return pieces_of(block, 2, side(link)) + swap(pieces_of(block, 2, 1 - side(link)), 1 << link)


def half_join(block, link):
    other = swap(block, 1 << link)
    return jnp.where(
        side(link) == 0, jnp.concatenate([block, other], axis=1), jnp.concatenate([other, block], axis=1)
    )


def whole_sum(block, link):
    return block + swap(block, 1 << link)


def pack_wide(values):
    high = lax.reduce_precision(values, 8, 7)
    both = jnp.concatenate([high, values - high]).astype(low_type)
    return jnp.concatenate([both, jnp.zeros((16 - both.shape[0], both.shape[1]), low_type)])


def unpack_wide(packed, count):
    packed = packed.astype(jnp.float32)
    return packed[:count] + packed[count : 2 * count]


def group_sum(block, wide, links):
    count = 1 << len(links)
    here = sum(side(link) << i for i, link in enumerate(links))
    total = pieces_of(block, count, here).astype(jnp.float32)
    shape = total.shape
    packed = pack_wide(wide)
    for mask in range(1, count):
        sent = pieces_of(block, count, here ^ mask).reshape(-1, shape[-1])
        come = swap(jnp.concatenate([sent, packed]), sum(((mask >> i) & 1) << link for i, link in enumerate(links)))
        total = total + come[: -packed.shape[0]].reshape(shape).astype(jnp.float32)
        wide = wide + unpack_wide(come[-packed.shape[0] :], wide.shape[0])
    return total.astype(low_type), wide


def group_join(block, links):
    found = [block]
    for mask in range(1, 1 << len(links)):
        found.append(swap(block, sum(((mask >> i) & 1) << link for i, link in enumerate(links))))
    for i, link in enumerate(links):
        turned = [found[k ^ (1 << i)] for k in range(len(found))]
        found = [jnp.where(side(link) == 0, kept, other) for kept, other in zip(found, turned)]
    return jnp.concatenate(found, axis=1)


def after(values, previous):
    return lax.optimization_barrier((values, previous))


def body(
    states,
    condition,
    mod_w,
    w_query,
    w_key,
    w_value,
    w_out,
    w_gate,
    w_up,
    w_down,
    counts,
    send_rows,
    neighbours,
    cotangent,
):
    rows, width = states.shape
    sends = send_rows.shape[2]
    ext = rows + len(halo_steps) * sends
    f32 = jnp.float32
    parcel = shaped((sends, width))
    send_list = send_rows[0]

    links = (lax.axis_size("nodes") * lax.axis_size("hid")).bit_length() - 1
    core, across, *around = range(links)

    normed, plain, modulation, *parcels = prepare(states, condition, mod_w, send_list)
    landed = [from_behind(part, everywhere, hop) for part, hop in zip(parcels, halo_steps)]
    shard, normed = after((w_gate, w_up, w_down), normed)
    near_half = side(around[0])
    middle_row = shard[1].shape[0] // 2
    far_half = jnp.where(
        near_half == 0,
        jnp.concatenate([shard[0], shard[1][:middle_row]]),
        jnp.concatenate([shard[1][middle_row:], shard[2]]),
    )
    far_half = swap(far_half, 1 << across)

    queries, own_keys, own_values, *own_raised, top, total, mixed, packed = attend_own(
        normed, neighbours.T, w_query, w_key, w_value, ext - rows
    )
    queries, far_half, landed, shard = lax.optimization_barrier((queries, far_half, landed, shard))
    core_shard = [swap(weight, 1 << core) for weight in shard]
    far_rest = swap(far_half, 1 << around[0])
    cross_half = swap(far_half, 1 << core)
    *far_raised, attended, spread_own, spread_far, far_keys, far_values, plain_far = attend_far(
        modulation, queries, w_key, w_value, packed, top, total, mixed, landed
    )

    low_rows = shaped((rows, width))
    wide_rows = shaped((rows, width), f32)
    shard_rows = sum(weight.size for weight in shard) // width
    all_units = shaped((shard_rows, width))
    half_grad = shaped((shard_rows // 2, width))
    joint_grad = shaped((shard_rows // 2 + width // 2, width))

    def room(*shapes):
        return [pltpu.VMEM(one.shape, one.dtype) for one in shapes]

    middle, second, branch, out, grad, core_one, core_two, own_one, own_two = call(
        feed_first_kernel,
        [wide_rows, low_rows, low_rows, wide_rows, wide_rows] + [half_grad] * 4,
        (counts, modulation, states, cotangent, attended, w_out, *core_shard, *shard),
        grant=56,
        specs=[scalars, whole] + [anywhere] * 10,
        out_specs=[anywhere] * 9,
        scratch=room(wide_rows, wide_rows, low_rows, w_out, all_units, all_units, low_rows, low_rows)
        + room(wide_rows, wide_rows)
        + room(*[half_grad] * 4, *[low_rows] * 3)
        + [pltpu.SemaphoreType.DMA((13,)), pltpu.SemaphoreType.DMA((9,))],
        flops=2**34,
        moved=2**24,
    )
    core_index = jnp.stack([lax.axis_index("hid") & 1, near_half])
    (cross_half, far_rest), grad = after((cross_half, far_rest), grad)
    cross_rest = swap(far_rest, 1 << core)
    fold = (-1, width // 2, width)

    def over_cores(*grads):
        return [[kept.reshape(fold), swap(sent, 1 << core).reshape(fold)] for kept, sent in grads]

    first, second_link, *rest = around
    sides = jnp.stack([side(first), side(second_link)])

    def lines(blocks, count):
        return shaped((blocks, count, width))

    def first_halves(side_ref, one, one_come, two, two_come):
        return *halves_of(side_ref[0], one, one_come), *halves_of(side_ref[1], two, two_come)

    own_sums = over_cores((own_one, core_one), (own_two, core_two))
    kept = own_sums[0][0].shape[0]
    eighth = fold[1] // 2
    quarter = eighth // 2
    one_sent, one_own, two_sent, two_own = small(
        first_halves, [lines(kept, eighth)] * 4, sides, (*own_sums[0], *own_sums[1])
    )
    (one_sent, two_sent), cross_rest = after((one_sent, two_sent), cross_rest)
    own_come = swap(one_sent, 1 << first), swap(two_sent, 1 << second_link)
    output, grad_middle, grad_own, grad_far, mod_two, cross_one, cross_two, far_one, far_two = call(
        feed_last_kernel,
        [wide_rows, wide_rows, low_rows, low_rows, shaped((2, width), f32)] + [half_grad, joint_grad] * 2,
        (counts, core_index, modulation, cotangent, attended, w_out, spread_own, spread_far)
        + (middle, second, branch, out, grad, cross_half, cross_rest, far_half, far_rest),
        grant=56,
        specs=[scalars, scalars, whole] + [anywhere] * 14,
        out_specs=[anywhere] * 4 + [whole] + [anywhere] * 4,
        scratch=room(wide_rows, low_rows, w_out, wide_rows, wide_rows, wide_rows, low_rows, low_rows)
        + room(wide_rows, wide_rows, all_units, all_units, low_rows, low_rows)
        + room(half_grad, joint_grad, half_grad, joint_grad)
        + room(w_out, *[low_rows] * 3)
        + [pltpu.SemaphoreType.DMA((14,)), pltpu.SemaphoreType.DMA((12,))],
        flops=2**34,
        moved=2**24,
    )

    (cross_one, cross_two), own_come = after((cross_one, cross_two), own_come)
    far_sums = over_cores((far_one, cross_one), (far_two, cross_two))
    one_sent, one_far, two_sent, two_far = small(
        first_halves,
        [lines(kept, eighth)] * 2 + [lines(kept + 1, eighth)] * 2,
        sides,
        (*far_sums[0], *far_sums[1]),
    )
    grad_far, (one_sent, two_sent) = after(grad_far, (one_sent, two_sent))
    far_come = swap(one_sent, 1 << first), swap(two_sent, 1 << second_link)
    partial, *far_pieces = attend_back(
        queries, attended, far_keys, far_values, grad_far, far_raised, returns=(w_key, w_value)
    )
    far_pieces, parcels = far_pieces[:2], far_pieces[2:]
    far_come, (grad_own, partial) = after(far_come, (grad_own, partial))

    def second_halves(side_ref, one_own, one_own_come, one_far, one_far_come, two_own, two_own_come, two_far, two_far_come):
        own_sent, own_kept = halves_of(side_ref[1], one_own, one_own_come)
        far_sent, far_kept = halves_of(side_ref[1], one_far, one_far_come)
        two_kept = two_own[...].astype(f32) + two_own_come[...].astype(f32)
        two_sent = two_far[...].astype(f32) + two_far_come[...].astype(f32)
        return jnp.concatenate([own_sent, far_sent]), own_kept, far_kept, two_kept, two_sent

    one_sent, one_own, one_far, two_own, two_sent = small(
        second_halves,
        [lines(2 * kept, quarter), lines(kept, quarter), lines(kept, quarter), lines(kept, eighth), lines(kept + 1, eighth)],
        sides,
        (one_own, own_come[0], one_far, far_come[0], two_own, own_come[1], two_far, far_come[1]),
    )
    (one_sent, two_sent), grad_own = after((one_sent, two_sent), grad_own)
    one_come, two_come = swap(one_sent, 1 << second_link), swap(two_sent, 1 << across)
    pieces = attend_back(queries, attended, own_keys, own_values, grad_own, own_raised, partial)
    (one_come, two_come), pieces = after((one_come, two_come), pieces)

    def third_halves(side_ref, one_own, one_far, one_come, two_own, two_last, two_come):
        one_kept = one_own[...].astype(f32) + one_come[:kept].astype(f32)
        one_sent = one_far[...].astype(f32) + one_come[kept:].astype(f32)
        here = side_ref[0]
        own_sent, own_kept = halves_of(here, two_own, two_come.at[:kept])
        last_sent, last_kept = halves_of(here, two_last.at[kept:], two_come.at[kept:])
        return one_sent, one_kept, jnp.concatenate([own_sent, last_sent]), jnp.concatenate([own_kept, last_kept])

    one_sent, one_kept, two_sent, two_kept = small(
        third_halves,
        [lines(kept, quarter)] * 2 + [lines(kept + 1, quarter)] * 2,
        sides,
        (one_own, one_far, one_come, two_own, two_sent, two_come),
    )
    (one_sent, two_sent), pieces = after((one_sent, two_sent), pieces)
    one_come, two_come = swap(one_sent, 1 << across), swap(two_sent, 1 << first)
    returned = [from_behind(part, everywhere, -hop) for part, hop in zip(parcels[:3], halo_steps)]
    far_low = shaped((ext - rows, width))
    attn_kept, attn_sent, mod_grad = call(
        project_back_kernel,
        [shaped((3, width // 2, width)), shaped((3 * width // 2 + 16, width)), shaped((4, width), f32)],
        (core_index, modulation, mod_two, plain, pieces[0], plain_far, pieces[1], far_pieces[0], pieces[2], far_pieces[1])
        + (w_query, w_key, w_value),
        specs=[scalars, whole, whole] + [anywhere] * 10,
        out_specs=[anywhere, anywhere, whole],
        scratch=room(low_rows, low_rows, far_low, low_rows, far_low, low_rows, far_low, w_query, w_key, w_value)
        + room(shaped((3, width, width)), shaped((16, width)))
        + [pltpu.SemaphoreType.DMA((10,)), pltpu.SemaphoreType.DMA((7,))],
        flops=2**32,
        moved=2**23,
    )

    def on_both(step, link):
        def run(one, two):
            both = step(jnp.concatenate([one, two]), link)
            return both[:kept], both[kept:]

        return run

    shard_steps = [on_both(whole_sum, link) for link in rest]
    shard_steps.append(lambda one, two: (half_join(one, second_link), half_join(two, first)))
    shard_steps.append(lambda one, two: (half_join(one, first), half_join(two, second_link)))

    groups = [[across, first]] + [around[i : i + 2] for i in range(1, len(around), 2)]
    def over_attn_cores(kept, wide):
        come = swap(attn_sent, 1 << core)
        total = kept.astype(f32) + come[:-16].reshape(kept.shape).astype(f32)
        return total.astype(low_type), wide + unpack_wide(come[-16:], wide.shape[0])

    attn_steps = [over_attn_cores] + [functools.partial(group_sum, links=group) for group in groups]
    attn_steps += [lambda grad, wide, group=group: (group_join(grad, group), wide) for group in reversed(groups)]

    returned, (one_come, two_come), parcels, attn_sent = lax.optimization_barrier(
        (returned, (one_come, two_come), parcels, attn_sent)
    )
    returned.append(from_behind(parcels[3], everywhere, -halo_steps[3]))
    shard_state = added([one_kept, one_come]), added([two_kept, two_come])
    attn_state = attn_kept, mod_grad
    shard_turns = [[]] + [[step] for step in shard_steps]
    for index in range(max(len(shard_turns), len(attn_steps))):
        for step in shard_turns[index] if index < len(shard_turns) else []:
            shard_state = step(*shard_state)
        if index < len(attn_steps):
            attn_state = attn_steps[index](*attn_state)
        if index == 1:
            returned, attn_state = after(returned, attn_state)
        if index == 3:
            grad_states = finish(
                states, grad_middle, pieces, modulation, send_list, (w_query, w_key, w_value), returned
            )
            grad_states, attn_state = after(grad_states, attn_state)
        if index in (1, 2):
            shard_state, attn_state = after(shard_state, attn_state)
    (one, two), (attn_grad, mod_grad) = shard_state, attn_state
    shard_grad = jnp.concatenate([one, two[:kept]]).reshape(-1, width).astype(f32)
    grad_w_gate, grad_w_up, grad_w_down = jnp.split(shard_grad, 3)
    grad_w_query, grad_w_key, grad_w_value = half_join(attn_grad, core).astype(f32)
    grad_w_out = half_join(two[kept:], core)[0].astype(f32)
    mod_grad = mod_grad.reshape(-1)
    grad_mod_w = condition[:, None] * mod_grad[None, :]
    grad_condition = jnp.sum(mod_w.astype(f32) * mod_grad[None, :], axis=1)
    return (
        output,
        grad_states,
        grad_condition,
        grad_mod_w,
        grad_w_query,
        grad_w_key,
        grad_w_value,
        grad_w_out,
        grad_w_gate,
        grad_w_up,
        grad_w_down,
    )


def solution(mesh):
    rows = P(everywhere, None)
    placed = (
        rows,
        P(),
        P(),
        P(),
        P(),
        P(),
        P(),
        P(None, "hid"),
        P(None, "hid"),
        P("hid", None),
        P(everywhere),
        P(everywhere, None, None),
        rows,
        rows,
    )
    return jax.shard_map(
        body,
        mesh=mesh,
        in_specs=placed,
        out_specs=(rows, rows, P(), P(), P(), P(), P(), P(), P(None, "hid"), P(None, "hid"), P("hid", None)),
        check_vma=False,
    )
```
